256 devices in a mesh: gx: 8 (over x, y_hi), gy: 32 (over y_lo, z, core).
Axes of the slice: x: 4, y: 4 (y_hi: 2, y_lo: 2; y = y_hi * 2 + y_lo), z: 8, core: 2. Of those that a mesh axis runs over, the one named last changes fastest.
Arguments:
- tensor: bfloat16 [2, 512, 1024, 1024], P(None, 'gy', 'gx'), may hold values from -6 to 6
- row_factor: float32 [96, 1024], P(None, ('gx', 'gy')), may hold values from -4 to 4
- column_factor: float32 [96, 1024], P(None, 'gy'), may hold values from -4 to 4
- band_factor: float32 [96, 512], P(None, ('gy', 'gx')), may hold values from -4 to 4
- time_factor: float32 [96, 2], replicated, may hold values from -4 to 4
Outputs:
- row_grad: float32 [96, 1024], P(None, ('gx', 'gy'))
- column_grad: float32 [96, 1024], P(None, 'gy')
- band_grad: float32 [96, 512], P(None, ('gy', 'gx'))
- time_grad: float32 [96, 2], replicated
The draws below stay inside these ranges and needn't reach their ends.
All inputs are finite; a program needn't handle non-finite values.
Results may differ from the reference program's by a relative error of at most 0.0028.
Values sent between devices are 32-bit elements; how exact they have to be, the bound alone decides.
A program may use at most 64 MiB of HBM per device.

```python
import jax
import jax.numpy as jnp
from jax import lax

ROWS = 1024
COLS = 1024
BANDS = 512
RANK = 96
FRAMES = 2


def apply_scales(key, base, rank_rows, extent):
    key_cols, key_rank = jax.random.split(key)
    position = jnp.arange(extent, dtype=jnp.float32) / extent
    spread = jax.random.uniform(key_cols, (extent,), jnp.float32, 0.0, 1.0)
    column_scale = jnp.exp(jnp.log(3.0) * position + jnp.log(10.0) * spread)
    rank_scale = jax.random.uniform(key_rank, (rank_rows, 1), jnp.float32, 0.7, 1.4)
    factor = jnp.sqrt(2.0 / (extent * 78.3 * 1.07))
    return base * rank_scale * column_scale[None, :] * factor


def draw_scaled(key, rank_rows, extent):
    key_base = jax.random.fold_in(key, 0)
    key_scale = jax.random.fold_in(key, 2)
    base = jnp.clip(jax.random.normal(key_base, (rank_rows, extent), jnp.float32), -4.0, 4.0)
    return apply_scales(key_scale, base, rank_rows, extent)


def draw_row_factor(key, part):
    key = jax.random.fold_in(key, 11)
    return draw_scaled(key, RANK, ROWS)


def draw_column_factor(key, part):
    key = jax.random.fold_in(key, 23)
    return draw_scaled(key, RANK, COLS)


def draw_band_factor(key, part):
    key = jax.random.fold_in(key, 37)
    return draw_scaled(key, RANK, BANDS)


def level_of(own_key, dims, shards, smallest, top_value):
    factor_of, own = 1.0, jax.random.fold_in(own_key, 6)
    for dim, parts in shards:
        steps = jnp.exp(jax.random.uniform(jax.random.fold_in(own, dim), (parts,), jnp.float32, smallest / len(shards), top_value / len(shards)))
        factor_of = factor_of * jnp.repeat(steps, dims[dim] // parts).reshape([-1 if axis == dim else 1 for axis in range(len(dims))])
    return factor_of


def centred(key, shape, scale, limit, cuts=(), held_as=jnp.bfloat16):
    gain = level_of(key, shape, cuts, -0.22, 0.18) if cuts else 1.0
    array = jax.random.normal(key, shape, jnp.float32) * scale * gain
    return jnp.minimum(jnp.maximum(array, -limit), limit).astype(held_as)


def setup_inputs(seed: int = 0) -> dict:
    key_of = jax.random.split(jax.random.key(seed), 6)
    return {
        "tensor": centred(key_of[0], (FRAMES, BANDS, ROWS, COLS), 1.0, 6.0, ((1, 32), (2, 8))),
        "row_factor": draw_row_factor(jax.random.fold_in(key_of[5], 71), 0),
        "column_factor": draw_column_factor(jax.random.fold_in(key_of[5], 71), 0),
        "band_factor": draw_band_factor(jax.random.fold_in(key_of[5], 71), 0),
        "time_factor": centred(key_of[4], (RANK, FRAMES), 1.0, 4.0, (), jnp.float32),
    }


def gram_of(factor):
    return jnp.dot(factor, factor.T, precision=lax.Precision.HIGHEST, preferred_element_type=jnp.float32)


def reference(tensor, row_factor, column_factor, band_factor, time_factor):
    highest = lax.Precision.HIGHEST
    flattened = tensor.reshape(FRAMES * BANDS * ROWS, COLS)
    low_cols = column_factor.astype(jnp.bfloat16)
    folded = lax.dot_general(low_cols, flattened, (((1,), (1,)), ((), ())), preferred_element_type=jnp.float32)
    folded = folded.reshape(RANK, FRAMES, BANDS, ROWS)
    by_time = jnp.einsum('rtbi,rt->rbi', folded, time_factor, precision=highest)
    by_band = jnp.einsum('rtbi,rb->rti', folded, band_factor, precision=highest)
    rows_term = jnp.einsum('rbi,rb->ri', by_time, band_factor, precision=highest)
    bands_term = jnp.einsum('rbi,ri->rb', by_time, row_factor, precision=highest)
    frames_term = jnp.einsum('rti,ri->rt', by_band, row_factor, precision=highest)
    product = (time_factor[:, :, None, None] * band_factor[:, None, :, None] * row_factor[:, None, None, :]).astype(jnp.bfloat16)
    product = product.reshape(RANK, FRAMES * BANDS * ROWS)
    cols_term = jnp.dot(product, flattened, preferred_element_type=jnp.float32)
    gram_rows = gram_of(row_factor)
    gram_cols = gram_of(column_factor)
    gram_bands = gram_of(band_factor)
    gram_time = gram_of(time_factor)
    row_grad = jnp.dot(gram_cols * gram_bands * gram_time, row_factor, precision=highest) - rows_term
    column_grad = jnp.dot(gram_rows * gram_bands * gram_time, column_factor, precision=highest) - cols_term
    band_grad = jnp.dot(gram_rows * gram_cols * gram_time, band_factor, precision=highest) - bands_term
    time_grad = jnp.dot(gram_rows * gram_cols * gram_bands, time_factor, precision=highest) - frames_term
    return (row_grad, column_grad, band_grad, time_grad)
```

```python
import jax
import jax.numpy as jnp
from jax import lax
from jax.experimental import pallas as pl
from jax.experimental.pallas import tpu as pltpu
from jax.sharding import PartitionSpec as P

MESH = pl.DeviceIdType.MESH
HIGHEST = lax.Precision.HIGHEST
F32 = jnp.float32
BF16 = jnp.bfloat16

NX, NY, NLZ = 8, 32, 16
RANK, LANES = 96, 128
FRAMES, BANDS, ROWS, COLS = 2, 16, 128, 1024
RW, CW, BW = 4, 32, 2
PACK = CW * RANK // LANES
TB = FRAMES * BANDS
HALF = BANDS * ROWS
CHUNKS = 2
CHUNK = COLS // CHUNKS
PER = NLZ // CHUNKS
LOADS = 8
MSG = CW + 8
QROWS = ROWS // 4

(
    S_ROW, S_BAND, S_BANDX, S_COL, S_COLC, S_R1, S_R2, S_R3, S_F1, S_F2,
    S_GRAM, S_GRAMP, S_ROWS, S_BANDS,
) = [0, 1, 2, 3, 4, 5, 7, 8, 9, 10, 11, 12, 13, 14]
N_SEMS = 15


def dot(x, y):
    return jnp.dot(x, y, preferred_element_type=F32)


def exact(x, y):
    return jnp.dot(x, y, precision=HIGHEST, preferred_element_type=F32)


def total(ref, count):
    out = ref[0]
    for k in range(1, count):
        out = out + ref[k]
    return out


def wrap(index, size):
    return jnp.where(index >= size, index - size, index)


def lane_of(x):
    return lax.broadcasted_iota(jnp.int32, x.shape, 1)


def pack(tiles):
    spare = lane_of(tiles[3]) >= RANK
    return [
        jnp.where(spare, pltpu.roll(tiles[3], RANK - 32 * m, 1), tiles[m]) for m in range(3)
    ]


def unpack(tiles):
    lane = lane_of(tiles[0])
    last = jnp.zeros_like(tiles[0])
    for m in (2, 1, 0):
        last = jnp.where(lane < 32 * m + 32, pltpu.roll(tiles[m], 32 * m + 32, 1), last)
    zero = jnp.zeros_like(last)
    return [jnp.where(lane < RANK, tile, zero) for tile in tiles] + [
        jnp.where(lane < RANK, last, zero)
    ]


def kernel(
    tensor, packed,
    out,
    data, mine4, mine2, rowg, bandg, bandx, row_t, band_t, bandx_t, tb_t,
    turned, prod, by_frame, part, recv1, sum1, recv2, fin, recv3,
    colg, colf, low, folded, partials,
    fpart, fg, fsum, fx, gpart, grecv, gall, gcols,
    rsend, rrecv, bsend, brecv,
    local_sems, send_sems, recv_sems,
):
    a = lax.axis_index("gx")
    g = lax.axis_index("gy")
    lz = lax.div(g, 2)
    c = g - 2 * lz
    l = lax.div(lz, 8)
    z = lz - 8 * l
    p = l * 2 + c
    other = 1 - c
    partner = lz * 2 + other
    gy_peers = [wrap(g + k, NY) for k in range(1, NY)]
    gx_peers = [wrap(a + k, NX) for k in range(1, NX)]
    core_peers = [wrap(lz + k, NLZ) * 2 + c for k in range(1, NLZ)]

    def send(src, dst, sem, device):
        pltpu.make_async_remote_copy(
            src_ref=src, dst_ref=dst, send_sem=send_sems.at[sem], recv_sem=recv_sems.at[sem],
            device_id=device, device_id_type=MESH,
        ).start()

    def arrived(ref, sem):
        pltpu.make_async_copy(ref, ref, recv_sems.at[sem]).wait()

    def sent(ref, sem):
        pltpu.make_async_copy(ref, ref, send_sems.at[sem]).wait()

    barrier = pltpu.get_barrier_semaphore()
    for to in gy_peers:
        pl.semaphore_signal(barrier, inc=1, device_id=(a, to), device_id_type=MESH)
    for to in gx_peers:
        pl.semaphore_signal(barrier, inc=1, device_id=(to, g), device_id_type=MESH)

    for k in range(LOADS):
        span = pl.ds(k * (TB // LOADS), TB // LOADS)
        pltpu.make_async_copy(tensor.at[span], data.at[span], local_sems.at[k]).start()

    tb_t[...] = jnp.zeros_like(tb_t)
    mine2[...] = packed[CW : CW + BW]
    mine4[...] = packed[MSG : MSG + RW]
    time8 = packed[MSG + 8 :]
    rowg[g] = mine4[...]
    bandg[a] = mine2[...]
    bandx[g] = mine2[...]
    for m, tile in enumerate(pack([packed[8 * m : 8 * m + 8] for m in range(4)])):
        colg[c, lz, 8 * m : 8 * m + 8] = tile

    pl.semaphore_wait(barrier, NY - 1 + NX - 1)

    for to in gy_peers:
        send(mine4, rowg.at[g], S_ROW, (a, to))
    for to in gx_peers:
        send(mine2, bandg.at[a], S_BAND, (to, g))
    for to in core_peers:
        send(colg.at[c, lz], colg.at[c, lz], S_COL, (a, to))
    for to in gy_peers:
        send(mine2, bandx.at[g], S_BANDX, (a, to))

    @pl.loop(0, LOADS)
    def _(k):
        per = TB // LOADS
        span = pl.ds(k * per, per)
        pltpu.make_async_copy(tensor.at[span], data.at[span], local_sems.at[k]).wait()
        for i in range(per):
            at = pl.multiple_of((k * per + i) * ROWS, ROWS)
            turned[:, pl.ds(at, ROWS)] = data[k * per + i].T

    arrived(bandg.at[pl.ds(0, NX - 1)], S_BAND)
    for k in range(NX):
        band_t[BW * k : BW * k + BW] = bandg[k]
    for t in range(FRAMES):
        tb_t[t * BANDS : (t + 1) * BANDS] = time8[t : t + 1] * band_t[...]
    tb_t[TB : TB + BANDS] = band_t[...]
    arrived(rowg.at[pl.ds(0, NY - 1)], S_ROW)
    for k in range(NY):
        row_t[RW * k : RW * k + RW] = rowg[k]

    @pl.loop(0, BANDS)
    def _(k):
        span = pl.ds(pl.multiple_of(k * ROWS, ROWS), ROWS)
        rows = row_t[...]
        plain = (tb_t[pl.ds(TB + k, 1)] * rows).astype(BF16)
        for t in range(FRAMES):
            prod[t, span, 0:LANES] = (tb_t[pl.ds(t * BANDS + k, 1)] * rows).astype(BF16)
            prod[t, span, LANES:] = plain

    def send_pieces(n):
        span = pl.ds(n * PER, PER)
        arrived(recv1.at[span], S_R1 + n)
        sum1[span] = part[c, span] + recv1[span]
        for i in range(PER):
            k = n * PER + i

            @pl.when(k != lz)
            def _():
                send(sum1.at[k], recv2.at[lz], S_R2, (a, k * 2 + c))

    @pl.loop(0, CHUNKS)
    def _(n):
        here = pl.ds(pl.multiple_of(n * CHUNK, CHUNK), CHUNK)
        acc = jnp.zeros((CHUNK, LANES), F32)
        for t in range(FRAMES):
            both = dot(turned[here, t * HALF : (t + 1) * HALF], prod[t])
            by_frame[t, here] = both[:, LANES:]
            acc = acc + both[:, 0:LANES]
        acc = acc.reshape(CHUNK // CW, 4, 8, LANES)
        tiles = pack([acc[:, m].reshape(CHUNK // 4, LANES) for m in range(4)])
        for k in range(CHUNK // CW):
            for m in range(3):
                part[k % 2, n * PER + k // 2, 8 * m : 8 * m + 8] = tiles[m][8 * k : 8 * k + 8]
        span = pl.ds(n * PER, PER)
        send(part.at[other, span], recv1.at[span], S_R1 + n, (a, partner))

        @pl.when(n > 0)
        def _():
            send_pieces(n - 1)

    arrived(colg.at[0, pl.ds(0, NLZ - 1)], S_COL)
    send(colg.at[c], colg.at[c], S_COLC, (a, partner))

    arrived(bandx.at[pl.ds(0, NY - 1)], S_BANDX)
    for k in range(NY):
        bandx_t[BW * k : BW * k + BW] = bandx[k]
    for i, ref in enumerate((row_t, bandx_t)):
        gram = exact(ref[...].T, ref[...])
        for k in range(4):
            gpart[k, i] = gram[24 * k : 24 * k + 24]
    grecv[a] = gpart[p]
    send_pieces(CHUNKS - 1)
    for to in gx_peers:
        send(gpart.at[p], grecv.at[a], S_GRAM, (to, g))

    arrived(colg.at[0], S_COLC)
    for i in range(2):
        tiles = unpack(
            [colg[i, :, 8 * m : 8 * m + 8].reshape(8 * NLZ, LANES) for m in range(3)]
        )
        for k in range(NLZ):
            block = jnp.concatenate([tile[8 * k : 8 * k + 8] for tile in tiles], axis=0)
            at = (2 * k + i) * CW
            colf[at : at + CW] = block
            low[at : at + CW] = block.astype(BF16)

    for t in range(FRAMES):
        fpart[t : t + 1] = jnp.sum(
            by_frame[t] * low[...].astype(F32), axis=0, keepdims=True
        )
    fg[g] = fpart[...]
    for to in gy_peers:
        send(fpart, fg.at[g], S_F1, (a, to))

    @pl.loop(0, 4)
    def _(q):
        here = pl.ds(pl.multiple_of(q * QROWS, QROWS), QROWS)
        folded[...] = dot(data[:, here, :].reshape(TB * QROWS, COLS), low[...])
        rows = jnp.zeros((QROWS, LANES), F32)
        row_here = row_t[here]
        for j in range(TB):
            block = folded[j * QROWS : (j + 1) * QROWS]
            rows = rows + block * tb_t[j : j + 1]
            block = block * row_here
            partials[q, j] = jnp.sum(block.reshape(QROWS // 8, 8, LANES), axis=0)
        for i in range(NY // 4):
            rsend[q * (NY // 4) + i] = rows[RW * i : RW * i + RW]
        for i in range(NY // 4):
            k = q * (NY // 4) + i

            @pl.when(k != g)
            def _():
                send(rsend.at[k], rrecv.at[g], S_ROWS, (a, k))

    sums = total(partials, 4)
    bands = jnp.zeros((BANDS, LANES), F32)
    for t in range(FRAMES):
        bands = bands + time8[t : t + 1] * jnp.sum(sums[t * BANDS : (t + 1) * BANDS], axis=1)
    for k in range(NX):
        bsend[k] = bands[BW * k : BW * k + BW]
    for k in range(1, NX):
        to = wrap(a + k, NX)
        send(bsend.at[to], brecv.at[a], S_BANDS, (to, g))
    brecv[a] = bsend[a]
    rrecv[g] = rsend[g]

    arrived(grecv.at[pl.ds(0, NX - 1)], S_GRAM)
    gall[p] = total(grecv, NX)
    for k in range(1, 4):
        to = wrap(p + k, 4)
        to_l = lax.div(to, 2)
        send(gall.at[p], gall.at[p], S_GRAMP, (a, (to_l * 8 + z) * 2 + to - 2 * to_l))
    arrived(fg.at[pl.ds(0, NY - 1)], S_F1)
    fsum[...] = total(fg, NY)
    fx[a] = fsum[...]
    for to in gx_peers:
        send(fsum, fx.at[a], S_F2, (to, g))
    recv2[lz] = sum1[lz]
    arrived(recv2.at[pl.ds(0, NLZ - 1)], S_R2)
    fin[...] = total(recv2, NLZ)
    recv3[a] = fin[...]
    for to in gx_peers:
        send(fin, recv3.at[a], S_R3, (to, g))

    gcols[...] = jnp.zeros_like(gcols)

    @pl.loop(0, 4)
    def _(i):
        block = colf[pl.ds(pl.multiple_of(i * 256, 256), 256)]
        gcols[...] += exact(block.T, block)

    gram_cols = gcols[...]
    arrived(gall.at[pl.ds(0, 3)], S_GRAMP)
    pad = jnp.zeros((LANES - RANK, LANES), F32)
    gram_rows, gram_bands = (
        jnp.concatenate([gall[:, i].reshape(RANK, LANES), pad], axis=0) for i in range(2)
    )
    time_n = jnp.concatenate([time8, jnp.zeros((LANES - 8, LANES), F32)], axis=0).T
    gram_time = time_n[:, 0:1] * time8[0:1] + time_n[:, 1:2] * time8[1:2]
    row_model = exact(packed[MSG : MSG + 8], gram_cols * gram_bands * gram_time)
    col_model = exact(packed[0:CW], gram_rows * gram_bands * gram_time)
    band_model = exact(packed[CW:MSG], gram_rows * gram_cols * gram_time)
    time_model = exact(time8, gram_rows * gram_cols * gram_bands)

    arrived(fx.at[pl.ds(0, NX - 1)], S_F2)
    out[CW : CW + FRAMES] = time_model[0:FRAMES] - total(fx, NX)
    arrived(recv3.at[pl.ds(0, NX - 1)], S_R3)
    sums = total(recv3, NX)
    sums = jnp.concatenate(unpack([sums[8 * m : 8 * m + 8] for m in range(3)]), axis=0)
    out[0:CW] = col_model - sums
    arrived(rrecv.at[pl.ds(0, NY - 1)], S_ROWS)
    out[CW + 8 : CW + 8 + RW] = row_model[0:RW] - total(rrecv, NY)
    arrived(brecv.at[pl.ds(0, NX - 1)], S_BANDS)
    out[CW + 16 : CW + 16 + BW] = band_model[0:BW] - total(brecv, NX)

    sent(rowg.at[pl.ds(0, NY - 1)], S_ROW)
    sent(bandg.at[pl.ds(0, NX - 1)], S_BAND)
    sent(bandx.at[pl.ds(0, NY - 1)], S_BANDX)
    sent(colg.at[0, pl.ds(0, NLZ - 1)], S_COL)
    sent(colg.at[0], S_COLC)
    for n in range(CHUNKS):
        sent(recv1.at[pl.ds(n * PER, PER)], S_R1 + n)
    sent(recv2.at[pl.ds(0, NLZ - 1)], S_R2)
    sent(recv3.at[pl.ds(0, NX - 1)], S_R3)
    sent(fg.at[pl.ds(0, NY - 1)], S_F1)
    sent(fx.at[pl.ds(0, NX - 1)], S_F2)
    sent(grecv.at[pl.ds(0, NX - 1)], S_GRAM)
    sent(gall.at[pl.ds(0, 3)], S_GRAMP)
    sent(rrecv.at[pl.ds(0, NY - 1)], S_ROWS)
    sent(brecv.at[pl.ds(0, NX - 1)], S_BANDS)


def shards(tensor, row_factor, column_factor, band_factor, time_factor):
    v = pltpu.VMEM
    packed = jnp.zeros((MSG + 16, LANES), F32)
    pieces = ((0, column_factor), (CW, band_factor), (MSG, row_factor), (MSG + 8, time_factor))
    for at, x in pieces:
        x = x.T
        packed = packed + jnp.pad(x, ((at, MSG + 16 - at - x.shape[0]), (0, LANES - RANK)))
    out = pl.pallas_call(
        kernel,
        out_shape=jax.ShapeDtypeStruct((CW + 24, LANES), F32),
        in_specs=[pl.BlockSpec(memory_space=pl.ANY), pl.BlockSpec(memory_space=v)],
        out_specs=pl.BlockSpec(memory_space=v),
        scratch_shapes=[
            v((TB, ROWS, COLS), BF16),
            v((RW, LANES), F32),
            v((BW, LANES), F32),
            v((NY, RW, LANES), F32),
            v((NX, BW, LANES), F32),
            v((NY, BW, LANES), F32),
            v((ROWS, LANES), F32),
            v((BANDS, LANES), F32),
            v((NY * BW, LANES), F32),
            v((LANES, LANES), F32),
            v((COLS, TB * ROWS), BF16),
            v((FRAMES, HALF, 2 * LANES), BF16),
            v((FRAMES, COLS, LANES), F32),
            v((2, NLZ, PACK, LANES), F32),
            v((NLZ, PACK, LANES), F32),
            v((NLZ, PACK, LANES), F32),
            v((NLZ, PACK, LANES), F32),
            v((PACK, LANES), F32),
            v((NX, PACK, LANES), F32),
            v((2, NLZ, PACK, LANES), F32),
            v((COLS, LANES), F32),
            v((COLS, LANES), BF16),
            v((TB * QROWS, LANES), F32),
            v((4, TB, 8, LANES), F32),
            v((FRAMES, LANES), F32),
            v((NY, FRAMES, LANES), F32),
            v((FRAMES, LANES), F32),
            v((NX, FRAMES, LANES), F32),
            v((4, 2, 24, LANES), F32),
            v((NX, 2, 24, LANES), F32),
            v((4, 2, 24, LANES), F32),
            v((LANES, LANES), F32),
            v((NY, RW, LANES), F32),
            v((NY, RW, LANES), F32),
            v((NX, BW, LANES), F32),
            v((NX, BW, LANES), F32),
            pltpu.SemaphoreType.DMA((LOADS,)),
            pltpu.SemaphoreType.DMA((N_SEMS,)),
            pltpu.SemaphoreType.DMA((N_SEMS,)),
        ],
        compiler_params=pltpu.CompilerParams(
            collective_id=0, has_side_effects=True, vmem_limit_bytes=48 * 1024 * 1024
        ),
        cost_estimate=pl.CostEstimate(
            flops=4 * RANK * TB * ROWS * COLS, bytes_accessed=2 * TB * ROWS * COLS, transcendentals=0
        ),
    )(
        tensor.reshape(TB, ROWS, COLS),
        packed,
    )
    places = ((CW + 8, RW), (0, CW), (CW + 16, BW), (CW, FRAMES))
    return tuple(out[at : at + n, 0:RANK].T for at, n in places)


def solution(mesh):
    return jax.shard_map(
        shards,
        mesh=mesh,
        in_specs=(
            P(None, "gy", "gx", None),
            P(None, ("gx", "gy")),
            P(None, "gy"),
            P(None, ("gy", "gx")),
            P(),
        ),
        out_specs=(P(None, ("gx", "gy")), P(None, "gy"), P(None, ("gy", "gx")), P()),
        check_vma=False,
    )
```

```python
import jax
import jax.numpy as jnp
from jax import lax
from jax.experimental import pallas as pl
from jax.experimental.pallas import tpu as pltpu
from jax.sharding import PartitionSpec as P

MESH = pl.DeviceIdType.MESH
HIGHEST = lax.Precision.HIGHEST
F32 = jnp.float32
BF16 = jnp.bfloat16

NX, NY, NLZ = 8, 32, 16
RANK, LANES = 96, 128
FRAMES, BANDS, ROWS, COLS = 2, 16, 128, 1024
RW, CW, BW = 4, 32, 2
PACK = CW * RANK // LANES
TB = FRAMES * BANDS
HALF = BANDS * ROWS
CHUNKS = 2
CHUNK = COLS // CHUNKS
PER = NLZ // CHUNKS
PERQ = NLZ // 4
LOADS = 8
MSG = CW + 8
QROWS = ROWS // 4

(
    S_ROW, S_ROWC, S_BAND, S_COL, S_COLC, S_R1, S_R2, S_R3, S_F2,
    S_GRAM, S_GRAMP, S_T1, S_ROWS, S_BANDS,
) = [0, 1, 2, 3, 4, 5, 7, 8, 9, 10, 11, 12, 16, 17]
N_SEMS = 18


def dot(x, y):
    return jnp.dot(x, y, preferred_element_type=F32)


def exact(x, y):
    return jnp.dot(x, y, precision=HIGHEST, preferred_element_type=F32)


def total(ref, count):
    out = ref[0]
    for k in range(1, count):
        out = out + ref[k]
    return out


def wrap(index, size):
    return jnp.where(index >= size, index - size, index)


def lane_of(x):
    return lax.broadcasted_iota(jnp.int32, x.shape, 1)


def pack(tiles):
    spare = lane_of(tiles[3]) >= RANK
    return [
        jnp.where(spare, pltpu.roll(tiles[3], RANK - 32 * m, 1), tiles[m]) for m in range(3)
    ]


def unpack(tiles):
    lane = lane_of(tiles[0])
    last = jnp.zeros_like(tiles[0])
    for m in (2, 1, 0):
        last = jnp.where(lane < 32 * m + 32, pltpu.roll(tiles[m], 32 * m + 32, 1), last)
    zero = jnp.zeros_like(last)
    return [jnp.where(lane < RANK, tile, zero) for tile in tiles] + [
        jnp.where(lane < RANK, last, zero)
    ]


def kernel(
    tensor, packed,
    out,
    data, mine2, rowg, bandg, row_t, band_t, bandx_t, tb_t,
    turned, prod, by_frame, part, recv1, sum1, recv2, fin, recv3,
    colg, colf, low, folded, partials,
    fpart, fsum, fx, gpart, grecv, gall, gcols,
    rsend, rcore, rsum, rrecv, bsend, brecv,
    local_sems, send_sems, recv_sems,
):
    a = lax.axis_index("gx")
    g = lax.axis_index("gy")
    lz = lax.div(g, 2)
    c = g - 2 * lz
    l = lax.div(lz, 8)
    z = lz - 8 * l
    p = l * 2 + c
    other = 1 - c
    partner = lz * 2 + other
    gx_peers = [wrap(a + k, NX) for k in range(1, NX)]
    core_peers = [wrap(lz + k, NLZ) * 2 + c for k in range(1, NLZ)]

    def send(src, dst, sem, device):
        pltpu.make_async_remote_copy(
            src_ref=src, dst_ref=dst, send_sem=send_sems.at[sem], recv_sem=recv_sems.at[sem],
            device_id=device, device_id_type=MESH,
        ).start()

    def arrived(ref, sem):
        pltpu.make_async_copy(ref, ref, recv_sems.at[sem]).wait()

    def sent(ref, sem):
        pltpu.make_async_copy(ref, ref, send_sems.at[sem]).wait()

    barrier = pltpu.get_barrier_semaphore()
    for to in core_peers + [partner, (lz + 8 - 16 * l) * 2 + other]:
        pl.semaphore_signal(barrier, inc=1, device_id=(a, to), device_id_type=MESH)
    for to in gx_peers:
        pl.semaphore_signal(barrier, inc=1, device_id=(to, g), device_id_type=MESH)

    for k in range(LOADS):
        span = pl.ds(k * (TB // LOADS), TB // LOADS)
        pltpu.make_async_copy(tensor.at[span], data.at[span], local_sems.at[k]).start()

    tb_t[...] = jnp.zeros_like(tb_t)
    mine2[...] = packed[CW : CW + BW]
    time8 = packed[MSG + 8 :]
    rowg[c, lz] = packed[MSG : MSG + 8]
    bandg[a] = mine2[...]
    for m, tile in enumerate(pack([packed[8 * m : 8 * m + 8] for m in range(4)])):
        colg[c, lz, 8 * m : 8 * m + 8] = tile

    pl.semaphore_wait(barrier, NLZ + 1 + NX - 1)

    for to in core_peers:
        send(rowg.at[c, lz], rowg.at[c, lz], S_ROW, (a, to))
    for to in gx_peers:
        send(mine2, bandg.at[a], S_BAND, (to, g))

    @pl.loop(0, LOADS)
    def _(k):
        per = TB // LOADS
        span = pl.ds(k * per, per)
        pltpu.make_async_copy(tensor.at[span], data.at[span], local_sems.at[k]).wait()
        for i in range(per):
            at = pl.multiple_of((k * per + i) * ROWS, ROWS)
            turned[:, pl.ds(at, ROWS)] = data[k * per + i].T

        @pl.when(k == 0)
        def _():
            for to in core_peers:
                send(colg.at[c, lz], colg.at[c, lz], S_COL, (a, to))

    arrived(rowg.at[0, pl.ds(0, NLZ - 1)], S_ROW)
    send(rowg.at[c], rowg.at[c], S_ROWC, (a, partner))
    arrived(bandg.at[pl.ds(0, NX - 1)], S_BAND)
    for k in range(NX):
        band_t[BW * k : BW * k + BW] = bandg[k]
    for t in range(FRAMES):
        tb_t[t * BANDS : (t + 1) * BANDS] = time8[t : t + 1] * band_t[...]
    tb_t[TB : TB + BANDS] = band_t[...]
    arrived(rowg.at[0], S_ROWC)
    for k in range(NY):
        row_t[RW * k : RW * k + RW] = rowg[k % 2, k // 2, 0:RW]
        bandx_t[RW * k : RW * k + RW] = rowg[k % 2, k // 2, RW : 2 * RW]

    @pl.loop(0, BANDS)
    def _(k):
        span = pl.ds(pl.multiple_of(k * ROWS, ROWS), ROWS)
        rows = row_t[...]
        plain = (tb_t[pl.ds(TB + k, 1)] * rows).astype(BF16)
        for t in range(FRAMES):
            prod[t, span, 0:LANES] = (tb_t[pl.ds(t * BANDS + k, 1)] * rows).astype(BF16)
            prod[t, span, LANES:] = plain

    def send_pieces(n):
        span = pl.ds(n * PER, PER)
        arrived(recv1.at[span], S_R1 + n)
        sum1[span] = part[c, span] + recv1[span]
        for i in range(PER):
            k = n * PER + i

            @pl.when(k != lz)
            def _():
                send(sum1.at[k], recv2.at[lz], S_R2, (a, k * 2 + c))

    @pl.loop(0, CHUNKS)
    def _(n):
        here = pl.ds(pl.multiple_of(n * CHUNK, CHUNK), CHUNK)
        acc = jnp.zeros((CHUNK, LANES), F32)
        for t in range(FRAMES):
            both = dot(turned[here, t * HALF : (t + 1) * HALF], prod[t])
            by_frame[t, here] = both[:, LANES:]
            acc = acc + both[:, 0:LANES]
        acc = acc.reshape(CHUNK // CW, 4, 8, LANES)
        tiles = pack([acc[:, m].reshape(CHUNK // 4, LANES) for m in range(4)])
        for k in range(CHUNK // CW):
            for m in range(3):
                part[k % 2, n * PER + k // 2, 8 * m : 8 * m + 8] = tiles[m][8 * k : 8 * k + 8]
        span = pl.ds(n * PER, PER)
        send(part.at[other, span], recv1.at[span], S_R1 + n, (a, partner))

        @pl.when(n > 0)
        def _():
            send_pieces(n - 1)

    arrived(colg.at[0, pl.ds(0, NLZ - 1)], S_COL)
    send(colg.at[c], colg.at[c], S_COLC, (a, partner))

    for i, ref in enumerate((row_t, bandx_t)):
        gram = exact(ref[...].T, ref[...])
        for k in range(4):
            gpart[k, i] = gram[24 * k : 24 * k + 24]
    grecv[a] = gpart[p]
    send_pieces(CHUNKS - 1)
    for to in gx_peers:
        send(gpart.at[p], grecv.at[a], S_GRAM, (to, g))

    arrived(colg.at[0], S_COLC)
    for i in range(2):
        tiles = unpack(
            [colg[i, :, 8 * m : 8 * m + 8].reshape(8 * NLZ, LANES) for m in range(3)]
        )
        for k in range(NLZ):
            block = jnp.concatenate([tile[8 * k : 8 * k + 8] for tile in tiles], axis=0)
            at = (2 * k + i) * CW
            colf[at : at + CW] = block
            low[at : at + CW] = block.astype(BF16)

    fpart[...] = jnp.zeros_like(fpart)
    for t in range(FRAMES):
        fpart[t : t + 1] = jnp.sum(
            by_frame[t] * low[...].astype(F32), axis=0, keepdims=True
        )

    def send_rows(q):
        span = pl.ds(q * PERQ, PERQ)
        arrived(rcore.at[span], S_T1 + q)
        rsum[span] = rsend[c, span] + rcore[span]
        for i in range(PERQ):
            k = q * PERQ + i

            @pl.when(k != lz)
            def _():
                send(rsum.at[k], rrecv.at[lz], S_ROWS, (a, k * 2 + c))

    @pl.loop(0, 4)
    def _(q):
        here = pl.ds(pl.multiple_of(q * QROWS, QROWS), QROWS)
        folded[...] = dot(data[:, here, :].reshape(TB * QROWS, COLS), low[...])
        rows = jnp.zeros((QROWS, LANES), F32)
        row_here = row_t[here]
        for j in range(TB):
            block = folded[j * QROWS : (j + 1) * QROWS]
            rows = rows + block * tb_t[j : j + 1]
            block = block * row_here
            partials[q, j] = jnp.sum(block.reshape(QROWS // 8, 8, LANES), axis=0)
        frames = fpart[...]
        for i in range(NY // 4):
            rsend[i % 2, q * PERQ + i // 2, 0:RW] = rows[RW * i : RW * i + RW]
            rsend[i % 2, q * PERQ + i // 2, RW : 2 * RW] = frames
        span = pl.ds(q * PERQ, PERQ)
        send(rsend.at[other, span], rcore.at[span], S_T1 + q, (a, partner))

        @pl.when(q > 0)
        def _():
            send_rows(q - 1)

    sums = total(partials, 4)
    bands = jnp.zeros((BANDS, LANES), F32)
    for t in range(FRAMES):
        bands = bands + time8[t : t + 1] * jnp.sum(sums[t * BANDS : (t + 1) * BANDS], axis=1)
    for k in range(NX):
        bsend[k] = bands[BW * k : BW * k + BW]
    for k in range(1, NX):
        to = wrap(a + k, NX)
        send(bsend.at[to], brecv.at[a], S_BANDS, (to, g))
    brecv[a] = bsend[a]

    arrived(grecv.at[pl.ds(0, NX - 1)], S_GRAM)
    gall[p] = total(grecv, NX)
    for k in range(1, 4):
        to = wrap(p + k, 4)
        to_l = lax.div(to, 2)
        send(gall.at[p], gall.at[p], S_GRAMP, (a, (to_l * 8 + z) * 2 + to - 2 * to_l))
    send_rows(3)
    rrecv[lz] = rsum[lz]
    recv2[lz] = sum1[lz]
    arrived(recv2.at[pl.ds(0, NLZ - 1)], S_R2)
    fin[...] = total(recv2, NLZ)
    recv3[a] = fin[...]
    for to in gx_peers:
        send(fin, recv3.at[a], S_R3, (to, g))

    gcols[...] = jnp.zeros_like(gcols)

    @pl.loop(0, 4)
    def _(i):
        block = colf[pl.ds(pl.multiple_of(i * 256, 256), 256)]
        gcols[...] += exact(block.T, block)

    arrived(rrecv.at[pl.ds(0, NLZ - 1)], S_ROWS)
    row_sums = total(rrecv, NLZ)
    fsum[...] = row_sums[RW : RW + FRAMES]
    fx[a] = fsum[...]
    for to in gx_peers:
        send(fsum, fx.at[a], S_F2, (to, g))

    gram_cols = gcols[...]
    arrived(gall.at[pl.ds(0, 3)], S_GRAMP)
    pad = jnp.zeros((LANES - RANK, LANES), F32)
    gram_rows, gram_bands = (
        jnp.concatenate([gall[:, i].reshape(RANK, LANES), pad], axis=0) for i in range(2)
    )
    time_n = jnp.concatenate([time8, jnp.zeros((LANES - 8, LANES), F32)], axis=0).T
    gram_time = time_n[:, 0:1] * time8[0:1] + time_n[:, 1:2] * time8[1:2]
    row_model = exact(packed[MSG : MSG + 8], gram_cols * gram_bands * gram_time)
    col_model = exact(packed[0:CW], gram_rows * gram_bands * gram_time)
    band_model = exact(packed[CW:MSG], gram_rows * gram_cols * gram_time)
    time_model = exact(time8, gram_rows * gram_cols * gram_bands)

    out[CW + 8 : CW + 8 + RW] = row_model[0:RW] - row_sums[0:RW]
    arrived(recv3.at[pl.ds(0, NX - 1)], S_R3)
    sums = total(recv3, NX)
    sums = jnp.concatenate(unpack([sums[8 * m : 8 * m + 8] for m in range(3)]), axis=0)
    out[0:CW] = col_model - sums
    arrived(brecv.at[pl.ds(0, NX - 1)], S_BANDS)
    out[CW + 16 : CW + 16 + BW] = band_model[0:BW] - total(brecv, NX)
    arrived(fx.at[pl.ds(0, NX - 1)], S_F2)
    out[CW : CW + FRAMES] = time_model[0:FRAMES] - total(fx, NX)

    sent(rowg.at[0, pl.ds(0, NLZ - 1)], S_ROW)
    sent(rowg.at[0], S_ROWC)
    sent(bandg.at[pl.ds(0, NX - 1)], S_BAND)
    sent(colg.at[0, pl.ds(0, NLZ - 1)], S_COL)
    sent(colg.at[0], S_COLC)
    for n in range(CHUNKS):
        sent(recv1.at[pl.ds(n * PER, PER)], S_R1 + n)
    sent(recv2.at[pl.ds(0, NLZ - 1)], S_R2)
    sent(recv3.at[pl.ds(0, NX - 1)], S_R3)
    sent(fx.at[pl.ds(0, NX - 1)], S_F2)
    sent(grecv.at[pl.ds(0, NX - 1)], S_GRAM)
    sent(gall.at[pl.ds(0, 3)], S_GRAMP)
    for q in range(4):
        sent(rcore.at[pl.ds(q * PERQ, PERQ)], S_T1 + q)
    sent(rrecv.at[pl.ds(0, NLZ - 1)], S_ROWS)
    sent(brecv.at[pl.ds(0, NX - 1)], S_BANDS)


def shards(tensor, row_factor, column_factor, band_factor, time_factor):
    v = pltpu.VMEM
    packed = jnp.zeros((MSG + 16, LANES), F32)
    pieces = ((0, column_factor), (CW, band_factor), (MSG, row_factor))
    pieces += ((MSG + RW, band_factor), (MSG + 8, time_factor))
    for at, x in pieces:
        x = x.T
        packed = packed + jnp.pad(x, ((at, MSG + 16 - at - x.shape[0]), (0, LANES - RANK)))
    out = pl.pallas_call(
        kernel,
        out_shape=jax.ShapeDtypeStruct((CW + 24, LANES), F32),
        in_specs=[pl.BlockSpec(memory_space=pl.ANY), pl.BlockSpec(memory_space=v)],
        out_specs=pl.BlockSpec(memory_space=v),
        scratch_shapes=[
            v((TB, ROWS, COLS), BF16),
            v((BW, LANES), F32),
            v((2, NLZ, 8, LANES), F32),
            v((NX, BW, LANES), F32),
            v((ROWS, LANES), F32),
            v((BANDS, LANES), F32),
            v((NY * RW, LANES), F32),
            v((LANES, LANES), F32),
            v((COLS, TB * ROWS), BF16),
            v((FRAMES, HALF, 2 * LANES), BF16),
            v((FRAMES, COLS, LANES), F32),
            v((2, NLZ, PACK, LANES), F32),
            v((NLZ, PACK, LANES), F32),
            v((NLZ, PACK, LANES), F32),
            v((NLZ, PACK, LANES), F32),
            v((PACK, LANES), F32),
            v((NX, PACK, LANES), F32),
            v((2, NLZ, PACK, LANES), F32),
            v((COLS, LANES), F32),
            v((COLS, LANES), BF16),
            v((TB * QROWS, LANES), F32),
            v((4, TB, 8, LANES), F32),
            v((RW, LANES), F32),
            v((FRAMES, LANES), F32),
            v((NX, FRAMES, LANES), F32),
            v((4, 2, 24, LANES), F32),
            v((NX, 2, 24, LANES), F32),
            v((4, 2, 24, LANES), F32),
            v((LANES, LANES), F32),
            v((2, NLZ, 8, LANES), F32),
            v((NLZ, 8, LANES), F32),
            v((NLZ, 8, LANES), F32),
            v((NLZ, 8, LANES), F32),
            v((NX, BW, LANES), F32),
            v((NX, BW, LANES), F32),
            pltpu.SemaphoreType.DMA((LOADS,)),
            pltpu.SemaphoreType.DMA((N_SEMS,)),
            pltpu.SemaphoreType.DMA((N_SEMS,)),
        ],
        compiler_params=pltpu.CompilerParams(
            collective_id=0, has_side_effects=True, vmem_limit_bytes=48 * 1024 * 1024
        ),
        cost_estimate=pl.CostEstimate(
            flops=4 * RANK * TB * ROWS * COLS, bytes_accessed=2 * TB * ROWS * COLS, transcendentals=0
        ),
    )(
        tensor.reshape(TB, ROWS, COLS),
        packed,
    )
    places = ((CW + 8, RW), (0, CW), (CW + 16, BW), (CW, FRAMES))
    return tuple(out[at : at + n, 0:RANK].T for at, n in places)


def solution(mesh):
    return jax.shard_map(
        shards,
        mesh=mesh,
        in_specs=(
            P(None, "gy", "gx", None),
            P(None, ("gx", "gy")),
            P(None, "gy"),
            P(None, ("gy", "gx")),
            P(),
        ),
        out_specs=(P(None, ("gx", "gy")), P(None, "gy"), P(None, ("gy", "gx")), P()),
        check_vma=False,
    )
```

```python
import jax
import jax.numpy as jnp
from jax import lax
from jax.experimental import pallas as pl
from jax.experimental.pallas import tpu as pltpu
from jax.sharding import PartitionSpec as P

MESH = pl.DeviceIdType.MESH
HIGHEST = lax.Precision.HIGHEST
F32 = jnp.float32
BF16 = jnp.bfloat16

NX, NY, NLZ = 8, 32, 16
RANK, LANES = 96, 128
FRAMES, BANDS, ROWS, COLS = 2, 16, 128, 1024
RW, CW, BW = 4, 32, 2
PACK = CW * RANK // LANES
TB = FRAMES * BANDS
HALF = BANDS * ROWS
CHUNKS = 2
CHUNK = COLS // CHUNKS
PER = NLZ // CHUNKS
LOADS = 8
MSG = CW + 8
QROWS = ROWS // 4

(
    S_ROW, S_BAND, S_BANDX, S_COL, S_COLC, S_R1, S_R2, S_R3, S_F1, S_F2,
    S_GRAM, S_GRAMP, S_ROWS, S_BANDS,
) = [0, 1, 2, 3, 4, 5, 7, 8, 9, 10, 11, 12, 13, 14]
N_SEMS = 15


def dot(x, y):
    return jnp.dot(x, y, preferred_element_type=F32)


def exact(x, y):
    return jnp.dot(x, y, precision=HIGHEST, preferred_element_type=F32)


def total(ref, count):
    out = ref[0]
    for k in range(1, count):
        out = out + ref[k]
    return out


def wrap(index, size):
    return jnp.where(index >= size, index - size, index)


def lane_of(x):
    return lax.broadcasted_iota(jnp.int32, x.shape, 1)


def pack(tiles):
    spare = lane_of(tiles[3]) >= RANK
    return [
        jnp.where(spare, pltpu.roll(tiles[3], RANK - 32 * m, 1), tiles[m]) for m in range(3)
    ]


def unpack(tiles):
    lane = lane_of(tiles[0])
    last = jnp.zeros_like(tiles[0])
    for m in (2, 1, 0):
        last = jnp.where(lane < 32 * m + 32, pltpu.roll(tiles[m], 32 * m + 32, 1), last)
    zero = jnp.zeros_like(last)
    return [jnp.where(lane < RANK, tile, zero) for tile in tiles] + [
        jnp.where(lane < RANK, last, zero)
    ]


def kernel(
    tensor, packed,
    out,
    data, mine4, mine2, rowg, bandg, bandx, row_t, band_t, bandx_t, tb_t,
    turned, prod, by_frame, part, recv1, sum1, recv2, fin, recv3,
    colg, colf, low, folded, partials,
    fpart, fg, fsum, fx, gpart, grecv, gall, gcols,
    rsend, rrecv, bsend, brecv,
    local_sems, send_sems, recv_sems,
):
    a = lax.axis_index("gx")
    g = lax.axis_index("gy")
    lz = lax.div(g, 2)
    c = g - 2 * lz
    l = lax.div(lz, 8)
    z = lz - 8 * l
    p = l * 2 + c
    other = 1 - c
    partner = lz * 2 + other
    gy_peers = [wrap(g + k, NY) for k in range(1, NY)]
    gx_peers = [wrap(a + k, NX) for k in range(1, NX)]
    core_peers = [wrap(lz + k, NLZ) * 2 + c for k in range(1, NLZ)]

    def send(src, dst, sem, device):
        pltpu.make_async_remote_copy(
            src_ref=src, dst_ref=dst, send_sem=send_sems.at[sem], recv_sem=recv_sems.at[sem],
            device_id=device, device_id_type=MESH,
        ).start()

    def arrived(ref, sem):
        pltpu.make_async_copy(ref, ref, recv_sems.at[sem]).wait()

    def sent(ref, sem):
        pltpu.make_async_copy(ref, ref, send_sems.at[sem]).wait()

    barrier = pltpu.get_barrier_semaphore()
    for to in gy_peers:
        pl.semaphore_signal(barrier, inc=1, device_id=(a, to), device_id_type=MESH)
    for to in gx_peers:
        pl.semaphore_signal(barrier, inc=1, device_id=(to, g), device_id_type=MESH)

    for k in range(LOADS):
        span = pl.ds(k * (TB // LOADS), TB // LOADS)
        pltpu.make_async_copy(tensor.at[span], data.at[span], local_sems.at[k]).start()

    tb_t[...] = jnp.zeros_like(tb_t)
    mine2[...] = packed[CW : CW + BW]
    mine4[...] = packed[MSG : MSG + RW]
    time8 = packed[MSG + 8 :]
    rowg[g] = mine4[...]
    bandg[a] = mine2[...]
    bandx[g] = mine2[...]
    for m, tile in enumerate(pack([packed[8 * m : 8 * m + 8] for m in range(4)])):
        colg[c, lz, 8 * m : 8 * m + 8] = tile

    pl.semaphore_wait(barrier, NY - 1 + NX - 1)

    for to in gy_peers:
        send(mine4, rowg.at[g], S_ROW, (a, to))
    for to in gx_peers:
        send(mine2, bandg.at[a], S_BAND, (to, g))

    @pl.loop(0, LOADS)
    def _(k):
        per = TB // LOADS
        span = pl.ds(k * per, per)
        pltpu.make_async_copy(tensor.at[span], data.at[span], local_sems.at[k]).wait()
        for i in range(per):
            at = pl.multiple_of((k * per + i) * ROWS, ROWS)
            turned[:, pl.ds(at, ROWS)] = data[k * per + i].T

    for to in core_peers:
        send(colg.at[c, lz], colg.at[c, lz], S_COL, (a, to))
    for to in gy_peers:
        send(mine2, bandx.at[g], S_BANDX, (a, to))

    arrived(bandg.at[pl.ds(0, NX - 1)], S_BAND)
    for k in range(NX):
        band_t[BW * k : BW * k + BW] = bandg[k]
    for t in range(FRAMES):
        tb_t[t * BANDS : (t + 1) * BANDS] = time8[t : t + 1] * band_t[...]
    tb_t[TB : TB + BANDS] = band_t[...]
    arrived(rowg.at[pl.ds(0, NY - 1)], S_ROW)
    for k in range(NY):
        row_t[RW * k : RW * k + RW] = rowg[k]

    @pl.loop(0, BANDS)
    def _(k):
        span = pl.ds(pl.multiple_of(k * ROWS, ROWS), ROWS)
        rows = row_t[...]
        plain = (tb_t[pl.ds(TB + k, 1)] * rows).astype(BF16)
        for t in range(FRAMES):
            prod[t, span, 0:LANES] = (tb_t[pl.ds(t * BANDS + k, 1)] * rows).astype(BF16)
            prod[t, span, LANES:] = plain

    def send_pieces(n):
        span = pl.ds(n * PER, PER)
        arrived(recv1.at[span], S_R1 + n)
        sum1[span] = part[c, span] + recv1[span]
        for i in range(PER):
            k = n * PER + i

            @pl.when(k != lz)
            def _():
                send(sum1.at[k], recv2.at[lz], S_R2, (a, k * 2 + c))

    @pl.loop(0, CHUNKS)
    def _(n):
        here = pl.ds(pl.multiple_of(n * CHUNK, CHUNK), CHUNK)
        acc = jnp.zeros((CHUNK, LANES), F32)
        for t in range(FRAMES):
            both = dot(turned[here, t * HALF : (t + 1) * HALF], prod[t])
            by_frame[t, here] = both[:, LANES:]
            acc = acc + both[:, 0:LANES]
        acc = acc.reshape(CHUNK // CW, 4, 8, LANES)
        tiles = pack([acc[:, m].reshape(CHUNK // 4, LANES) for m in range(4)])
        for k in range(CHUNK // CW):
            for m in range(3):
                part[k % 2, n * PER + k // 2, 8 * m : 8 * m + 8] = tiles[m][8 * k : 8 * k + 8]
        span = pl.ds(n * PER, PER)
        send(part.at[other, span], recv1.at[span], S_R1 + n, (a, partner))

        @pl.when(n > 0)
        def _():
            send_pieces(n - 1)

    gram = exact(row_t[...].T, row_t[...])
    for k in range(4):
        gpart[k, 0] = gram[24 * k : 24 * k + 24]
    send_pieces(CHUNKS - 1)
    arrived(colg.at[0, pl.ds(0, NLZ - 1)], S_COL)
    send(colg.at[c], colg.at[c], S_COLC, (a, partner))
    arrived(bandx.at[pl.ds(0, NY - 1)], S_BANDX)
    for k in range(NY):
        bandx_t[BW * k : BW * k + BW] = bandx[k]
    gram = exact(bandx_t[...].T, bandx_t[...])
    for k in range(4):
        gpart[k, 1] = gram[24 * k : 24 * k + 24]
    grecv[a] = gpart[p]
    for to in gx_peers:
        send(gpart.at[p], grecv.at[a], S_GRAM, (to, g))

    arrived(colg.at[0], S_COLC)
    for i in range(2):
        tiles = unpack(
            [colg[i, :, 8 * m : 8 * m + 8].reshape(8 * NLZ, LANES) for m in range(3)]
        )
        for k in range(NLZ):
            block = jnp.concatenate([tile[8 * k : 8 * k + 8] for tile in tiles], axis=0)
            at = (2 * k + i) * CW
            colf[at : at + CW] = block
            low[at : at + CW] = block.astype(BF16)

    for t in range(FRAMES):
        fpart[t : t + 1] = jnp.sum(
            by_frame[t] * low[...].astype(F32), axis=0, keepdims=True
        )
    fg[g] = fpart[...]
    for to in gy_peers:
        send(fpart, fg.at[g], S_F1, (a, to))

    @pl.loop(0, 4)
    def _(q):
        here = pl.ds(pl.multiple_of(q * QROWS, QROWS), QROWS)
        folded[...] = dot(data[:, here, :].reshape(TB * QROWS, COLS), low[...])
        rows = jnp.zeros((QROWS, LANES), F32)
        row_here = row_t[here]
        for j in range(TB):
            block = folded[j * QROWS : (j + 1) * QROWS]
            rows = rows + block * tb_t[j : j + 1]
            block = block * row_here
            partials[q, j] = jnp.sum(block.reshape(QROWS // 8, 8, LANES), axis=0)
        for i in range(NY // 4):
            rsend[q * (NY // 4) + i] = rows[RW * i : RW * i + RW]
        for i in range(NY // 4):
            k = q * (NY // 4) + i

            @pl.when(k != g)
            def _():
                send(rsend.at[k], rrecv.at[g], S_ROWS, (a, k))

    sums = total(partials, 4)
    bands = jnp.zeros((BANDS, LANES), F32)
    for t in range(FRAMES):
        bands = bands + time8[t : t + 1] * jnp.sum(sums[t * BANDS : (t + 1) * BANDS], axis=1)
    for k in range(NX):
        bsend[k] = bands[BW * k : BW * k + BW]
    for k in range(1, NX):
        to = wrap(a + k, NX)
        send(bsend.at[to], brecv.at[a], S_BANDS, (to, g))
    brecv[a] = bsend[a]
    rrecv[g] = rsend[g]

    arrived(grecv.at[pl.ds(0, NX - 1)], S_GRAM)
    gall[p] = total(grecv, NX)
    for k in range(1, 4):
        to = wrap(p + k, 4)
        to_l = lax.div(to, 2)
        send(gall.at[p], gall.at[p], S_GRAMP, (a, (to_l * 8 + z) * 2 + to - 2 * to_l))
    arrived(fg.at[pl.ds(0, NY - 1)], S_F1)
    fsum[...] = total(fg, NY)
    fx[a] = fsum[...]
    for to in gx_peers:
        send(fsum, fx.at[a], S_F2, (to, g))
    recv2[lz] = sum1[lz]
    arrived(recv2.at[pl.ds(0, NLZ - 1)], S_R2)
    fin[...] = total(recv2, NLZ)
    recv3[a] = fin[...]
    for to in gx_peers:
        send(fin, recv3.at[a], S_R3, (to, g))

    gcols[...] = jnp.zeros_like(gcols)

    @pl.loop(0, 4)
    def _(i):
        block = colf[pl.ds(pl.multiple_of(i * 256, 256), 256)]
        gcols[...] += exact(block.T, block)

    gram_cols = gcols[...]
    arrived(gall.at[pl.ds(0, 3)], S_GRAMP)
    pad = jnp.zeros((LANES - RANK, LANES), F32)
    gram_rows, gram_bands = (
        jnp.concatenate([gall[:, i].reshape(RANK, LANES), pad], axis=0) for i in range(2)
    )
    time_n = jnp.concatenate([time8, jnp.zeros((LANES - 8, LANES), F32)], axis=0).T
    gram_time = time_n[:, 0:1] * time8[0:1] + time_n[:, 1:2] * time8[1:2]
    row_model = exact(packed[MSG : MSG + 8], gram_cols * gram_bands * gram_time)
    col_model = exact(packed[0:CW], gram_rows * gram_bands * gram_time)
    band_model = exact(packed[CW:MSG], gram_rows * gram_cols * gram_time)
    time_model = exact(time8, gram_rows * gram_cols * gram_bands)

    arrived(fx.at[pl.ds(0, NX - 1)], S_F2)
    out[CW : CW + FRAMES] = time_model[0:FRAMES] - total(fx, NX)
    arrived(recv3.at[pl.ds(0, NX - 1)], S_R3)
    sums = total(recv3, NX)
    sums = jnp.concatenate(unpack([sums[8 * m : 8 * m + 8] for m in range(3)]), axis=0)
    out[0:CW] = col_model - sums
    arrived(rrecv.at[pl.ds(0, NY - 1)], S_ROWS)
    out[CW + 8 : CW + 8 + RW] = row_model[0:RW] - total(rrecv, NY)
    arrived(brecv.at[pl.ds(0, NX - 1)], S_BANDS)
    out[CW + 16 : CW + 16 + BW] = band_model[0:BW] - total(brecv, NX)

    sent(rowg.at[pl.ds(0, NY - 1)], S_ROW)
    sent(bandg.at[pl.ds(0, NX - 1)], S_BAND)
    sent(bandx.at[pl.ds(0, NY - 1)], S_BANDX)
    sent(colg.at[0, pl.ds(0, NLZ - 1)], S_COL)
    sent(colg.at[0], S_COLC)
    for n in range(CHUNKS):
        sent(recv1.at[pl.ds(n * PER, PER)], S_R1 + n)
    sent(recv2.at[pl.ds(0, NLZ - 1)], S_R2)
    sent(recv3.at[pl.ds(0, NX - 1)], S_R3)
    sent(fg.at[pl.ds(0, NY - 1)], S_F1)
    sent(fx.at[pl.ds(0, NX - 1)], S_F2)
    sent(grecv.at[pl.ds(0, NX - 1)], S_GRAM)
    sent(gall.at[pl.ds(0, 3)], S_GRAMP)
    sent(rrecv.at[pl.ds(0, NY - 1)], S_ROWS)
    sent(brecv.at[pl.ds(0, NX - 1)], S_BANDS)


def shards(tensor, row_factor, column_factor, band_factor, time_factor):
    v = pltpu.VMEM
    packed = jnp.zeros((MSG + 16, LANES), F32)
    pieces = ((0, column_factor), (CW, band_factor), (MSG, row_factor), (MSG + 8, time_factor))
    for at, x in pieces:
        x = x.T
        packed = packed + jnp.pad(x, ((at, MSG + 16 - at - x.shape[0]), (0, LANES - RANK)))
    out = pl.pallas_call(
        kernel,
        out_shape=jax.ShapeDtypeStruct((CW + 24, LANES), F32),
        in_specs=[pl.BlockSpec(memory_space=pl.ANY), pl.BlockSpec(memory_space=v)],
        out_specs=pl.BlockSpec(memory_space=v),
        scratch_shapes=[
            v((TB, ROWS, COLS), BF16),
            v((RW, LANES), F32),
            v((BW, LANES), F32),
            v((NY, RW, LANES), F32),
            v((NX, BW, LANES), F32),
            v((NY, BW, LANES), F32),
            v((ROWS, LANES), F32),
            v((BANDS, LANES), F32),
            v((NY * BW, LANES), F32),
            v((LANES, LANES), F32),
            v((COLS, TB * ROWS), BF16),
            v((FRAMES, HALF, 2 * LANES), BF16),
            v((FRAMES, COLS, LANES), F32),
            v((2, NLZ, PACK, LANES), F32),
            v((NLZ, PACK, LANES), F32),
            v((NLZ, PACK, LANES), F32),
            v((NLZ, PACK, LANES), F32),
            v((PACK, LANES), F32),
            v((NX, PACK, LANES), F32),
            v((2, NLZ, PACK, LANES), F32),
            v((COLS, LANES), F32),
            v((COLS, LANES), BF16),
            v((TB * QROWS, LANES), F32),
            v((4, TB, 8, LANES), F32),
            v((FRAMES, LANES), F32),
            v((NY, FRAMES, LANES), F32),
            v((FRAMES, LANES), F32),
            v((NX, FRAMES, LANES), F32),
            v((4, 2, 24, LANES), F32),
            v((NX, 2, 24, LANES), F32),
            v((4, 2, 24, LANES), F32),
            v((LANES, LANES), F32),
            v((NY, RW, LANES), F32),
            v((NY, RW, LANES), F32),
            v((NX, BW, LANES), F32),
            v((NX, BW, LANES), F32),
            pltpu.SemaphoreType.DMA((LOADS,)),
            pltpu.SemaphoreType.DMA((N_SEMS,)),
            pltpu.SemaphoreType.DMA((N_SEMS,)),
        ],
        compiler_params=pltpu.CompilerParams(
            collective_id=0, has_side_effects=True, vmem_limit_bytes=48 * 1024 * 1024
        ),
        cost_estimate=pl.CostEstimate(
            flops=4 * RANK * TB * ROWS * COLS, bytes_accessed=2 * TB * ROWS * COLS, transcendentals=0
        ),
    )(
        tensor.reshape(TB, ROWS, COLS),
        packed,
    )
    places = ((CW + 8, RW), (0, CW), (CW + 16, BW), (CW, FRAMES))
    return tuple(out[at : at + n, 0:RANK].T for at, n in places)


def solution(mesh):
    return jax.shard_map(
        shards,
        mesh=mesh,
        in_specs=(
            P(None, "gy", "gx", None),
            P(None, ("gx", "gy")),
            P(None, "gy"),
            P(None, ("gy", "gx")),
            P(),
        ),
        out_specs=(P(None, ("gx", "gy")), P(None, "gy"), P(None, ("gy", "gx")), P()),
        check_vma=False,
    )
```

```python
import jax
import jax.numpy as jnp
from jax import lax
from jax.experimental import pallas as pl
from jax.experimental.pallas import tpu as pltpu
from jax.sharding import PartitionSpec as P

MESH = pl.DeviceIdType.MESH
HIGHEST = lax.Precision.HIGHEST
F32 = jnp.float32
BF16 = jnp.bfloat16

NX, NY, NLZ = 8, 32, 16
RANK, LANES = 96, 128
FRAMES, BANDS, ROWS, COLS = 2, 16, 128, 1024
RW, CW, BW = 4, 32, 2
PACK = CW * RANK // LANES
TB = FRAMES * BANDS
HALF = BANDS * ROWS
CHUNKS = 4
CHUNK = COLS // CHUNKS
PER = NLZ // CHUNKS
LOADS = 8
MSG = CW + 8
QROWS = ROWS // 4

(
    S_ROW, S_BAND, S_BANDX, S_COL, S_COLC, S_R1, S_R2, S_R3, S_F1, S_F2,
    S_GRAM, S_GRAMP, S_ROWS, S_BANDS,
) = [0, 1, 2, 3, 4, 5, 9, 10, 11, 12, 13, 14, 15, 16]
N_SEMS = 17


def dot(x, y):
    return jnp.dot(x, y, preferred_element_type=F32)


def exact(x, y):
    return jnp.dot(x, y, precision=HIGHEST, preferred_element_type=F32)


def total(ref, count):
    out = ref[0]
    for k in range(1, count):
        out = out + ref[k]
    return out


def wrap(index, size):
    return jnp.where(index >= size, index - size, index)


def lane_of(x):
    return lax.broadcasted_iota(jnp.int32, x.shape, 1)


def pack(tiles):
    spare = lane_of(tiles[3]) >= RANK
    return [
        jnp.where(spare, pltpu.roll(tiles[3], RANK - 32 * m, 1), tiles[m]) for m in range(3)
    ]


def unpack(tiles):
    lane = lane_of(tiles[0])
    last = jnp.zeros_like(tiles[0])
    for m in (2, 1, 0):
        last = jnp.where(lane < 32 * m + 32, pltpu.roll(tiles[m], 32 * m + 32, 1), last)
    zero = jnp.zeros_like(last)
    return [jnp.where(lane < RANK, tile, zero) for tile in tiles] + [
        jnp.where(lane < RANK, last, zero)
    ]


def kernel(
    tensor, row_in, col_in, band_in, time_in,
    row_out, col_out, band_out, time_out,
    packed, row_v, col_v, band_v, time_v,
    data, mine4, mine2, rowg, bandg, bandx, row_t, band_t, bandx_t, tb_t,
    turned, prod, by_frame, part, recv1, sum1, recv2, fin, recv3,
    colg, colf, low, folded, partials,
    fpart, fg, fsum, fx, gpart, grecv, gall, gcols,
    rsend, rrecv, bsend, brecv,
    local_sems, send_sems, recv_sems,
):
    a = lax.axis_index("gx")
    g = lax.axis_index("gy")
    lz = lax.div(g, 2)
    c = g - 2 * lz
    l = lax.div(lz, 8)
    z = lz - 8 * l
    p = l * 2 + c
    other = 1 - c
    partner = lz * 2 + other
    gy_peers = [wrap(g + k, NY) for k in range(1, NY)]
    gx_peers = [wrap(a + k, NX) for k in range(1, NX)]
    core_peers = [wrap(lz + k, NLZ) * 2 + c for k in range(1, NLZ)]

    def send(src, dst, sem, device):
        pltpu.make_async_remote_copy(
            src_ref=src, dst_ref=dst, send_sem=send_sems.at[sem], recv_sem=recv_sems.at[sem],
            device_id=device, device_id_type=MESH,
        ).start()

    def arrived(ref, sem):
        pltpu.make_async_copy(ref, ref, recv_sems.at[sem]).wait()

    def sent(ref, sem):
        pltpu.make_async_copy(ref, ref, send_sems.at[sem]).wait()

    small = [
        pltpu.make_async_copy(src, dst, local_sems.at[LOADS + k])
        for k, (src, dst) in enumerate(
            [(row_in, row_v), (band_in, band_v), (col_in, col_v), (time_in, time_v)]
        )
    ]
    for copy in small:
        copy.start()

    barrier = pltpu.get_barrier_semaphore()
    for to in gy_peers:
        pl.semaphore_signal(barrier, inc=1, device_id=(a, to), device_id_type=MESH)
    for to in gx_peers:
        pl.semaphore_signal(barrier, inc=1, device_id=(to, g), device_id_type=MESH)

    for k in range(LOADS):
        span = pl.ds(k * (TB // LOADS), TB // LOADS)
        pltpu.make_async_copy(tensor.at[span], data.at[span], local_sems.at[k]).start()

    tb_t[...] = jnp.zeros_like(tb_t)
    packed[...] = jnp.zeros_like(packed)
    for copy in small:
        copy.wait()
    packed[0:CW, 0:RANK] = col_v[...]
    packed[CW : CW + BW, 0:RANK] = band_v[...]
    packed[MSG : MSG + RW, 0:RANK] = row_v[...]
    packed[MSG + 8 : MSG + 8 + FRAMES, 0:RANK] = time_v[...]
    mine2[...] = packed[CW : CW + BW]
    mine4[...] = packed[MSG : MSG + RW]
    time8 = packed[MSG + 8 :]
    rowg[g] = mine4[...]
    bandg[a] = mine2[...]
    bandx[g] = mine2[...]
    for m, tile in enumerate(pack([packed[8 * m : 8 * m + 8] for m in range(4)])):
        colg[c, lz, 8 * m : 8 * m + 8] = tile

    pl.semaphore_wait(barrier, NY - 1 + NX - 1)

    for to in gy_peers:
        send(mine4, rowg.at[g], S_ROW, (a, to))
    for to in gx_peers:
        send(mine2, bandg.at[a], S_BAND, (to, g))

    @pl.loop(0, LOADS)
    def _(k):
        per = TB // LOADS
        span = pl.ds(k * per, per)
        pltpu.make_async_copy(tensor.at[span], data.at[span], local_sems.at[k]).wait()
        for i in range(per):
            at = pl.multiple_of((k * per + i) * ROWS, ROWS)
            turned[:, pl.ds(at, ROWS)] = data[k * per + i].T

    for to in core_peers:
        send(colg.at[c, lz], colg.at[c, lz], S_COL, (a, to))
    for to in gy_peers:
        send(mine2, bandx.at[g], S_BANDX, (a, to))

    arrived(bandg.at[pl.ds(0, NX - 1)], S_BAND)
    for k in range(NX):
        band_t[BW * k : BW * k + BW] = bandg[k]
    for t in range(FRAMES):
        tb_t[t * BANDS : (t + 1) * BANDS] = time8[t : t + 1] * band_t[...]
    tb_t[TB : TB + BANDS] = band_t[...]
    arrived(rowg.at[pl.ds(0, NY - 1)], S_ROW)
    for k in range(NY):
        row_t[RW * k : RW * k + RW] = rowg[k]

    @pl.loop(0, BANDS)
    def _(k):
        span = pl.ds(pl.multiple_of(k * ROWS, ROWS), ROWS)
        rows = row_t[...]
        plain = (tb_t[pl.ds(TB + k, 1)] * rows).astype(BF16)
        for t in range(FRAMES):
            prod[t, span, 0:LANES] = (tb_t[pl.ds(t * BANDS + k, 1)] * rows).astype(BF16)
            prod[t, span, LANES:] = plain

    def send_pieces(n):
        span = pl.ds(n * PER, PER)
        arrived(recv1.at[span], S_R1 + n)
        sum1[span] = part[c, span] + recv1[span]
        for i in range(PER):
            k = n * PER + i

            @pl.when(k != lz)
            def _():
                send(sum1.at[k], recv2.at[lz], S_R2, (a, k * 2 + c))

    @pl.loop(0, CHUNKS)
    def _(n):
        here = pl.ds(pl.multiple_of(n * CHUNK, CHUNK), CHUNK)
        acc = jnp.zeros((CHUNK, LANES), F32)
        for t in range(FRAMES):
            both = dot(turned[here, t * HALF : (t + 1) * HALF], prod[t])
            by_frame[t, here] = both[:, LANES:]
            acc = acc + both[:, 0:LANES]
        acc = acc.reshape(CHUNK // CW, 4, 8, LANES)
        tiles = pack([acc[:, m].reshape(CHUNK // 4, LANES) for m in range(4)])
        for k in range(CHUNK // CW):
            for m in range(3):
                part[k % 2, n * PER + k // 2, 8 * m : 8 * m + 8] = tiles[m][8 * k : 8 * k + 8]
        span = pl.ds(n * PER, PER)
        send(part.at[other, span], recv1.at[span], S_R1 + n, (a, partner))

        @pl.when(n > 0)
        def _():
            send_pieces(n - 1)

    gram = exact(row_t[...].T, row_t[...])
    for k in range(4):
        gpart[k, 0] = gram[24 * k : 24 * k + 24]
    send_pieces(CHUNKS - 1)
    arrived(colg.at[0, pl.ds(0, NLZ - 1)], S_COL)
    send(colg.at[c], colg.at[c], S_COLC, (a, partner))
    arrived(bandx.at[pl.ds(0, NY - 1)], S_BANDX)
    for k in range(NY):
        bandx_t[BW * k : BW * k + BW] = bandx[k]
    gram = exact(bandx_t[...].T, bandx_t[...])
    for k in range(4):
        gpart[k, 1] = gram[24 * k : 24 * k + 24]
    grecv[a] = gpart[p]
    for to in gx_peers:
        send(gpart.at[p], grecv.at[a], S_GRAM, (to, g))

    arrived(colg.at[0], S_COLC)
    for i in range(2):
        tiles = unpack(
            [colg[i, :, 8 * m : 8 * m + 8].reshape(8 * NLZ, LANES) for m in range(3)]
        )
        for k in range(NLZ):
            block = jnp.concatenate([tile[8 * k : 8 * k + 8] for tile in tiles], axis=0)
            at = (2 * k + i) * CW
            colf[at : at + CW] = block
            low[at : at + CW] = block.astype(BF16)

    for t in range(FRAMES):
        fpart[t : t + 1] = jnp.sum(
            by_frame[t] * low[...].astype(F32), axis=0, keepdims=True
        )
    fg[g] = fpart[...]
    for to in gy_peers:
        send(fpart, fg.at[g], S_F1, (a, to))

    @pl.loop(0, 4)
    def _(q):
        here = pl.ds(pl.multiple_of(q * QROWS, QROWS), QROWS)
        folded[...] = dot(data[:, here, :].reshape(TB * QROWS, COLS), low[...])
        rows = jnp.zeros((QROWS, LANES), F32)
        row_here = row_t[here]
        for j in range(TB):
            block = folded[j * QROWS : (j + 1) * QROWS]
            rows = rows + block * tb_t[j : j + 1]
            block = block * row_here
            partials[q, j] = jnp.sum(block.reshape(QROWS // 8, 8, LANES), axis=0)
        for i in range(NY // 4):
            rsend[q * (NY // 4) + i] = rows[RW * i : RW * i + RW]
        for i in range(NY // 4):
            k = q * (NY // 4) + i

            @pl.when(k != g)
            def _():
                send(rsend.at[k], rrecv.at[g], S_ROWS, (a, k))

    sums = total(partials, 4)
    bands = jnp.zeros((BANDS, LANES), F32)
    for t in range(FRAMES):
        bands = bands + time8[t : t + 1] * jnp.sum(sums[t * BANDS : (t + 1) * BANDS], axis=1)
    for k in range(NX):
        bsend[k] = bands[BW * k : BW * k + BW]
    for k in range(1, NX):
        to = wrap(a + k, NX)
        send(bsend.at[to], brecv.at[a], S_BANDS, (to, g))
    brecv[a] = bsend[a]
    rrecv[g] = rsend[g]

    arrived(grecv.at[pl.ds(0, NX - 1)], S_GRAM)
    gall[p] = total(grecv, NX)
    for k in range(1, 4):
        to = wrap(p + k, 4)
        to_l = lax.div(to, 2)
        send(gall.at[p], gall.at[p], S_GRAMP, (a, (to_l * 8 + z) * 2 + to - 2 * to_l))
    arrived(fg.at[pl.ds(0, NY - 1)], S_F1)
    fsum[...] = total(fg, NY)
    fx[a] = fsum[...]
    for to in gx_peers:
        send(fsum, fx.at[a], S_F2, (to, g))
    recv2[lz] = sum1[lz]
    arrived(recv2.at[pl.ds(0, NLZ - 1)], S_R2)
    fin[...] = total(recv2, NLZ)
    recv3[a] = fin[...]
    for to in gx_peers:
        send(fin, recv3.at[a], S_R3, (to, g))

    gcols[...] = jnp.zeros_like(gcols)

    @pl.loop(0, 4)
    def _(i):
        block = colf[pl.ds(pl.multiple_of(i * 256, 256), 256)]
        gcols[...] += exact(block.T, block)

    gram_cols = gcols[...]
    arrived(gall.at[pl.ds(0, 3)], S_GRAMP)
    pad = jnp.zeros((LANES - RANK, LANES), F32)
    gram_rows, gram_bands = (
        jnp.concatenate([gall[:, i].reshape(RANK, LANES), pad], axis=0) for i in range(2)
    )
    time_n = jnp.concatenate([time8, jnp.zeros((LANES - 8, LANES), F32)], axis=0).T
    gram_time = time_n[:, 0:1] * time8[0:1] + time_n[:, 1:2] * time8[1:2]
    row_model = exact(packed[MSG : MSG + 8], gram_cols * gram_bands * gram_time)
    col_model = exact(packed[0:CW], gram_rows * gram_bands * gram_time)
    band_model = exact(packed[CW:MSG], gram_rows * gram_cols * gram_time)
    time_model = exact(time8, gram_rows * gram_cols * gram_bands)

    arrived(fx.at[pl.ds(0, NX - 1)], S_F2)
    time_out[...] = (time_model[0:FRAMES] - total(fx, NX))[:, 0:RANK]
    arrived(recv3.at[pl.ds(0, NX - 1)], S_R3)
    sums = total(recv3, NX)
    sums = jnp.concatenate(unpack([sums[8 * m : 8 * m + 8] for m in range(3)]), axis=0)
    col_out[...] = (col_model - sums)[:, 0:RANK]
    arrived(rrecv.at[pl.ds(0, NY - 1)], S_ROWS)
    row_out[...] = (row_model[0:RW] - total(rrecv, NY))[:, 0:RANK]
    arrived(brecv.at[pl.ds(0, NX - 1)], S_BANDS)
    band_out[...] = (band_model[0:BW] - total(brecv, NX))[:, 0:RANK]

    sent(rowg.at[pl.ds(0, NY - 1)], S_ROW)
    sent(bandg.at[pl.ds(0, NX - 1)], S_BAND)
    sent(bandx.at[pl.ds(0, NY - 1)], S_BANDX)
    sent(colg.at[0, pl.ds(0, NLZ - 1)], S_COL)
    sent(colg.at[0], S_COLC)
    for n in range(CHUNKS):
        sent(recv1.at[pl.ds(n * PER, PER)], S_R1 + n)
    sent(recv2.at[pl.ds(0, NLZ - 1)], S_R2)
    sent(recv3.at[pl.ds(0, NX - 1)], S_R3)
    sent(fg.at[pl.ds(0, NY - 1)], S_F1)
    sent(fx.at[pl.ds(0, NX - 1)], S_F2)
    sent(grecv.at[pl.ds(0, NX - 1)], S_GRAM)
    sent(gall.at[pl.ds(0, 3)], S_GRAMP)
    sent(rrecv.at[pl.ds(0, NY - 1)], S_ROWS)
    sent(brecv.at[pl.ds(0, NX - 1)], S_BANDS)


def hand_over(*refs):
    sems = refs[8]
    copies = [
        pltpu.make_async_copy(refs[k], refs[4 + k], sems.at[k]) for k in range(4)
    ]
    for copy in copies:
        copy.start()
    for copy in copies:
        copy.wait()


def shards(tensor, row_factor, column_factor, band_factor, time_factor):
    v = pltpu.VMEM
    shapes = tuple(jax.ShapeDtypeStruct((n, RANK), F32) for n in (RW, CW, BW, FRAMES))
    factors = (row_factor, column_factor, band_factor, time_factor)
    factors = [pltpu.with_memory_space_constraint(x.T, pltpu.HBM) for x in factors]
    out = pl.pallas_call(
        kernel,
        out_shape=shapes,
        in_specs=[pl.BlockSpec(memory_space=pl.ANY)] + [pl.BlockSpec(memory_space=pltpu.HBM)] * 4,
        out_specs=[pl.BlockSpec(memory_space=v)] * 4,
        scratch_shapes=[
            v((MSG + 16, LANES), F32),
            v((RW, RANK), F32),
            v((CW, RANK), F32),
            v((BW, RANK), F32),
            v((FRAMES, RANK), F32),
            v((TB, ROWS, COLS), BF16),
            v((RW, LANES), F32),
            v((BW, LANES), F32),
            v((NY, RW, LANES), F32),
            v((NX, BW, LANES), F32),
            v((NY, BW, LANES), F32),
            v((ROWS, LANES), F32),
            v((BANDS, LANES), F32),
            v((NY * BW, LANES), F32),
            v((LANES, LANES), F32),
            v((COLS, TB * ROWS), BF16),
            v((FRAMES, HALF, 2 * LANES), BF16),
            v((FRAMES, COLS, LANES), F32),
            v((2, NLZ, PACK, LANES), F32),
            v((NLZ, PACK, LANES), F32),
            v((NLZ, PACK, LANES), F32),
            v((NLZ, PACK, LANES), F32),
            v((PACK, LANES), F32),
            v((NX, PACK, LANES), F32),
            v((2, NLZ, PACK, LANES), F32),
            v((COLS, LANES), F32),
            v((COLS, LANES), BF16),
            v((TB * QROWS, LANES), F32),
            v((4, TB, 8, LANES), F32),
            v((FRAMES, LANES), F32),
            v((NY, FRAMES, LANES), F32),
            v((FRAMES, LANES), F32),
            v((NX, FRAMES, LANES), F32),
            v((4, 2, 24, LANES), F32),
            v((NX, 2, 24, LANES), F32),
            v((4, 2, 24, LANES), F32),
            v((LANES, LANES), F32),
            v((NY, RW, LANES), F32),
            v((NY, RW, LANES), F32),
            v((NX, BW, LANES), F32),
            v((NX, BW, LANES), F32),
            pltpu.SemaphoreType.DMA((LOADS + 4,)),
            pltpu.SemaphoreType.DMA((N_SEMS,)),
            pltpu.SemaphoreType.DMA((N_SEMS,)),
        ],
        compiler_params=pltpu.CompilerParams(
            collective_id=0, has_side_effects=True, vmem_limit_bytes=48 * 1024 * 1024
        ),
        cost_estimate=pl.CostEstimate(
            flops=4 * RANK * TB * ROWS * COLS, bytes_accessed=2 * TB * ROWS * COLS, transcendentals=0
        ),
    )(
        tensor.reshape(TB, ROWS, COLS),
        *factors,
    )
    out = pl.pallas_call(
        hand_over,
        out_shape=shapes,
        in_specs=[pl.BlockSpec(memory_space=v)] * 4,
        out_specs=[pl.BlockSpec(memory_space=pl.ANY)] * 4,
        scratch_shapes=[pltpu.SemaphoreType.DMA((4,))],
    )(*[pltpu.with_memory_space_constraint(x, v) for x in out])
    return tuple(x.T for x in out)


def solution(mesh):
    return jax.shard_map(
        shards,
        mesh=mesh,
        in_specs=(
            P(None, "gy", "gx", None),
            P(None, ("gx", "gy")),
            P(None, "gy"),
            P(None, ("gy", "gx")),
            P(),
        ),
        out_specs=(P(None, ("gx", "gy")), P(None, "gy"), P(None, ("gy", "gx")), P()),
        check_vma=False,
    )
```

```python
import jax
import jax.numpy as jnp
from jax import lax
from jax.experimental import pallas as pl
from jax.experimental.pallas import tpu as pltpu
from jax.sharding import PartitionSpec as P

MESH = pl.DeviceIdType.MESH
HIGHEST = lax.Precision.HIGHEST
F32 = jnp.float32
BF16 = jnp.bfloat16

NX, NY, NLZ = 8, 32, 16
RANK, LANES = 96, 128
FRAMES, BANDS, ROWS, COLS = 2, 16, 128, 1024
RW, CW, BW = 4, 32, 2
PACK = CW * RANK // LANES
TB = FRAMES * BANDS
HALF = BANDS * ROWS
CHUNKS = 4
CHUNK = COLS // CHUNKS
PER = NLZ // CHUNKS
LOADS = 8
MSG = CW + 8
QROWS = ROWS // 4

(
    S_ROW, S_BAND, S_BANDX, S_COL, S_COLC, S_R1, S_R2, S_R3, S_F1, S_F2,
    S_GRAM, S_GRAMP, S_ROWS, S_BANDS,
) = [0, 1, 2, 3, 4, 5, 9, 10, 11, 12, 13, 14, 15, 16]
N_SEMS = 17


def dot(x, y):
    return jnp.dot(x, y, preferred_element_type=F32)


def exact(x, y):
    return jnp.dot(x, y, precision=HIGHEST, preferred_element_type=F32)


def total(ref, count):
    out = ref[0]
    for k in range(1, count):
        out = out + ref[k]
    return out


def wrap(index, size):
    return jnp.where(index >= size, index - size, index)


def lane_of(x):
    return lax.broadcasted_iota(jnp.int32, x.shape, 1)


def pack(tiles):
    spare = lane_of(tiles[3]) >= RANK
    return [
        jnp.where(spare, pltpu.roll(tiles[3], RANK - 32 * m, 1), tiles[m]) for m in range(3)
    ]


def unpack(tiles):
    lane = lane_of(tiles[0])
    last = jnp.zeros_like(tiles[0])
    for m in (2, 1, 0):
        last = jnp.where(lane < 32 * m + 32, pltpu.roll(tiles[m], 32 * m + 32, 1), last)
    zero = jnp.zeros_like(last)
    return [jnp.where(lane < RANK, tile, zero) for tile in tiles] + [
        jnp.where(lane < RANK, last, zero)
    ]


def kernel(
    tensor, row_in, col_in, band_in, time_in,
    row_out, col_out, band_out, time_out,
    packed, row_v, col_v, band_v, time_v,
    data, mine4, mine2, rowg, bandg, bandx, row_t, band_t, bandx_t, tb_t,
    turned, prod, by_frame, part, recv1, sum1, recv2, fin, recv3,
    colg, colf, low, folded, partials,
    fpart, fg, fsum, fx, gpart, grecv, gall, gcols,
    rsend, rrecv, bsend, brecv,
    local_sems, send_sems, recv_sems,
):
    a = lax.axis_index("gx")
    g = lax.axis_index("gy")
    lz = lax.div(g, 2)
    c = g - 2 * lz
    l = lax.div(lz, 8)
    z = lz - 8 * l
    p = l * 2 + c
    other = 1 - c
    partner = lz * 2 + other
    gy_peers = [wrap(g + k, NY) for k in range(1, NY)]
    gx_peers = [wrap(a + k, NX) for k in range(1, NX)]
    core_peers = [wrap(lz + k, NLZ) * 2 + c for k in range(1, NLZ)]

    def send(src, dst, sem, device):
        pltpu.make_async_remote_copy(
            src_ref=src, dst_ref=dst, send_sem=send_sems.at[sem], recv_sem=recv_sems.at[sem],
            device_id=device, device_id_type=MESH,
        ).start()

    def arrived(ref, sem):
        pltpu.make_async_copy(ref, ref, recv_sems.at[sem]).wait()

    def sent(ref, sem):
        pltpu.make_async_copy(ref, ref, send_sems.at[sem]).wait()

    small = [
        pltpu.make_async_copy(src, dst, local_sems.at[LOADS + k])
        for k, (src, dst) in enumerate(
            [(row_in, row_v), (band_in, band_v), (col_in, col_v), (time_in, time_v)]
        )
    ]
    for copy in small:
        copy.start()

    barrier = pltpu.get_barrier_semaphore()
    for to in gy_peers:
        pl.semaphore_signal(barrier, inc=1, device_id=(a, to), device_id_type=MESH)
    for to in gx_peers:
        pl.semaphore_signal(barrier, inc=1, device_id=(to, g), device_id_type=MESH)

    for k in range(LOADS):
        span = pl.ds(k * (TB // LOADS), TB // LOADS)
        pltpu.make_async_copy(tensor.at[span], data.at[span], local_sems.at[k]).start()

    tb_t[...] = jnp.zeros_like(tb_t)
    packed[...] = jnp.zeros_like(packed)
    for copy in small:
        copy.wait()
    packed[0:CW, 0:RANK] = col_v[...]
    packed[CW : CW + BW, 0:RANK] = band_v[...]
    packed[MSG : MSG + RW, 0:RANK] = row_v[...]
    packed[MSG + 8 : MSG + 8 + FRAMES, 0:RANK] = time_v[...]
    mine2[...] = packed[CW : CW + BW]
    mine4[...] = packed[MSG : MSG + RW]
    time8 = packed[MSG + 8 :]
    rowg[g] = mine4[...]
    bandg[a] = mine2[...]
    bandx[g] = mine2[...]
    for m, tile in enumerate(pack([packed[8 * m : 8 * m + 8] for m in range(4)])):
        colg[c, lz, 8 * m : 8 * m + 8] = tile

    pl.semaphore_wait(barrier, NY - 1 + NX - 1)

    for to in gy_peers:
        send(mine4, rowg.at[g], S_ROW, (a, to))
    for to in gx_peers:
        send(mine2, bandg.at[a], S_BAND, (to, g))
    for to in core_peers:
        send(colg.at[c, lz], colg.at[c, lz], S_COL, (a, to))

    @pl.loop(0, LOADS)
    def _(k):
        per = TB // LOADS
        span = pl.ds(k * per, per)
        pltpu.make_async_copy(tensor.at[span], data.at[span], local_sems.at[k]).wait()
        for i in range(per):
            at = pl.multiple_of((k * per + i) * ROWS, ROWS)
            turned[:, pl.ds(at, ROWS)] = data[k * per + i].T

    for to in gy_peers:
        send(mine2, bandx.at[g], S_BANDX, (a, to))

    arrived(bandg.at[pl.ds(0, NX - 1)], S_BAND)
    for k in range(NX):
        band_t[BW * k : BW * k + BW] = bandg[k]
    for t in range(FRAMES):
        tb_t[t * BANDS : (t + 1) * BANDS] = time8[t : t + 1] * band_t[...]
    tb_t[TB : TB + BANDS] = band_t[...]
    arrived(rowg.at[pl.ds(0, NY - 1)], S_ROW)
    for k in range(NY):
        row_t[RW * k : RW * k + RW] = rowg[k]

    @pl.loop(0, BANDS)
    def _(k):
        span = pl.ds(pl.multiple_of(k * ROWS, ROWS), ROWS)
        rows = row_t[...]
        plain = (tb_t[pl.ds(TB + k, 1)] * rows).astype(BF16)
        for t in range(FRAMES):
            prod[t, span, 0:LANES] = (tb_t[pl.ds(t * BANDS + k, 1)] * rows).astype(BF16)
            prod[t, span, LANES:] = plain

    def slot_lz(n, i):
        return (i // 2) * (NLZ // 2) + 2 * n + i % 2

    def send_pieces(n):
        span = pl.ds(n * PER, PER)
        arrived(recv1.at[span], S_R1 + n)
        sum1[span] = part[c, span] + recv1[span]
        for i in range(PER):
            k = slot_lz(n, i)

            @pl.when(k != lz)
            def _():
                send(sum1.at[n * PER + i], recv2.at[lz], S_R2, (a, k * 2 + c))

            @pl.when(k == lz)
            def _():
                recv2[lz] = sum1[n * PER + i]

    @pl.loop(0, CHUNKS)
    def _(n):
        heres = [
            pl.ds(pl.multiple_of(i * (COLS // 2) + n * (CHUNK // 2), CHUNK // 2), CHUNK // 2)
            for i in range(2)
        ]
        acc = jnp.zeros((CHUNK, LANES), F32)
        for t in range(FRAMES):
            both = dot(
                jnp.concatenate(
                    [turned[here, t * HALF : (t + 1) * HALF] for here in heres], axis=0
                ),
                prod[t],
            )
            for i, here in enumerate(heres):
                by_frame[t, here] = both[i * (CHUNK // 2) : (i + 1) * (CHUNK // 2), LANES:]
            acc = acc + both[:, 0:LANES]
        acc = acc.reshape(CHUNK // CW, 4, 8, LANES)
        tiles = pack([acc[:, m].reshape(CHUNK // 4, LANES) for m in range(4)])
        for k in range(CHUNK // CW):
            for m in range(3):
                part[k % 2, n * PER + k // 2, 8 * m : 8 * m + 8] = tiles[m][8 * k : 8 * k + 8]
        span = pl.ds(n * PER, PER)
        send(part.at[other, span], recv1.at[span], S_R1 + n, (a, partner))

    gram = exact(row_t[...].T, row_t[...])
    for k in range(4):
        gpart[k, 0] = gram[24 * k : 24 * k + 24]

    @pl.loop(0, CHUNKS)
    def _(n):
        send_pieces(n)

    arrived(colg.at[0, pl.ds(0, NLZ - 1)], S_COL)
    send(colg.at[c], colg.at[c], S_COLC, (a, partner))
    arrived(bandx.at[pl.ds(0, NY - 1)], S_BANDX)
    for k in range(NY):
        bandx_t[BW * k : BW * k + BW] = bandx[k]
    gram = exact(bandx_t[...].T, bandx_t[...])
    for k in range(4):
        gpart[k, 1] = gram[24 * k : 24 * k + 24]
    grecv[a] = gpart[p]
    for to in gx_peers:
        send(gpart.at[p], grecv.at[a], S_GRAM, (to, g))

    arrived(colg.at[0], S_COLC)
    for i in range(2):
        tiles = unpack(
            [colg[i, :, 8 * m : 8 * m + 8].reshape(8 * NLZ, LANES) for m in range(3)]
        )
        for k in range(NLZ):
            block = jnp.concatenate([tile[8 * k : 8 * k + 8] for tile in tiles], axis=0)
            at = (2 * k + i) * CW
            colf[at : at + CW] = block
            low[at : at + CW] = block.astype(BF16)

    for t in range(FRAMES):
        fpart[t : t + 1] = jnp.sum(
            by_frame[t] * low[...].astype(F32), axis=0, keepdims=True
        )
    fg[g] = fpart[...]
    for to in gy_peers:
        send(fpart, fg.at[g], S_F1, (a, to))

    @pl.loop(0, 4)
    def _(q):
        half = QROWS // 2
        heres = [pl.ds(pl.multiple_of(i * (ROWS // 2) + q * half, half), half) for i in range(2)]
        block = jnp.concatenate([data[:, here, :] for here in heres], axis=1)
        folded[...] = dot(block.reshape(TB * QROWS, COLS), low[...])
        rows = jnp.zeros((QROWS, LANES), F32)
        row_here = jnp.concatenate([row_t[here] for here in heres], axis=0)
        for j in range(TB):
            block = folded[j * QROWS : (j + 1) * QROWS]
            rows = rows + block * tb_t[j : j + 1]
            block = block * row_here
            partials[q, j] = jnp.sum(block.reshape(QROWS // 8, 8, LANES), axis=0)
        owners = [(i // 4) * (NY // 2) + 4 * q + i % 4 for i in range(NY // 4)]
        for i, k in enumerate(owners):
            rsend[k] = rows[RW * i : RW * i + RW]
        for k in owners:

            @pl.when(k != g)
            def _():
                send(rsend.at[k], rrecv.at[g], S_ROWS, (a, k))

    sums = total(partials, 4)
    bands = jnp.zeros((BANDS, LANES), F32)
    for t in range(FRAMES):
        bands = bands + time8[t : t + 1] * jnp.sum(sums[t * BANDS : (t + 1) * BANDS], axis=1)
    for k in range(NX):
        bsend[k] = bands[BW * k : BW * k + BW]
    for k in range(1, NX):
        to = wrap(a + k, NX)
        send(bsend.at[to], brecv.at[a], S_BANDS, (to, g))
    brecv[a] = bsend[a]
    rrecv[g] = rsend[g]

    arrived(grecv.at[pl.ds(0, NX - 1)], S_GRAM)
    gall[p] = total(grecv, NX)
    for k in range(1, 4):
        to = wrap(p + k, 4)
        to_l = lax.div(to, 2)
        send(gall.at[p], gall.at[p], S_GRAMP, (a, (to_l * 8 + z) * 2 + to - 2 * to_l))
    arrived(recv2.at[pl.ds(0, NLZ - 1)], S_R2)
    fin[...] = total(recv2, NLZ)
    recv3[a] = fin[...]
    for to in gx_peers:
        send(fin, recv3.at[a], S_R3, (to, g))
    arrived(fg.at[pl.ds(0, NY - 1)], S_F1)
    fsum[...] = total(fg, NY)
    fx[a] = fsum[...]
    for to in gx_peers:
        send(fsum, fx.at[a], S_F2, (to, g))

    gcols[...] = jnp.zeros_like(gcols)

    @pl.loop(0, 4)
    def _(i):
        block = colf[pl.ds(pl.multiple_of(i * 256, 256), 256)]
        gcols[...] += exact(block.T, block)

    gram_cols = gcols[...]
    arrived(gall.at[pl.ds(0, 3)], S_GRAMP)
    pad = jnp.zeros((LANES - RANK, LANES), F32)
    gram_rows, gram_bands = (
        jnp.concatenate([gall[:, i].reshape(RANK, LANES), pad], axis=0) for i in range(2)
    )
    time_n = jnp.concatenate([time8, jnp.zeros((LANES - 8, LANES), F32)], axis=0).T
    gram_time = time_n[:, 0:1] * time8[0:1] + time_n[:, 1:2] * time8[1:2]
    row_model = exact(packed[MSG : MSG + 8], gram_cols * gram_bands * gram_time)
    col_model = exact(packed[0:CW], gram_rows * gram_bands * gram_time)
    band_model = exact(packed[CW:MSG], gram_rows * gram_cols * gram_time)
    time_model = exact(time8, gram_rows * gram_cols * gram_bands)

    arrived(fx.at[pl.ds(0, NX - 1)], S_F2)
    time_out[...] = (time_model[0:FRAMES] - total(fx, NX))[:, 0:RANK]
    arrived(recv3.at[pl.ds(0, NX - 1)], S_R3)
    sums = total(recv3, NX)
    sums = jnp.concatenate(unpack([sums[8 * m : 8 * m + 8] for m in range(3)]), axis=0)
    col_out[...] = (col_model - sums)[:, 0:RANK]
    arrived(rrecv.at[pl.ds(0, NY - 1)], S_ROWS)
    row_out[...] = (row_model[0:RW] - total(rrecv, NY))[:, 0:RANK]
    arrived(brecv.at[pl.ds(0, NX - 1)], S_BANDS)
    band_out[...] = (band_model[0:BW] - total(brecv, NX))[:, 0:RANK]

    sent(rowg.at[pl.ds(0, NY - 1)], S_ROW)
    sent(bandg.at[pl.ds(0, NX - 1)], S_BAND)
    sent(bandx.at[pl.ds(0, NY - 1)], S_BANDX)
    sent(colg.at[0, pl.ds(0, NLZ - 1)], S_COL)
    sent(colg.at[0], S_COLC)
    for n in range(CHUNKS):
        sent(recv1.at[pl.ds(n * PER, PER)], S_R1 + n)
    sent(recv2.at[pl.ds(0, NLZ - 1)], S_R2)
    sent(recv3.at[pl.ds(0, NX - 1)], S_R3)
    sent(fg.at[pl.ds(0, NY - 1)], S_F1)
    sent(fx.at[pl.ds(0, NX - 1)], S_F2)
    sent(grecv.at[pl.ds(0, NX - 1)], S_GRAM)
    sent(gall.at[pl.ds(0, 3)], S_GRAMP)
    sent(rrecv.at[pl.ds(0, NY - 1)], S_ROWS)
    sent(brecv.at[pl.ds(0, NX - 1)], S_BANDS)


def hand_over(*refs):
    sems = refs[8]
    copies = [
        pltpu.make_async_copy(refs[k], refs[4 + k], sems.at[k]) for k in range(4)
    ]
    for copy in copies:
        copy.start()
    for copy in copies:
        copy.wait()


def shards(tensor, row_factor, column_factor, band_factor, time_factor):
    v = pltpu.VMEM
    shapes = tuple(jax.ShapeDtypeStruct((n, RANK), F32) for n in (RW, CW, BW, FRAMES))
    factors = (row_factor, column_factor, band_factor, time_factor)
    factors = [pltpu.with_memory_space_constraint(x.T, pltpu.HBM) for x in factors]
    out = pl.pallas_call(
        kernel,
        out_shape=shapes,
        in_specs=[pl.BlockSpec(memory_space=pl.ANY)] + [pl.BlockSpec(memory_space=pltpu.HBM)] * 4,
        out_specs=[pl.BlockSpec(memory_space=v)] * 4,
        scratch_shapes=[
            v((MSG + 16, LANES), F32),
            v((RW, RANK), F32),
            v((CW, RANK), F32),
            v((BW, RANK), F32),
            v((FRAMES, RANK), F32),
            v((TB, ROWS, COLS), BF16),
            v((RW, LANES), F32),
            v((BW, LANES), F32),
            v((NY, RW, LANES), F32),
            v((NX, BW, LANES), F32),
            v((NY, BW, LANES), F32),
            v((ROWS, LANES), F32),
            v((BANDS, LANES), F32),
            v((NY * BW, LANES), F32),
            v((LANES, LANES), F32),
            v((COLS, TB * ROWS), BF16),
            v((FRAMES, HALF, 2 * LANES), BF16),
            v((FRAMES, COLS, LANES), F32),
            v((2, NLZ, PACK, LANES), F32),
            v((NLZ, PACK, LANES), F32),
            v((NLZ, PACK, LANES), F32),
            v((NLZ, PACK, LANES), F32),
            v((PACK, LANES), F32),
            v((NX, PACK, LANES), F32),
            v((2, NLZ, PACK, LANES), F32),
            v((COLS, LANES), F32),
            v((COLS, LANES), BF16),
            v((TB * QROWS, LANES), F32),
            v((4, TB, 8, LANES), F32),
            v((FRAMES, LANES), F32),
            v((NY, FRAMES, LANES), F32),
            v((FRAMES, LANES), F32),
            v((NX, FRAMES, LANES), F32),
            v((4, 2, 24, LANES), F32),
            v((NX, 2, 24, LANES), F32),
            v((4, 2, 24, LANES), F32),
            v((LANES, LANES), F32),
            v((NY, RW, LANES), F32),
            v((NY, RW, LANES), F32),
            v((NX, BW, LANES), F32),
            v((NX, BW, LANES), F32),
            pltpu.SemaphoreType.DMA((LOADS + 4,)),
            pltpu.SemaphoreType.DMA((N_SEMS,)),
            pltpu.SemaphoreType.DMA((N_SEMS,)),
        ],
        compiler_params=pltpu.CompilerParams(
            collective_id=0, has_side_effects=True, vmem_limit_bytes=48 * 1024 * 1024
        ),
        cost_estimate=pl.CostEstimate(
            flops=4 * RANK * TB * ROWS * COLS, bytes_accessed=2 * TB * ROWS * COLS, transcendentals=0
        ),
    )(
        tensor.reshape(TB, ROWS, COLS),
        *factors,
    )
    out = pl.pallas_call(
        hand_over,
        out_shape=shapes,
        in_specs=[pl.BlockSpec(memory_space=v)] * 4,
        out_specs=[pl.BlockSpec(memory_space=pl.ANY)] * 4,
        scratch_shapes=[pltpu.SemaphoreType.DMA((4,))],
    )(*[pltpu.with_memory_space_constraint(x, v) for x in out])
    return tuple(x.T for x in out)


def solution(mesh):
    return jax.shard_map(
        shards,
        mesh=mesh,
        in_specs=(
            P(None, "gy", "gx", None),
            P(None, ("gx", "gy")),
            P(None, "gy"),
            P(None, ("gy", "gx")),
            P(),
        ),
        out_specs=(P(None, ("gx", "gy")), P(None, "gy"), P(None, ("gy", "gx")), P()),
        check_vma=False,
    )
```

```python
import jax
import jax.numpy as jnp
from jax import lax
from jax.experimental import pallas as pl
from jax.experimental.pallas import tpu as pltpu
from jax.sharding import PartitionSpec as P

MESH = pl.DeviceIdType.MESH
HIGHEST = lax.Precision.HIGHEST
F32 = jnp.float32
BF16 = jnp.bfloat16

NX, NY, NLZ = 8, 32, 16
RANK, LANES = 96, 128
FRAMES, BANDS, ROWS, COLS = 2, 16, 128, 1024
RW, CW, BW = 4, 32, 2
PACK = CW * RANK // LANES
TB = FRAMES * BANDS
HALF = BANDS * ROWS
CHUNKS = 4
CHUNK = COLS // CHUNKS
PER = NLZ // CHUNKS
LOADS = 8
MSG = CW + 8
QROWS = ROWS // 4

(
    S_ROW, S_ROWC, S_BAND, S_COL, S_COLC, S_R1, S_R2, S_R3, S_F2,
    S_GRAM, S_GRAMP, S_T1, S_ROWS,
) = [0, 1, 2, 3, 4, 5, 9, 10, 11, 12, 13, 14, 18]
N_SEMS = 19


def dot(x, y):
    return jnp.dot(x, y, preferred_element_type=F32)


def exact(x, y):
    return jnp.dot(x, y, precision=HIGHEST, preferred_element_type=F32)


def total(ref, count):
    out = ref[0]
    for k in range(1, count):
        out = out + ref[k]
    return out


def wrap(index, size):
    return jnp.where(index >= size, index - size, index)


def lane_of(x):
    return lax.broadcasted_iota(jnp.int32, x.shape, 1)


def pack(tiles):
    spare = lane_of(tiles[3]) >= RANK
    return [
        jnp.where(spare, pltpu.roll(tiles[3], RANK - 32 * m, 1), tiles[m]) for m in range(3)
    ]


def unpack(tiles):
    lane = lane_of(tiles[0])
    last = jnp.zeros_like(tiles[0])
    for m in (2, 1, 0):
        last = jnp.where(lane < 32 * m + 32, pltpu.roll(tiles[m], 32 * m + 32, 1), last)
    zero = jnp.zeros_like(last)
    return [jnp.where(lane < RANK, tile, zero) for tile in tiles] + [
        jnp.where(lane < RANK, last, zero)
    ]


def kernel(
    tensor, row_in, col_in, band_in, time_in,
    row_out, col_out, band_out, time_out,
    packed, row_v, col_v, band_v, time_v,
    data, mine2, rowg, bandg, row_t, band_t, bandx_t, tb_t,
    turned, prod, by_frame, part, recv1, sum1, recv2, xsend, recv3,
    colg, colf, low, folded, partials,
    fpart, fsum, fx, gpart, grecv, gall, gcols,
    rsend, rcore, rsum, rrecv,
    local_sems, send_sems, recv_sems,
):
    a = lax.axis_index("gx")
    g = lax.axis_index("gy")
    lz = lax.div(g, 2)
    c = g - 2 * lz
    l = lax.div(lz, 8)
    z = lz - 8 * l
    p = l * 2 + c
    other = 1 - c
    partner = lz * 2 + other
    gx_peers = [wrap(a + k, NX) for k in range(1, NX)]
    core_peers = [wrap(lz + k, NLZ) * 2 + c for k in range(1, NLZ)]

    def send(src, dst, sem, device):
        pltpu.make_async_remote_copy(
            src_ref=src, dst_ref=dst, send_sem=send_sems.at[sem], recv_sem=recv_sems.at[sem],
            device_id=device, device_id_type=MESH,
        ).start()

    def arrived(ref, sem):
        pltpu.make_async_copy(ref, ref, recv_sems.at[sem]).wait()

    def sent(ref, sem):
        pltpu.make_async_copy(ref, ref, send_sems.at[sem]).wait()

    small = [
        pltpu.make_async_copy(src, dst, local_sems.at[LOADS + k])
        for k, (src, dst) in enumerate(
            [(row_in, row_v), (band_in, band_v), (col_in, col_v), (time_in, time_v)]
        )
    ]
    for copy in small:
        copy.start()

    barrier = pltpu.get_barrier_semaphore()
    for to in core_peers + [partner, (lz + 8 - 16 * l) * 2 + other]:
        pl.semaphore_signal(barrier, inc=1, device_id=(a, to), device_id_type=MESH)
    for to in gx_peers:
        pl.semaphore_signal(barrier, inc=1, device_id=(to, g), device_id_type=MESH)

    for k in range(LOADS):
        span = pl.ds(k * (TB // LOADS), TB // LOADS)
        pltpu.make_async_copy(tensor.at[span], data.at[span], local_sems.at[k]).start()

    tb_t[...] = jnp.zeros_like(tb_t)
    packed[...] = jnp.zeros_like(packed)
    for copy in small:
        copy.wait()
    packed[0:CW, 0:RANK] = col_v[...]
    packed[CW : CW + BW, 0:RANK] = band_v[...]
    packed[MSG : MSG + RW, 0:RANK] = row_v[...]
    packed[MSG + RW : MSG + RW + BW, 0:RANK] = band_v[...]
    packed[MSG + 8 : MSG + 8 + FRAMES, 0:RANK] = time_v[...]
    mine2[...] = packed[CW : CW + BW]
    time8 = packed[MSG + 8 :]
    rowg[c, lz] = packed[MSG : MSG + 8]
    bandg[a] = mine2[...]
    for m, tile in enumerate(pack([packed[8 * m : 8 * m + 8] for m in range(4)])):
        colg[c, lz, 8 * m : 8 * m + 8] = tile

    pl.semaphore_wait(barrier, NLZ + 1 + NX - 1)

    for to in core_peers:
        send(rowg.at[c, lz], rowg.at[c, lz], S_ROW, (a, to))
    for to in gx_peers:
        send(mine2, bandg.at[a], S_BAND, (to, g))
    for to in core_peers:
        send(colg.at[c, lz], colg.at[c, lz], S_COL, (a, to))

    @pl.loop(0, LOADS)
    def _(k):
        per = TB // LOADS
        span = pl.ds(k * per, per)
        pltpu.make_async_copy(tensor.at[span], data.at[span], local_sems.at[k]).wait()
        for i in range(per):
            at = pl.multiple_of((k * per + i) * ROWS, ROWS)
            turned[:, pl.ds(at, ROWS)] = data[k * per + i].T

    arrived(rowg.at[0, pl.ds(0, NLZ - 1)], S_ROW)
    send(rowg.at[c], rowg.at[c], S_ROWC, (a, partner))
    arrived(bandg.at[pl.ds(0, NX - 1)], S_BAND)
    for k in range(NX):
        band_t[BW * k : BW * k + BW] = bandg[k]
    for t in range(FRAMES):
        tb_t[t * BANDS : (t + 1) * BANDS] = time8[t : t + 1] * band_t[...]
    tb_t[TB : TB + BANDS] = band_t[...]
    arrived(rowg.at[0], S_ROWC)
    for k in range(NY):
        row_t[RW * k : RW * k + RW] = rowg[k % 2, k // 2, 0:RW]
        bandx_t[RW * k : RW * k + RW] = rowg[k % 2, k // 2, RW : 2 * RW]

    @pl.loop(0, BANDS)
    def _(k):
        span = pl.ds(pl.multiple_of(k * ROWS, ROWS), ROWS)
        rows = row_t[...]
        plain = (tb_t[pl.ds(TB + k, 1)] * rows).astype(BF16)
        for t in range(FRAMES):
            prod[t, span, 0:LANES] = (tb_t[pl.ds(t * BANDS + k, 1)] * rows).astype(BF16)
            prod[t, span, LANES:] = plain

    def slot_lz(n, i):
        return (i // 2) * (NLZ // 2) + 2 * n + i % 2

    def send_pieces(n):
        span = pl.ds(n * PER, PER)
        arrived(recv1.at[span], S_R1 + n)
        sum1[span] = part[c, span] + recv1[span]
        for i in range(PER):
            k = slot_lz(n, i)

            @pl.when(k != lz)
            def _():
                send(sum1.at[n * PER + i], recv2.at[lz], S_R2, (a, k * 2 + c))

            @pl.when(k == lz)
            def _():
                recv2[lz] = sum1[n * PER + i]

    @pl.loop(0, CHUNKS)
    def _(n):
        heres = [
            pl.ds(pl.multiple_of(i * (COLS // 2) + n * (CHUNK // 2), CHUNK // 2), CHUNK // 2)
            for i in range(2)
        ]
        acc = jnp.zeros((CHUNK, LANES), F32)
        for t in range(FRAMES):
            both = dot(
                jnp.concatenate(
                    [turned[here, t * HALF : (t + 1) * HALF] for here in heres], axis=0
                ),
                prod[t],
            )
            for i, here in enumerate(heres):
                by_frame[t, here] = both[i * (CHUNK // 2) : (i + 1) * (CHUNK // 2), LANES:]
            acc = acc + both[:, 0:LANES]
        acc = acc.reshape(CHUNK // CW, 4, 8, LANES)
        tiles = pack([acc[:, m].reshape(CHUNK // 4, LANES) for m in range(4)])
        for k in range(CHUNK // CW):
            for m in range(3):
                part[k % 2, n * PER + k // 2, 8 * m : 8 * m + 8] = tiles[m][8 * k : 8 * k + 8]
        span = pl.ds(n * PER, PER)
        send(part.at[other, span], recv1.at[span], S_R1 + n, (a, partner))

    for i, ref in enumerate((row_t, bandx_t)):
        gram = exact(ref[...].T, ref[...])
        for k in range(4):
            gpart[k, i] = gram[24 * k : 24 * k + 24]
    grecv[a] = gpart[p]
    for to in gx_peers:
        send(gpart.at[p], grecv.at[a], S_GRAM, (to, g))
    arrived(colg.at[0, pl.ds(0, NLZ - 1)], S_COL)
    send(colg.at[c], colg.at[c], S_COLC, (a, partner))

    @pl.loop(0, CHUNKS)
    def _(n):
        send_pieces(n)

    arrived(colg.at[0], S_COLC)
    for i in range(2):
        tiles = unpack(
            [colg[i, :, 8 * m : 8 * m + 8].reshape(8 * NLZ, LANES) for m in range(3)]
        )
        for k in range(NLZ):
            block = jnp.concatenate([tile[8 * k : 8 * k + 8] for tile in tiles], axis=0)
            at = (2 * k + i) * CW
            colf[at : at + CW] = block
            low[at : at + CW] = block.astype(BF16)

    fpart[...] = jnp.zeros_like(fpart)
    for t in range(FRAMES):
        fpart[t : t + 1] = jnp.sum(
            by_frame[t] * low[...].astype(F32), axis=0, keepdims=True
        )

    def send_rows(q):
        span = pl.ds(q * PER, PER)
        arrived(rcore.at[span], S_T1 + q)
        rsum[span] = rsend[c, span] + rcore[span]
        for i in range(PER):
            k = slot_lz(q, i)

            @pl.when(k != lz)
            def _():
                send(rsum.at[q * PER + i], rrecv.at[lz], S_ROWS, (a, k * 2 + c))

            @pl.when(k == lz)
            def _():
                rrecv[lz] = rsum[q * PER + i]

    @pl.loop(0, 4)
    def _(q):
        half = QROWS // 2
        heres = [pl.ds(pl.multiple_of(i * (ROWS // 2) + q * half, half), half) for i in range(2)]
        block = jnp.concatenate([data[:, here, :] for here in heres], axis=1)
        folded[...] = dot(block.reshape(TB * QROWS, COLS), low[...])
        rows = jnp.zeros((QROWS, LANES), F32)
        row_here = jnp.concatenate([row_t[here] for here in heres], axis=0)
        for j in range(TB):
            block = folded[j * QROWS : (j + 1) * QROWS]
            rows = rows + block * tb_t[j : j + 1]
            block = block * row_here
            partials[q, j] = jnp.sum(block.reshape(QROWS // 8, 8, LANES), axis=0)
        frames = fpart[...]
        for i in range(NY // 4):
            rsend[i % 2, q * PER + i // 2, 0:RW] = rows[RW * i : RW * i + RW]
            rsend[i % 2, q * PER + i // 2, RW : 2 * RW] = frames
        span = pl.ds(q * PER, PER)
        send(rsend.at[other, span], rcore.at[span], S_T1 + q, (a, partner))

    @pl.loop(0, 4)
    def _(q):
        send_rows(q)

    sums = total(partials, 4)
    bands = jnp.zeros((BANDS, LANES), F32)
    for t in range(FRAMES):
        bands = bands + time8[t : t + 1] * jnp.sum(sums[t * BANDS : (t + 1) * BANDS], axis=1)

    arrived(recv2.at[pl.ds(0, NLZ - 1)], S_R2)
    fin = total(recv2, NLZ)
    for k in range(NX):
        xsend[k, 0:PACK] = fin
        xsend[k, PACK : PACK + BW] = bands[BW * k : BW * k + BW]
    recv3[a] = xsend[a]
    for to in gx_peers:
        send(xsend.at[to], recv3.at[a], S_R3, (to, g))
    arrived(grecv.at[pl.ds(0, NX - 1)], S_GRAM)
    gall[p] = total(grecv, NX)
    for k in range(1, 4):
        to = wrap(p + k, 4)
        to_l = lax.div(to, 2)
        send(gall.at[p], gall.at[p], S_GRAMP, (a, (to_l * 8 + z) * 2 + to - 2 * to_l))
    arrived(rrecv.at[pl.ds(0, NLZ - 1)], S_ROWS)
    row_sums = total(rrecv, NLZ)
    fsum[...] = row_sums[RW : RW + FRAMES]
    fx[a] = fsum[...]
    for to in gx_peers:
        send(fsum, fx.at[a], S_F2, (to, g))

    gcols[...] = jnp.zeros_like(gcols)

    @pl.loop(0, 4)
    def _(i):
        block = colf[pl.ds(pl.multiple_of(i * 256, 256), 256)]
        gcols[...] += exact(block.T, block)

    gram_cols = gcols[...]
    arrived(gall.at[pl.ds(0, 3)], S_GRAMP)
    pad = jnp.zeros((LANES - RANK, LANES), F32)
    gram_rows, gram_bands = (
        jnp.concatenate([gall[:, i].reshape(RANK, LANES), pad], axis=0) for i in range(2)
    )
    time_n = jnp.concatenate([time8, jnp.zeros((LANES - 8, LANES), F32)], axis=0).T
    gram_time = time_n[:, 0:1] * time8[0:1] + time_n[:, 1:2] * time8[1:2]
    row_model = exact(packed[MSG : MSG + 8], gram_cols * gram_bands * gram_time)
    col_model = exact(packed[0:CW], gram_rows * gram_bands * gram_time)
    band_model = exact(packed[CW:MSG], gram_rows * gram_cols * gram_time)
    time_model = exact(time8, gram_rows * gram_cols * gram_bands)

    row_out[...] = (row_model[0:RW] - row_sums[0:RW])[:, 0:RANK]
    arrived(recv3.at[pl.ds(0, NX - 1)], S_R3)
    sums = total(recv3, NX)
    band_out[...] = (band_model[0:BW] - sums[PACK : PACK + BW])[:, 0:RANK]
    sums = jnp.concatenate(unpack([sums[8 * m : 8 * m + 8] for m in range(3)]), axis=0)
    col_out[...] = (col_model - sums)[:, 0:RANK]
    arrived(fx.at[pl.ds(0, NX - 1)], S_F2)
    time_out[...] = (time_model[0:FRAMES] - total(fx, NX))[:, 0:RANK]

    sent(rowg.at[0, pl.ds(0, NLZ - 1)], S_ROW)
    sent(rowg.at[0], S_ROWC)
    sent(bandg.at[pl.ds(0, NX - 1)], S_BAND)
    sent(colg.at[0, pl.ds(0, NLZ - 1)], S_COL)
    sent(colg.at[0], S_COLC)
    for n in range(CHUNKS):
        sent(recv1.at[pl.ds(n * PER, PER)], S_R1 + n)
    sent(recv2.at[pl.ds(0, NLZ - 1)], S_R2)
    sent(recv3.at[pl.ds(0, NX - 1)], S_R3)
    sent(fx.at[pl.ds(0, NX - 1)], S_F2)
    sent(grecv.at[pl.ds(0, NX - 1)], S_GRAM)
    sent(gall.at[pl.ds(0, 3)], S_GRAMP)
    for q in range(4):
        sent(rcore.at[pl.ds(q * PER, PER)], S_T1 + q)
    sent(rrecv.at[pl.ds(0, NLZ - 1)], S_ROWS)


def hand_over(*refs):
    sems = refs[8]
    copies = [
        pltpu.make_async_copy(refs[k], refs[4 + k], sems.at[k]) for k in range(4)
    ]
    for copy in copies:
        copy.start()
    for copy in copies:
        copy.wait()


def shards(tensor, row_factor, column_factor, band_factor, time_factor):
    v = pltpu.VMEM
    shapes = tuple(jax.ShapeDtypeStruct((n, RANK), F32) for n in (RW, CW, BW, FRAMES))
    factors = (row_factor, column_factor, band_factor, time_factor)
    factors = [pltpu.with_memory_space_constraint(x.T, pltpu.HBM) for x in factors]
    out = pl.pallas_call(
        kernel,
        out_shape=shapes,
        in_specs=[pl.BlockSpec(memory_space=pl.ANY)] + [pl.BlockSpec(memory_space=pltpu.HBM)] * 4,
        out_specs=[pl.BlockSpec(memory_space=v)] * 4,
        scratch_shapes=[
            v((MSG + 16, LANES), F32),
            v((RW, RANK), F32),
            v((CW, RANK), F32),
            v((BW, RANK), F32),
            v((FRAMES, RANK), F32),
            v((TB, ROWS, COLS), BF16),
            v((BW, LANES), F32),
            v((2, NLZ, 8, LANES), F32),
            v((NX, BW, LANES), F32),
            v((ROWS, LANES), F32),
            v((BANDS, LANES), F32),
            v((NY * RW, LANES), F32),
            v((LANES, LANES), F32),
            v((COLS, TB * ROWS), BF16),
            v((FRAMES, HALF, 2 * LANES), BF16),
            v((FRAMES, COLS, LANES), F32),
            v((2, NLZ, PACK, LANES), F32),
            v((NLZ, PACK, LANES), F32),
            v((NLZ, PACK, LANES), F32),
            v((NLZ, PACK, LANES), F32),
            v((NX, PACK + 8, LANES), F32),
            v((NX, PACK + 8, LANES), F32),
            v((2, NLZ, PACK, LANES), F32),
            v((COLS, LANES), F32),
            v((COLS, LANES), BF16),
            v((TB * QROWS, LANES), F32),
            v((4, TB, 8, LANES), F32),
            v((RW, LANES), F32),
            v((FRAMES, LANES), F32),
            v((NX, FRAMES, LANES), F32),
            v((4, 2, 24, LANES), F32),
            v((NX, 2, 24, LANES), F32),
            v((4, 2, 24, LANES), F32),
            v((LANES, LANES), F32),
            v((2, NLZ, 8, LANES), F32),
            v((NLZ, 8, LANES), F32),
            v((NLZ, 8, LANES), F32),
            v((NLZ, 8, LANES), F32),
            pltpu.SemaphoreType.DMA((LOADS + 4,)),
            pltpu.SemaphoreType.DMA((N_SEMS,)),
            pltpu.SemaphoreType.DMA((N_SEMS,)),
        ],
        compiler_params=pltpu.CompilerParams(
            collective_id=0, has_side_effects=True, vmem_limit_bytes=48 * 1024 * 1024
        ),
        cost_estimate=pl.CostEstimate(
            flops=4 * RANK * TB * ROWS * COLS, bytes_accessed=2 * TB * ROWS * COLS, transcendentals=0
        ),
    )(
        tensor.reshape(TB, ROWS, COLS),
        *factors,
    )
    out = pl.pallas_call(
        hand_over,
        out_shape=shapes,
        in_specs=[pl.BlockSpec(memory_space=v)] * 4,
        out_specs=[pl.BlockSpec(memory_space=pl.ANY)] * 4,
        scratch_shapes=[pltpu.SemaphoreType.DMA((4,))],
    )(*[pltpu.with_memory_space_constraint(x, v) for x in out])
    return tuple(x.T for x in out)


def solution(mesh):
    return jax.shard_map(
        shards,
        mesh=mesh,
        in_specs=(
            P(None, "gy", "gx", None),
            P(None, ("gx", "gy")),
            P(None, "gy"),
            P(None, ("gy", "gx")),
            P(),
        ),
        out_specs=(P(None, ("gx", "gy")), P(None, "gy"), P(None, ("gy", "gx")), P()),
        check_vma=False,
    )
```

```python
import jax
import jax.numpy as jnp
from jax import lax
from jax.experimental import pallas as pl
from jax.experimental.pallas import tpu as pltpu
from jax.sharding import PartitionSpec as P

MESH = pl.DeviceIdType.MESH
HIGHEST = lax.Precision.HIGHEST
F32 = jnp.float32
BF16 = jnp.bfloat16

NX, NY, NLZ = 8, 32, 16
RANK, LANES = 96, 128
FRAMES, BANDS, ROWS, COLS = 2, 16, 128, 1024
RW, CW, BW = 4, 32, 2
PACK = CW * RANK // LANES
TB = FRAMES * BANDS
HALF = BANDS * ROWS
CHUNKS = 4
CHUNK = COLS // CHUNKS
PER = NLZ // CHUNKS
LOADS = 8
MSG = CW + 8
QROWS = ROWS // 4

(
    S_ROW, S_BAND, S_BANDX, S_COL, S_COLC, S_R1, S_R2, S_R3, S_F1, S_F2,
    S_GRAM, S_GRAMP, S_ROWS, S_BANDS,
) = [0, 1, 2, 3, 4, 5, 9, 10, 11, 12, 13, 14, 15, 16]
N_SEMS = 17


def dot(x, y):
    return jnp.dot(x, y, preferred_element_type=F32)


def exact(x, y):
    return jnp.dot(x, y, precision=HIGHEST, preferred_element_type=F32)


def total(ref, count):
    out = ref[0]
    for k in range(1, count):
        out = out + ref[k]
    return out


def wrap(index, size):
    return jnp.where(index >= size, index - size, index)


def lane_of(x):
    return lax.broadcasted_iota(jnp.int32, x.shape, 1)


def pack(tiles):
    spare = lane_of(tiles[3]) >= RANK
    return [
        jnp.where(spare, pltpu.roll(tiles[3], RANK - 32 * m, 1), tiles[m]) for m in range(3)
    ]


def unpack(tiles):
    lane = lane_of(tiles[0])
    last = jnp.zeros_like(tiles[0])
    for m in (2, 1, 0):
        last = jnp.where(lane < 32 * m + 32, pltpu.roll(tiles[m], 32 * m + 32, 1), last)
    zero = jnp.zeros_like(last)
    return [jnp.where(lane < RANK, tile, zero) for tile in tiles] + [
        jnp.where(lane < RANK, last, zero)
    ]


def kernel(
    tensor, row_in, col_in, band_in, time_in,
    row_out, col_out, band_out, time_out,
    packed, row_v, col_v, band_v, time_v,
    data, mine4, mine2, rowg, bandg, bandx, row_t, band_t, bandx_t, tb_t,
    turned, prod, by_frame, part, recv1, sum1, recv2, fin, recv3,
    colg, colf, low, folded, partials,
    fpart, fg, fsum, fx, gpart, grecv, gall, gcols,
    rsend, rrecv, bsend, brecv,
    local_sems, send_sems, recv_sems,
):
    a = lax.axis_index("gx")
    g = lax.axis_index("gy")
    lz = lax.div(g, 2)
    c = g - 2 * lz
    l = lax.div(lz, 8)
    z = lz - 8 * l
    p = l * 2 + c
    other = 1 - c
    partner = lz * 2 + other
    gy_peers = [wrap(g + k, NY) for k in range(1, NY)]
    gx_peers = [wrap(a + k, NX) for k in range(1, NX)]
    core_peers = [wrap(lz + k, NLZ) * 2 + c for k in range(1, NLZ)]

    def send(src, dst, sem, device):
        pltpu.make_async_remote_copy(
            src_ref=src, dst_ref=dst, send_sem=send_sems.at[sem], recv_sem=recv_sems.at[sem],
            device_id=device, device_id_type=MESH,
        ).start()

    def arrived(ref, sem):
        pltpu.make_async_copy(ref, ref, recv_sems.at[sem]).wait()

    def sent(ref, sem):
        pltpu.make_async_copy(ref, ref, send_sems.at[sem]).wait()

    small = [
        pltpu.make_async_copy(src, dst, local_sems.at[LOADS + k])
        for k, (src, dst) in enumerate(
            [(row_in, row_v), (band_in, band_v), (col_in, col_v), (time_in, time_v)]
        )
    ]
    for copy in small:
        copy.start()

    barrier = pltpu.get_barrier_semaphore()
    for to in gy_peers:
        pl.semaphore_signal(barrier, inc=1, device_id=(a, to), device_id_type=MESH)
    for to in gx_peers:
        pl.semaphore_signal(barrier, inc=1, device_id=(to, g), device_id_type=MESH)

    for k in range(LOADS):
        span = pl.ds(k * (TB // LOADS), TB // LOADS)
        pltpu.make_async_copy(tensor.at[span], data.at[span], local_sems.at[k]).start()

    tb_t[...] = jnp.zeros_like(tb_t)
    packed[...] = jnp.zeros_like(packed)
    for copy in small:
        copy.wait()
    packed[0:CW, 0:RANK] = col_v[...]
    packed[CW : CW + BW, 0:RANK] = band_v[...]
    packed[MSG : MSG + RW, 0:RANK] = row_v[...]
    packed[MSG + 8 : MSG + 8 + FRAMES, 0:RANK] = time_v[...]
    mine2[...] = packed[CW : CW + BW]
    mine4[...] = packed[MSG : MSG + RW]
    time8 = packed[MSG + 8 :]
    rowg[g] = mine4[...]
    bandg[a] = mine2[...]
    bandx[g] = mine2[...]
    for m, tile in enumerate(pack([packed[8 * m : 8 * m + 8] for m in range(4)])):
        colg[c, lz, 8 * m : 8 * m + 8] = tile

    pl.semaphore_wait(barrier, NY - 1 + NX - 1)

    for to in gy_peers:
        send(mine4, rowg.at[g], S_ROW, (a, to))
    for to in gx_peers:
        send(mine2, bandg.at[a], S_BAND, (to, g))
    for to in core_peers:
        send(colg.at[c, lz], colg.at[c, lz], S_COL, (a, to))
    for to in gy_peers:
        send(mine2, bandx.at[g], S_BANDX, (a, to))

    @pl.loop(0, LOADS)
    def _(k):
        per = TB // LOADS
        span = pl.ds(k * per, per)
        pltpu.make_async_copy(tensor.at[span], data.at[span], local_sems.at[k]).wait()
        for i in range(per):
            at = pl.multiple_of((k * per + i) * ROWS, ROWS)
            turned[:, pl.ds(at, ROWS)] = data[k * per + i].T


    arrived(bandg.at[pl.ds(0, NX - 1)], S_BAND)
    for k in range(NX):
        band_t[BW * k : BW * k + BW] = bandg[k]
    for t in range(FRAMES):
        tb_t[t * BANDS : (t + 1) * BANDS] = time8[t : t + 1] * band_t[...]
    tb_t[TB : TB + BANDS] = band_t[...]
    arrived(rowg.at[pl.ds(0, NY - 1)], S_ROW)
    for k in range(NY):
        row_t[RW * k : RW * k + RW] = rowg[k]

    @pl.loop(0, BANDS)
    def _(k):
        span = pl.ds(pl.multiple_of(k * ROWS, ROWS), ROWS)
        rows = row_t[...]
        plain = (tb_t[pl.ds(TB + k, 1)] * rows).astype(BF16)
        for t in range(FRAMES):
            prod[t, span, 0:LANES] = (tb_t[pl.ds(t * BANDS + k, 1)] * rows).astype(BF16)
            prod[t, span, LANES:] = plain

    def slot_lz(n, i):
        return (i // 2) * (NLZ // 2) + 2 * n + i % 2

    def send_pieces(n):
        span = pl.ds(n * PER, PER)
        arrived(recv1.at[span], S_R1 + n)
        sum1[span] = part[c, span] + recv1[span]
        for i in range(PER):
            k = slot_lz(n, i)

            @pl.when(k != lz)
            def _():
                send(sum1.at[n * PER + i], recv2.at[lz], S_R2, (a, k * 2 + c))

            @pl.when(k == lz)
            def _():
                recv2[lz] = sum1[n * PER + i]

    @pl.loop(0, CHUNKS)
    def _(n):
        heres = [
            pl.ds(pl.multiple_of(i * (COLS // 2) + n * (CHUNK // 2), CHUNK // 2), CHUNK // 2)
            for i in range(2)
        ]
        acc = jnp.zeros((CHUNK, LANES), F32)
        for t in range(FRAMES):
            both = dot(
                jnp.concatenate(
                    [turned[here, t * HALF : (t + 1) * HALF] for here in heres], axis=0
                ),
                prod[t],
            )
            for i, here in enumerate(heres):
                by_frame[t, here] = both[i * (CHUNK // 2) : (i + 1) * (CHUNK // 2), LANES:]
            acc = acc + both[:, 0:LANES]
        acc = acc.reshape(CHUNK // CW, 4, 8, LANES)
        tiles = pack([acc[:, m].reshape(CHUNK // 4, LANES) for m in range(4)])
        for k in range(CHUNK // CW):
            for m in range(3):
                part[k % 2, n * PER + k // 2, 8 * m : 8 * m + 8] = tiles[m][8 * k : 8 * k + 8]
        span = pl.ds(n * PER, PER)

        @pl.when(n == 0)
        def _():
            for i in range(PER):
                for j in range(2):
                    to = slot_lz(0, i) * 2 + j

                    @pl.when(to != g)
                    def _():
                        send(part.at[j, i], recv2.at[c * NLZ + lz], S_R2, (a, to))

                    @pl.when(to == g)
                    def _():
                        recv2[c * NLZ + lz] = part[j, i]

        @pl.when(n > 0)
        def _():
            send(part.at[other, span], recv1.at[span], S_R1 + n, (a, partner))

    arrived(colg.at[0, pl.ds(0, NLZ - 1)], S_COL)
    send(colg.at[c], colg.at[c], S_COLC, (a, partner))

    arrived(bandx.at[pl.ds(0, NY - 1)], S_BANDX)
    for k in range(NY):
        bandx_t[BW * k : BW * k + BW] = bandx[k]
    for i, ref in enumerate((row_t, bandx_t)):
        gram = exact(ref[...].T, ref[...])
        for k in range(4):
            gpart[k, i] = gram[24 * k : 24 * k + 24]
    grecv[a] = gpart[p]
    for to in gx_peers:
        send(gpart.at[p], grecv.at[a], S_GRAM, (to, g))

    @pl.loop(1, CHUNKS)
    def _(n):
        send_pieces(n)

    arrived(colg.at[0], S_COLC)
    for i in range(2):
        tiles = unpack(
            [colg[i, :, 8 * m : 8 * m + 8].reshape(8 * NLZ, LANES) for m in range(3)]
        )
        for k in range(NLZ):
            block = jnp.concatenate([tile[8 * k : 8 * k + 8] for tile in tiles], axis=0)
            at = (2 * k + i) * CW
            colf[at : at + CW] = block
            low[at : at + CW] = block.astype(BF16)

    for t in range(FRAMES):
        fpart[t : t + 1] = jnp.sum(
            by_frame[t] * low[...].astype(F32), axis=0, keepdims=True
        )
    fg[g] = fpart[...]
    for to in gy_peers:
        send(fpart, fg.at[g], S_F1, (a, to))

    @pl.loop(0, 4)
    def _(q):
        half = QROWS // 2
        heres = [pl.ds(pl.multiple_of(i * (ROWS // 2) + q * half, half), half) for i in range(2)]
        block = jnp.concatenate([data[:, here, :] for here in heres], axis=1)
        folded[...] = dot(block.reshape(TB * QROWS, COLS), low[...])
        rows = jnp.zeros((QROWS, LANES), F32)
        row_here = jnp.concatenate([row_t[here] for here in heres], axis=0)
        for j in range(TB):
            block = folded[j * QROWS : (j + 1) * QROWS]
            rows = rows + block * tb_t[j : j + 1]
            block = block * row_here
            partials[q, j] = jnp.sum(block.reshape(QROWS // 8, 8, LANES), axis=0)
        owners = [(i // 4) * (NY // 2) + 4 * q + i % 4 for i in range(NY // 4)]
        for i, k in enumerate(owners):
            rsend[k] = rows[RW * i : RW * i + RW]
        for k in owners:

            @pl.when(k != g)
            def _():
                send(rsend.at[k], rrecv.at[g], S_ROWS, (a, k))

    sums = total(partials, 4)
    bands = jnp.zeros((BANDS, LANES), F32)
    for t in range(FRAMES):
        bands = bands + time8[t : t + 1] * jnp.sum(sums[t * BANDS : (t + 1) * BANDS], axis=1)
    for k in range(NX):
        bsend[k] = bands[BW * k : BW * k + BW]
    for k in range(1, NX):
        to = wrap(a + k, NX)
        send(bsend.at[to], brecv.at[a], S_BANDS, (to, g))
    brecv[a] = bsend[a]
    rrecv[g] = rsend[g]

    arrived(grecv.at[pl.ds(0, NX - 1)], S_GRAM)
    gall[p] = total(grecv, NX)
    for k in range(1, 4):
        to = wrap(p + k, 4)
        to_l = lax.div(to, 2)
        send(gall.at[p], gall.at[p], S_GRAMP, (a, (to_l * 8 + z) * 2 + to - 2 * to_l))

    @pl.when(z < 2)
    def _():
        arrived(recv2.at[pl.ds(0, NY - 1)], S_R2)
        fin[...] = total(recv2, NY)

    @pl.when(z >= 2)
    def _():
        arrived(recv2.at[pl.ds(0, NLZ - 1)], S_R2)
        fin[...] = total(recv2, NLZ)

    recv3[a] = fin[...]
    for to in gx_peers:
        send(fin, recv3.at[a], S_R3, (to, g))
    arrived(fg.at[pl.ds(0, NY - 1)], S_F1)
    fsum[...] = total(fg, NY)
    fx[a] = fsum[...]
    for to in gx_peers:
        send(fsum, fx.at[a], S_F2, (to, g))

    gcols[...] = jnp.zeros_like(gcols)

    @pl.loop(0, 4)
    def _(i):
        block = colf[pl.ds(pl.multiple_of(i * 256, 256), 256)]
        gcols[...] += exact(block.T, block)

    gram_cols = gcols[...]
    arrived(gall.at[pl.ds(0, 3)], S_GRAMP)
    pad = jnp.zeros((LANES - RANK, LANES), F32)
    gram_rows, gram_bands = (
        jnp.concatenate([gall[:, i].reshape(RANK, LANES), pad], axis=0) for i in range(2)
    )
    time_n = jnp.concatenate([time8, jnp.zeros((LANES - 8, LANES), F32)], axis=0).T
    gram_time = time_n[:, 0:1] * time8[0:1] + time_n[:, 1:2] * time8[1:2]
    row_model = exact(packed[MSG : MSG + 8], gram_cols * gram_bands * gram_time)
    col_model = exact(packed[0:CW], gram_rows * gram_bands * gram_time)
    band_model = exact(packed[CW:MSG], gram_rows * gram_cols * gram_time)
    time_model = exact(time8, gram_rows * gram_cols * gram_bands)

    arrived(fx.at[pl.ds(0, NX - 1)], S_F2)
    time_out[...] = (time_model[0:FRAMES] - total(fx, NX))[:, 0:RANK]
    arrived(recv3.at[pl.ds(0, NX - 1)], S_R3)
    sums = total(recv3, NX)
    sums = jnp.concatenate(unpack([sums[8 * m : 8 * m + 8] for m in range(3)]), axis=0)
    col_out[...] = (col_model - sums)[:, 0:RANK]
    arrived(rrecv.at[pl.ds(0, NY - 1)], S_ROWS)
    row_out[...] = (row_model[0:RW] - total(rrecv, NY))[:, 0:RANK]
    arrived(brecv.at[pl.ds(0, NX - 1)], S_BANDS)
    band_out[...] = (band_model[0:BW] - total(brecv, NX))[:, 0:RANK]

    sent(rowg.at[pl.ds(0, NY - 1)], S_ROW)
    sent(bandg.at[pl.ds(0, NX - 1)], S_BAND)
    sent(bandx.at[pl.ds(0, NY - 1)], S_BANDX)
    sent(colg.at[0, pl.ds(0, NLZ - 1)], S_COL)
    sent(colg.at[0], S_COLC)
    for n in range(1, CHUNKS):
        sent(recv1.at[pl.ds(n * PER, PER)], S_R1 + n)
    sent(recv2.at[pl.ds(0, 2 * PER + (CHUNKS - 1) * PER - 1)], S_R2)
    sent(recv3.at[pl.ds(0, NX - 1)], S_R3)
    sent(fg.at[pl.ds(0, NY - 1)], S_F1)
    sent(fx.at[pl.ds(0, NX - 1)], S_F2)
    sent(grecv.at[pl.ds(0, NX - 1)], S_GRAM)
    sent(gall.at[pl.ds(0, 3)], S_GRAMP)
    sent(rrecv.at[pl.ds(0, NY - 1)], S_ROWS)
    sent(brecv.at[pl.ds(0, NX - 1)], S_BANDS)


def hand_over(*refs):
    sems = refs[8]
    copies = [
        pltpu.make_async_copy(refs[k], refs[4 + k], sems.at[k]) for k in range(4)
    ]
    for copy in copies:
        copy.start()
    for copy in copies:
        copy.wait()


def shards(tensor, row_factor, column_factor, band_factor, time_factor):
    v = pltpu.VMEM
    shapes = tuple(jax.ShapeDtypeStruct((n, RANK), F32) for n in (RW, CW, BW, FRAMES))
    factors = (row_factor, column_factor, band_factor, time_factor)
    factors = [pltpu.with_memory_space_constraint(x.T, pltpu.HBM) for x in factors]
    out = pl.pallas_call(
        kernel,
        out_shape=shapes,
        in_specs=[pl.BlockSpec(memory_space=pl.ANY)] + [pl.BlockSpec(memory_space=pltpu.HBM)] * 4,
        out_specs=[pl.BlockSpec(memory_space=v)] * 4,
        scratch_shapes=[
            v((MSG + 16, LANES), F32),
            v((RW, RANK), F32),
            v((CW, RANK), F32),
            v((BW, RANK), F32),
            v((FRAMES, RANK), F32),
            v((TB, ROWS, COLS), BF16),
            v((RW, LANES), F32),
            v((BW, LANES), F32),
            v((NY, RW, LANES), F32),
            v((NX, BW, LANES), F32),
            v((NY, BW, LANES), F32),
            v((ROWS, LANES), F32),
            v((BANDS, LANES), F32),
            v((NY * BW, LANES), F32),
            v((LANES, LANES), F32),
            v((COLS, TB * ROWS), BF16),
            v((FRAMES, HALF, 2 * LANES), BF16),
            v((FRAMES, COLS, LANES), F32),
            v((2, NLZ, PACK, LANES), F32),
            v((NLZ, PACK, LANES), F32),
            v((NLZ, PACK, LANES), F32),
            v((NY, PACK, LANES), F32),
            v((PACK, LANES), F32),
            v((NX, PACK, LANES), F32),
            v((2, NLZ, PACK, LANES), F32),
            v((COLS, LANES), F32),
            v((COLS, LANES), BF16),
            v((TB * QROWS, LANES), F32),
            v((4, TB, 8, LANES), F32),
            v((FRAMES, LANES), F32),
            v((NY, FRAMES, LANES), F32),
            v((FRAMES, LANES), F32),
            v((NX, FRAMES, LANES), F32),
            v((4, 2, 24, LANES), F32),
            v((NX, 2, 24, LANES), F32),
            v((4, 2, 24, LANES), F32),
            v((LANES, LANES), F32),
            v((NY, RW, LANES), F32),
            v((NY, RW, LANES), F32),
            v((NX, BW, LANES), F32),
            v((NX, BW, LANES), F32),
            pltpu.SemaphoreType.DMA((LOADS + 4,)),
            pltpu.SemaphoreType.DMA((N_SEMS,)),
            pltpu.SemaphoreType.DMA((N_SEMS,)),
        ],
        compiler_params=pltpu.CompilerParams(
            collective_id=0, has_side_effects=True, vmem_limit_bytes=48 * 1024 * 1024
        ),
        cost_estimate=pl.CostEstimate(
            flops=4 * RANK * TB * ROWS * COLS, bytes_accessed=2 * TB * ROWS * COLS, transcendentals=0
        ),
    )(
        tensor.reshape(TB, ROWS, COLS),
        *factors,
    )
    out = pl.pallas_call(
        hand_over,
        out_shape=shapes,
        in_specs=[pl.BlockSpec(memory_space=v)] * 4,
        out_specs=[pl.BlockSpec(memory_space=pl.ANY)] * 4,
        scratch_shapes=[pltpu.SemaphoreType.DMA((4,))],
    )(*[pltpu.with_memory_space_constraint(x, v) for x in out])
    return tuple(x.T for x in out)


def solution(mesh):
    return jax.shard_map(
        shards,
        mesh=mesh,
        in_specs=(
            P(None, "gy", "gx", None),
            P(None, ("gx", "gy")),
            P(None, "gy"),
            P(None, ("gy", "gx")),
            P(),
        ),
        out_specs=(P(None, ("gx", "gy")), P(None, "gy"), P(None, ("gy", "gx")), P()),
        check_vma=False,
    )
```

```python
import jax
import jax.numpy as jnp
from jax import lax
from jax.experimental import pallas as pl
from jax.experimental.pallas import tpu as pltpu
from jax.sharding import PartitionSpec as P

MESH = pl.DeviceIdType.MESH
HIGHEST = lax.Precision.HIGHEST
F32 = jnp.float32
BF16 = jnp.bfloat16

NX, NY, NLZ = 8, 32, 16
RANK, LANES = 96, 128
FRAMES, BANDS, ROWS, COLS = 2, 16, 128, 1024
RW, CW, BW = 4, 32, 2
PACK = CW * RANK // LANES
TB = FRAMES * BANDS
HALF = BANDS * ROWS
CHUNKS = 4
CHUNK = COLS // CHUNKS
PER = NLZ // CHUNKS
LOADS = 8
MSG = CW + 8
QROWS = ROWS // 4

(
    S_ROW, S_BAND, S_BANDX, S_COL, S_COLC, S_R1, S_R2, S_R3, S_F1, S_F2,
    S_GRAM, S_GRAMP, S_ROWS, S_BANDS,
) = [0, 1, 2, 3, 4, 5, 9, 10, 11, 12, 13, 14, 15, 16]
N_SEMS = 17


def dot(x, y):
    return jnp.dot(x, y, preferred_element_type=F32)


def exact(x, y):
    return jnp.dot(x, y, precision=HIGHEST, preferred_element_type=F32)


def total(ref, count):
    out = ref[0]
    for k in range(1, count):
        out = out + ref[k]
    return out


def wrap(index, size):
    return jnp.where(index >= size, index - size, index)


def lane_of(x):
    return lax.broadcasted_iota(jnp.int32, x.shape, 1)


def pack(tiles):
    spare = lane_of(tiles[3]) >= RANK
    return [
        jnp.where(spare, pltpu.roll(tiles[3], RANK - 32 * m, 1), tiles[m]) for m in range(3)
    ]


def unpack(tiles):
    lane = lane_of(tiles[0])
    last = jnp.zeros_like(tiles[0])
    for m in (2, 1, 0):
        last = jnp.where(lane < 32 * m + 32, pltpu.roll(tiles[m], 32 * m + 32, 1), last)
    zero = jnp.zeros_like(last)
    return [jnp.where(lane < RANK, tile, zero) for tile in tiles] + [
        jnp.where(lane < RANK, last, zero)
    ]


def kernel(
    tensor, row_in, col_in, band_in, time_in,
    row_out, col_out, band_out, time_out,
    packed, row_v, col_v, band_v, time_v,
    data, mine4, mine2, rowg, bandg, bandx, row_t, band_t, bandx_t, tb_t,
    turned, prod, by_frame, part, recv1, sum1, recv2, fin, recv3,
    colg, colf, low, folded, partials,
    fpart, fg, fsum, fx, gpart, grecv, gall, gcols,
    rsend, rrecv, bsend, brecv,
    local_sems, send_sems, recv_sems,
):
    a = lax.axis_index("gx")
    g = lax.axis_index("gy")
    lz = lax.div(g, 2)
    c = g - 2 * lz
    l = lax.div(lz, 8)
    z = lz - 8 * l
    p = l * 2 + c
    other = 1 - c
    partner = lz * 2 + other
    gy_peers = [wrap(g + k, NY) for k in range(1, NY)]
    gx_peers = [wrap(a + k, NX) for k in range(1, NX)]
    core_peers = [wrap(lz + k, NLZ) * 2 + c for k in range(1, NLZ)]

    def send(src, dst, sem, device):
        pltpu.make_async_remote_copy(
            src_ref=src, dst_ref=dst, send_sem=send_sems.at[sem], recv_sem=recv_sems.at[sem],
            device_id=device, device_id_type=MESH,
        ).start()

    def arrived(ref, sem):
        pltpu.make_async_copy(ref, ref, recv_sems.at[sem]).wait()

    def sent(ref, sem):
        pltpu.make_async_copy(ref, ref, send_sems.at[sem]).wait()

    small = [
        pltpu.make_async_copy(src, dst, local_sems.at[LOADS + k])
        for k, (src, dst) in enumerate(
            [(row_in, row_v), (band_in, band_v), (col_in, col_v), (time_in, time_v)]
        )
    ]
    for copy in small:
        copy.start()

    barrier = pltpu.get_barrier_semaphore()
    for to in gy_peers:
        pl.semaphore_signal(barrier, inc=1, device_id=(a, to), device_id_type=MESH)
    for to in gx_peers:
        pl.semaphore_signal(barrier, inc=1, device_id=(to, g), device_id_type=MESH)

    for k in range(LOADS):
        span = pl.ds(k * (TB // LOADS), TB // LOADS)
        pltpu.make_async_copy(tensor.at[span], data.at[span], local_sems.at[k]).start()

    tb_t[...] = jnp.zeros_like(tb_t)
    packed[...] = jnp.zeros_like(packed)
    for copy in small:
        copy.wait()
    packed[0:CW, 0:RANK] = col_v[...]
    packed[CW : CW + BW, 0:RANK] = band_v[...]
    packed[MSG : MSG + RW, 0:RANK] = row_v[...]
    packed[MSG + 8 : MSG + 8 + FRAMES, 0:RANK] = time_v[...]
    mine2[...] = packed[CW : CW + BW]
    mine4[...] = packed[MSG : MSG + RW]
    time8 = packed[MSG + 8 :]
    rowg[g] = mine4[...]
    bandg[a] = mine2[...]
    bandx[g] = mine2[...]
    for m, tile in enumerate(pack([packed[8 * m : 8 * m + 8] for m in range(4)])):
        colg[c, lz, 8 * m : 8 * m + 8] = tile

    def turn(k):
        per = TB // LOADS
        span = pl.ds(k * per, per)
        pltpu.make_async_copy(tensor.at[span], data.at[span], local_sems.at[k]).wait()
        for i in range(per):
            at = pl.multiple_of((k * per + i) * ROWS, ROWS)
            turned[:, pl.ds(at, ROWS)] = data[k * per + i].T

    early = jnp.where(z == 0, 6, jnp.where(z == 1, 5, jnp.where(z == 2, 3, jnp.where(z == 3, 1, 0))))
    pl.loop(0, early)(turn)
    pl.semaphore_wait(barrier, NY - 1 + NX - 1)

    for to in gy_peers:
        send(mine4, rowg.at[g], S_ROW, (a, to))
    for to in gx_peers:
        send(mine2, bandg.at[a], S_BAND, (to, g))
    for to in core_peers:
        send(colg.at[c, lz], colg.at[c, lz], S_COL, (a, to))

    pl.loop(early, LOADS)(turn)

    for to in gy_peers:
        send(mine2, bandx.at[g], S_BANDX, (a, to))

    arrived(bandg.at[pl.ds(0, NX - 1)], S_BAND)
    for k in range(NX):
        band_t[BW * k : BW * k + BW] = bandg[k]
    for t in range(FRAMES):
        tb_t[t * BANDS : (t + 1) * BANDS] = time8[t : t + 1] * band_t[...]
    tb_t[TB : TB + BANDS] = band_t[...]
    arrived(rowg.at[pl.ds(0, NY - 1)], S_ROW)
    for k in range(NY):
        row_t[RW * k : RW * k + RW] = rowg[k]

    @pl.loop(0, BANDS)
    def _(k):
        span = pl.ds(pl.multiple_of(k * ROWS, ROWS), ROWS)
        rows = row_t[...]
        plain = (tb_t[pl.ds(TB + k, 1)] * rows).astype(BF16)
        for t in range(FRAMES):
            prod[t, span, 0:LANES] = (tb_t[pl.ds(t * BANDS + k, 1)] * rows).astype(BF16)
            prod[t, span, LANES:] = plain

    def slot_lz(n, i):
        return (i // 2) * (NLZ // 2) + 2 * n + i % 2

    def send_pieces(n):
        span = pl.ds(n * PER, PER)
        arrived(recv1.at[span], S_R1 + n)
        sum1[span] = part[c, span] + recv1[span]
        for i in range(PER):
            k = slot_lz(n, i)

            @pl.when(k != lz)
            def _():
                send(sum1.at[n * PER + i], recv2.at[lz], S_R2, (a, k * 2 + c))

            @pl.when(k == lz)
            def _():
                recv2[lz] = sum1[n * PER + i]

    @pl.loop(0, CHUNKS)
    def _(n):
        heres = [
            pl.ds(pl.multiple_of(i * (COLS // 2) + n * (CHUNK // 2), CHUNK // 2), CHUNK // 2)
            for i in range(2)
        ]
        acc = jnp.zeros((CHUNK, LANES), F32)
        for t in range(FRAMES):
            both = dot(
                jnp.concatenate(
                    [turned[here, t * HALF : (t + 1) * HALF] for here in heres], axis=0
                ),
                prod[t],
            )
            for i, here in enumerate(heres):
                by_frame[t, here] = both[i * (CHUNK // 2) : (i + 1) * (CHUNK // 2), LANES:]
            acc = acc + both[:, 0:LANES]
        acc = acc.reshape(CHUNK // CW, 4, 8, LANES)
        tiles = pack([acc[:, m].reshape(CHUNK // 4, LANES) for m in range(4)])
        for k in range(CHUNK // CW):
            for m in range(3):
                part[k % 2, n * PER + k // 2, 8 * m : 8 * m + 8] = tiles[m][8 * k : 8 * k + 8]
        span = pl.ds(n * PER, PER)
        send(part.at[other, span], recv1.at[span], S_R1 + n, (a, partner))

    gram = exact(row_t[...].T, row_t[...])
    for k in range(4):
        gpart[k, 0] = gram[24 * k : 24 * k + 24]

    @pl.loop(0, CHUNKS)
    def _(n):
        send_pieces(n)

    arrived(colg.at[0, pl.ds(0, NLZ - 1)], S_COL)
    send(colg.at[c], colg.at[c], S_COLC, (a, partner))
    arrived(bandx.at[pl.ds(0, NY - 1)], S_BANDX)
    for k in range(NY):
        bandx_t[BW * k : BW * k + BW] = bandx[k]
    gram = exact(bandx_t[...].T, bandx_t[...])
    for k in range(4):
        gpart[k, 1] = gram[24 * k : 24 * k + 24]
    grecv[a] = gpart[p]
    for to in gx_peers:
        send(gpart.at[p], grecv.at[a], S_GRAM, (to, g))

    arrived(colg.at[0], S_COLC)
    for i in range(2):
        tiles = unpack(
            [colg[i, :, 8 * m : 8 * m + 8].reshape(8 * NLZ, LANES) for m in range(3)]
        )
        for k in range(NLZ):
            block = jnp.concatenate([tile[8 * k : 8 * k + 8] for tile in tiles], axis=0)
            at = (2 * k + i) * CW
            colf[at : at + CW] = block
            low[at : at + CW] = block.astype(BF16)

    for t in range(FRAMES):
        fpart[t : t + 1] = jnp.sum(
            by_frame[t] * low[...].astype(F32), axis=0, keepdims=True
        )
    fg[g] = fpart[...]
    for to in gy_peers:
        send(fpart, fg.at[g], S_F1, (a, to))

    @pl.loop(0, 4)
    def _(q):
        half = QROWS // 2
        heres = [pl.ds(pl.multiple_of(i * (ROWS // 2) + q * half, half), half) for i in range(2)]
        block = jnp.concatenate([data[:, here, :] for here in heres], axis=1)
        folded[...] = dot(block.reshape(TB * QROWS, COLS), low[...])
        rows = jnp.zeros((QROWS, LANES), F32)
        row_here = jnp.concatenate([row_t[here] for here in heres], axis=0)
        for j in range(TB):
            block = folded[j * QROWS : (j + 1) * QROWS]
            rows = rows + block * tb_t[j : j + 1]
            block = block * row_here
            partials[q, j] = jnp.sum(block.reshape(QROWS // 8, 8, LANES), axis=0)
        owners = [(i // 4) * (NY // 2) + 4 * q + i % 4 for i in range(NY // 4)]
        for i, k in enumerate(owners):
            rsend[k] = rows[RW * i : RW * i + RW]
        for k in owners:

            @pl.when(k != g)
            def _():
                send(rsend.at[k], rrecv.at[g], S_ROWS, (a, k))

    sums = total(partials, 4)
    bands = jnp.zeros((BANDS, LANES), F32)
    for t in range(FRAMES):
        bands = bands + time8[t : t + 1] * jnp.sum(sums[t * BANDS : (t + 1) * BANDS], axis=1)
    for k in range(NX):
        bsend[k] = bands[BW * k : BW * k + BW]
    for k in range(1, NX):
        to = wrap(a + k, NX)
        send(bsend.at[to], brecv.at[a], S_BANDS, (to, g))
    brecv[a] = bsend[a]
    rrecv[g] = rsend[g]

    arrived(grecv.at[pl.ds(0, NX - 1)], S_GRAM)
    gall[p] = total(grecv, NX)
    for k in range(1, 4):
        to = wrap(p + k, 4)
        to_l = lax.div(to, 2)
        send(gall.at[p], gall.at[p], S_GRAMP, (a, (to_l * 8 + z) * 2 + to - 2 * to_l))
    arrived(recv2.at[pl.ds(0, NLZ - 1)], S_R2)
    fin[...] = total(recv2, NLZ)
    recv3[a] = fin[...]
    for to in gx_peers:
        send(fin, recv3.at[a], S_R3, (to, g))
    arrived(fg.at[pl.ds(0, NY - 1)], S_F1)
    fsum[...] = total(fg, NY)
    fx[a] = fsum[...]
    for to in gx_peers:
        send(fsum, fx.at[a], S_F2, (to, g))

    gcols[...] = jnp.zeros_like(gcols)

    @pl.loop(0, 4)
    def _(i):
        block = colf[pl.ds(pl.multiple_of(i * 256, 256), 256)]
        gcols[...] += exact(block.T, block)

    gram_cols = gcols[...]
    arrived(gall.at[pl.ds(0, 3)], S_GRAMP)
    pad = jnp.zeros((LANES - RANK, LANES), F32)
    gram_rows, gram_bands = (
        jnp.concatenate([gall[:, i].reshape(RANK, LANES), pad], axis=0) for i in range(2)
    )
    time_n = jnp.concatenate([time8, jnp.zeros((LANES - 8, LANES), F32)], axis=0).T
    gram_time = time_n[:, 0:1] * time8[0:1] + time_n[:, 1:2] * time8[1:2]
    row_model = exact(packed[MSG : MSG + 8], gram_cols * gram_bands * gram_time)
    col_model = exact(packed[0:CW], gram_rows * gram_bands * gram_time)
    band_model = exact(packed[CW:MSG], gram_rows * gram_cols * gram_time)
    time_model = exact(time8, gram_rows * gram_cols * gram_bands)

    arrived(fx.at[pl.ds(0, NX - 1)], S_F2)
    time_out[...] = (time_model[0:FRAMES] - total(fx, NX))[:, 0:RANK]
    arrived(recv3.at[pl.ds(0, NX - 1)], S_R3)
    sums = total(recv3, NX)
    sums = jnp.concatenate(unpack([sums[8 * m : 8 * m + 8] for m in range(3)]), axis=0)
    col_out[...] = (col_model - sums)[:, 0:RANK]
    arrived(rrecv.at[pl.ds(0, NY - 1)], S_ROWS)
    row_out[...] = (row_model[0:RW] - total(rrecv, NY))[:, 0:RANK]
    arrived(brecv.at[pl.ds(0, NX - 1)], S_BANDS)
    band_out[...] = (band_model[0:BW] - total(brecv, NX))[:, 0:RANK]

    sent(rowg.at[pl.ds(0, NY - 1)], S_ROW)
    sent(bandg.at[pl.ds(0, NX - 1)], S_BAND)
    sent(bandx.at[pl.ds(0, NY - 1)], S_BANDX)
    sent(colg.at[0, pl.ds(0, NLZ - 1)], S_COL)
    sent(colg.at[0], S_COLC)
    for n in range(CHUNKS):
        sent(recv1.at[pl.ds(n * PER, PER)], S_R1 + n)
    sent(recv2.at[pl.ds(0, NLZ - 1)], S_R2)
    sent(recv3.at[pl.ds(0, NX - 1)], S_R3)
    sent(fg.at[pl.ds(0, NY - 1)], S_F1)
    sent(fx.at[pl.ds(0, NX - 1)], S_F2)
    sent(grecv.at[pl.ds(0, NX - 1)], S_GRAM)
    sent(gall.at[pl.ds(0, 3)], S_GRAMP)
    sent(rrecv.at[pl.ds(0, NY - 1)], S_ROWS)
    sent(brecv.at[pl.ds(0, NX - 1)], S_BANDS)


def hand_over(*refs):
    sems = refs[8]
    copies = [
        pltpu.make_async_copy(refs[k], refs[4 + k], sems.at[k]) for k in range(4)
    ]
    for copy in copies:
        copy.start()
    for copy in copies:
        copy.wait()


def shards(tensor, row_factor, column_factor, band_factor, time_factor):
    v = pltpu.VMEM
    shapes = tuple(jax.ShapeDtypeStruct((n, RANK), F32) for n in (RW, CW, BW, FRAMES))
    factors = (row_factor, column_factor, band_factor, time_factor)
    factors = [pltpu.with_memory_space_constraint(x.T, pltpu.HBM) for x in factors]
    out = pl.pallas_call(
        kernel,
        out_shape=shapes,
        in_specs=[pl.BlockSpec(memory_space=pl.ANY)] + [pl.BlockSpec(memory_space=pltpu.HBM)] * 4,
        out_specs=[pl.BlockSpec(memory_space=v)] * 4,
        scratch_shapes=[
            v((MSG + 16, LANES), F32),
            v((RW, RANK), F32),
            v((CW, RANK), F32),
            v((BW, RANK), F32),
            v((FRAMES, RANK), F32),
            v((TB, ROWS, COLS), BF16),
            v((RW, LANES), F32),
            v((BW, LANES), F32),
            v((NY, RW, LANES), F32),
            v((NX, BW, LANES), F32),
            v((NY, BW, LANES), F32),
            v((ROWS, LANES), F32),
            v((BANDS, LANES), F32),
            v((NY * BW, LANES), F32),
            v((LANES, LANES), F32),
            v((COLS, TB * ROWS), BF16),
            v((FRAMES, HALF, 2 * LANES), BF16),
            v((FRAMES, COLS, LANES), F32),
            v((2, NLZ, PACK, LANES), F32),
            v((NLZ, PACK, LANES), F32),
            v((NLZ, PACK, LANES), F32),
            v((NLZ, PACK, LANES), F32),
            v((PACK, LANES), F32),
            v((NX, PACK, LANES), F32),
            v((2, NLZ, PACK, LANES), F32),
            v((COLS, LANES), F32),
            v((COLS, LANES), BF16),
            v((TB * QROWS, LANES), F32),
            v((4, TB, 8, LANES), F32),
            v((FRAMES, LANES), F32),
            v((NY, FRAMES, LANES), F32),
            v((FRAMES, LANES), F32),
            v((NX, FRAMES, LANES), F32),
            v((4, 2, 24, LANES), F32),
            v((NX, 2, 24, LANES), F32),
            v((4, 2, 24, LANES), F32),
            v((LANES, LANES), F32),
            v((NY, RW, LANES), F32),
            v((NY, RW, LANES), F32),
            v((NX, BW, LANES), F32),
            v((NX, BW, LANES), F32),
            pltpu.SemaphoreType.DMA((LOADS + 4,)),
            pltpu.SemaphoreType.DMA((N_SEMS,)),
            pltpu.SemaphoreType.DMA((N_SEMS,)),
        ],
        compiler_params=pltpu.CompilerParams(
            collective_id=0, has_side_effects=True, vmem_limit_bytes=48 * 1024 * 1024
        ),
        cost_estimate=pl.CostEstimate(
            flops=4 * RANK * TB * ROWS * COLS, bytes_accessed=2 * TB * ROWS * COLS, transcendentals=0
        ),
    )(
        tensor.reshape(TB, ROWS, COLS),
        *factors,
    )
    out = pl.pallas_call(
        hand_over,
        out_shape=shapes,
        in_specs=[pl.BlockSpec(memory_space=v)] * 4,
        out_specs=[pl.BlockSpec(memory_space=pl.ANY)] * 4,
        scratch_shapes=[pltpu.SemaphoreType.DMA((4,))],
    )(*[pltpu.with_memory_space_constraint(x, v) for x in out])
    return tuple(x.T for x in out)


def solution(mesh):
    return jax.shard_map(
        shards,
        mesh=mesh,
        in_specs=(
            P(None, "gy", "gx", None),
            P(None, ("gx", "gy")),
            P(None, "gy"),
            P(None, ("gy", "gx")),
            P(),
        ),
        out_specs=(P(None, ("gx", "gy")), P(None, "gy"), P(None, ("gy", "gx")), P()),
        check_vma=False,
    )
```

```python
import jax
import jax.numpy as jnp
from jax import lax
from jax.experimental import pallas as pl
from jax.experimental.pallas import tpu as pltpu
from jax.sharding import PartitionSpec as P

MESH = pl.DeviceIdType.MESH
HIGHEST = lax.Precision.HIGHEST
F32 = jnp.float32
BF16 = jnp.bfloat16

NX, NY, NLZ = 8, 32, 16
RANK, LANES = 96, 128
FRAMES, BANDS, ROWS, COLS = 2, 16, 128, 1024
RW, CW, BW = 4, 32, 2
PACK = CW * RANK // LANES
TB = FRAMES * BANDS
HALF = BANDS * ROWS
CHUNKS = 4
CHUNK = COLS // CHUNKS
PER = NLZ // CHUNKS
LOADS = 8
MSG = CW + 8
QROWS = ROWS // 4

(
    S_ROW, S_BAND, S_BANDX, S_COL, S_COLC, S_R1, S_R2, S_R3, S_F1, S_F2,
    S_GRAM, S_GRAMP, S_ROWS, S_BANDS,
) = [0, 1, 2, 3, 4, 5, 9, 10, 11, 12, 13, 14, 15, 16]
N_SEMS = 17


def dot(x, y):
    return jnp.dot(x, y, preferred_element_type=F32)


def exact(x, y):
    return jnp.dot(x, y, precision=HIGHEST, preferred_element_type=F32)


def total(ref, count):
    out = ref[0]
    for k in range(1, count):
        out = out + ref[k]
    return out


def wrap(index, size):
    return jnp.where(index >= size, index - size, index)


def lane_of(x):
    return lax.broadcasted_iota(jnp.int32, x.shape, 1)


def pack(tiles):
    spare = lane_of(tiles[3]) >= RANK
    return [
        jnp.where(spare, pltpu.roll(tiles[3], RANK - 32 * m, 1), tiles[m]) for m in range(3)
    ]


def unpack(tiles):
    lane = lane_of(tiles[0])
    last = jnp.zeros_like(tiles[0])
    for m in (2, 1, 0):
        last = jnp.where(lane < 32 * m + 32, pltpu.roll(tiles[m], 32 * m + 32, 1), last)
    zero = jnp.zeros_like(last)
    return [jnp.where(lane < RANK, tile, zero) for tile in tiles] + [
        jnp.where(lane < RANK, last, zero)
    ]


def kernel(
    tensor, row_in, col_in, band_in, time_in,
    row_out, col_out, band_out, time_out,
    packed, row_v, col_v, band_v, time_v,
    data, mine4, mine2, rowg, bandg, bandx, row_t, band_t, bandx_t, tb_t,
    turned, prod, by_frame, part, recv1, sum1, recv2, fin, recv3,
    colg, colf, low, folded, partials,
    fpart, fg, fsum, fx, gpart, grecv, gall, gcols,
    rsend, rrecv, bsend, brecv,
    local_sems, send_sems, recv_sems,
):
    a = lax.axis_index("gx")
    g = lax.axis_index("gy")
    lz = lax.div(g, 2)
    c = g - 2 * lz
    l = lax.div(lz, 8)
    z = lz - 8 * l
    p = l * 2 + c
    other = 1 - c
    partner = lz * 2 + other
    def gy_peers(act):
        pl.loop(1, NY)(lambda k: act((a, wrap(g + k, NY))))

    def gx_peers(act):
        pl.loop(1, NX)(lambda k: act((wrap(a + k, NX), g)))

    def core_peers(act):
        pl.loop(1, NLZ)(lambda k: act((a, wrap(lz + k, NLZ) * 2 + c)))

    def send(src, dst, sem, device):
        pltpu.make_async_remote_copy(
            src_ref=src, dst_ref=dst, send_sem=send_sems.at[sem], recv_sem=recv_sems.at[sem],
            device_id=device, device_id_type=MESH,
        ).start()

    def arrived(ref, sem):
        pltpu.make_async_copy(ref, ref, recv_sems.at[sem]).wait()

    def sent(ref, sem):
        pltpu.make_async_copy(ref, ref, send_sems.at[sem]).wait()

    small = [
        pltpu.make_async_copy(src, dst, local_sems.at[LOADS + k])
        for k, (src, dst) in enumerate(
            [(row_in, row_v), (band_in, band_v), (col_in, col_v), (time_in, time_v)]
        )
    ]
    for copy in small:
        copy.start()

    barrier = pltpu.get_barrier_semaphore()
    def greet(to):
        pl.semaphore_signal(barrier, inc=1, device_id=to, device_id_type=MESH)

    gy_peers(greet)
    gx_peers(greet)

    for k in range(LOADS):
        span = pl.ds(k * (TB // LOADS), TB // LOADS)
        pltpu.make_async_copy(tensor.at[span], data.at[span], local_sems.at[k]).start()

    tb_t[...] = jnp.zeros_like(tb_t)
    packed[...] = jnp.zeros_like(packed)
    for copy in small:
        copy.wait()
    packed[0:CW, 0:RANK] = col_v[...]
    packed[CW : CW + BW, 0:RANK] = band_v[...]
    packed[MSG : MSG + RW, 0:RANK] = row_v[...]
    packed[MSG + 8 : MSG + 8 + FRAMES, 0:RANK] = time_v[...]
    mine2[...] = packed[CW : CW + BW]
    mine4[...] = packed[MSG : MSG + RW]
    time8 = packed[MSG + 8 :]
    rowg[g] = mine4[...]
    bandg[a] = mine2[...]
    bandx[g] = mine2[...]
    for m, tile in enumerate(pack([packed[8 * m : 8 * m + 8] for m in range(4)])):
        colg[c, lz, 8 * m : 8 * m + 8] = tile

    pl.semaphore_wait(barrier, NY - 1 + NX - 1)

    gy_peers(lambda to: send(mine4, rowg.at[g], S_ROW, to))
    gx_peers(lambda to: send(mine2, bandg.at[a], S_BAND, to))
    core_peers(lambda to: send(colg.at[c, lz], colg.at[c, lz], S_COL, to))

    @pl.loop(0, LOADS)
    def _(k):
        per = TB // LOADS
        span = pl.ds(k * per, per)
        pltpu.make_async_copy(tensor.at[span], data.at[span], local_sems.at[k]).wait()
        for i in range(per):
            at = pl.multiple_of((k * per + i) * ROWS, ROWS)
            turned[:, pl.ds(at, ROWS)] = data[k * per + i].T

    gy_peers(lambda to: send(mine2, bandx.at[g], S_BANDX, to))

    arrived(bandg.at[pl.ds(0, NX - 1)], S_BAND)
    for k in range(NX):
        band_t[BW * k : BW * k + BW] = bandg[k]
    for t in range(FRAMES):
        tb_t[t * BANDS : (t + 1) * BANDS] = time8[t : t + 1] * band_t[...]
    tb_t[TB : TB + BANDS] = band_t[...]
    arrived(rowg.at[pl.ds(0, NY - 1)], S_ROW)
    for k in range(NY):
        row_t[RW * k : RW * k + RW] = rowg[k]

    @pl.loop(0, BANDS)
    def _(k):
        span = pl.ds(pl.multiple_of(k * ROWS, ROWS), ROWS)
        rows = row_t[...]
        plain = (tb_t[pl.ds(TB + k, 1)] * rows).astype(BF16)
        for t in range(FRAMES):
            prod[t, span, 0:LANES] = (tb_t[pl.ds(t * BANDS + k, 1)] * rows).astype(BF16)
            prod[t, span, LANES:] = plain

    def send_pieces(n):
        arrived(recv1.at[pl.ds(0, 3), pl.ds(0, 2)], S_R1 + n)
        for i in range(2):
            k = 2 * n + i
            recv1[p, k] = part[p, k]
            sum1[k] = recv1[0, k] + recv1[1, k] + recv1[2, k] + recv1[3, k]

            @pl.when(k != z)
            def _():
                send(sum1.at[k], recv2.at[z], S_R2, (a, (l * 8 + k) * 2 + c))

            @pl.when(k == z)
            def _():
                recv2[z] = sum1[k]

    @pl.loop(0, CHUNKS)
    def _(n):
        heres = [
            pl.ds(pl.multiple_of(i * (COLS // 2) + n * (CHUNK // 2), CHUNK // 2), CHUNK // 2)
            for i in range(2)
        ]
        acc = jnp.zeros((CHUNK, LANES), F32)
        for t in range(FRAMES):
            both = dot(
                jnp.concatenate(
                    [turned[here, t * HALF : (t + 1) * HALF] for here in heres], axis=0
                ),
                prod[t],
            )
            for i, here in enumerate(heres):
                by_frame[t, here] = both[i * (CHUNK // 2) : (i + 1) * (CHUNK // 2), LANES:]
            acc = acc + both[:, 0:LANES]
        acc = acc.reshape(CHUNK // CW, 4, 8, LANES)
        tiles = pack([acc[:, m].reshape(CHUNK // 4, LANES) for m in range(4)])
        for k in range(CHUNK // CW):
            for m in range(3):
                at = (k // 4) * 2 + k % 2, 2 * n + (k // 2) % 2
                part[at[0], at[1], 8 * m : 8 * m + 8] = tiles[m][8 * k : 8 * k + 8]
        span = pl.ds(2 * n, 2)
        for k in range(1, 4):
            to = wrap(p + k, 4)
            to_l = lax.div(to, 2)
            send(
                part.at[to, span], recv1.at[p, span], S_R1 + n,
                (a, (to_l * 8 + z) * 2 + to - 2 * to_l),
            )

    gram = exact(row_t[...].T, row_t[...])
    for k in range(4):
        gpart[k, 0] = gram[24 * k : 24 * k + 24]

    @pl.loop(0, CHUNKS)
    def _(n):
        send_pieces(n)

    arrived(colg.at[0, pl.ds(0, NLZ - 1)], S_COL)
    send(colg.at[c], colg.at[c], S_COLC, (a, partner))
    arrived(bandx.at[pl.ds(0, NY - 1)], S_BANDX)
    for k in range(NY):
        bandx_t[BW * k : BW * k + BW] = bandx[k]
    gram = exact(bandx_t[...].T, bandx_t[...])
    for k in range(4):
        gpart[k, 1] = gram[24 * k : 24 * k + 24]
    grecv[a] = gpart[p]
    gx_peers(lambda to: send(gpart.at[p], grecv.at[a], S_GRAM, to))

    arrived(colg.at[0], S_COLC)
    for i in range(2):
        tiles = unpack(
            [colg[i, :, 8 * m : 8 * m + 8].reshape(8 * NLZ, LANES) for m in range(3)]
        )
        for k in range(NLZ):
            block = jnp.concatenate([tile[8 * k : 8 * k + 8] for tile in tiles], axis=0)
            at = (2 * k + i) * CW
            colf[at : at + CW] = block
            low[at : at + CW] = block.astype(BF16)

    for t in range(FRAMES):
        fpart[t : t + 1] = jnp.sum(
            by_frame[t] * low[...].astype(F32), axis=0, keepdims=True
        )
    fg[g] = fpart[...]
    gy_peers(lambda to: send(fpart, fg.at[g], S_F1, to))

    @pl.loop(0, 4)
    def _(q):
        half = QROWS // 2
        heres = [pl.ds(pl.multiple_of(i * (ROWS // 2) + q * half, half), half) for i in range(2)]
        block = jnp.concatenate([data[:, here, :] for here in heres], axis=1)
        folded[...] = dot(block.reshape(TB * QROWS, COLS), low[...])
        rows = jnp.zeros((QROWS, LANES), F32)
        row_here = jnp.concatenate([row_t[here] for here in heres], axis=0)
        for j in range(TB):
            block = folded[j * QROWS : (j + 1) * QROWS]
            rows = rows + block * tb_t[j : j + 1]
            block = block * row_here
            partials[q, j] = jnp.sum(block.reshape(QROWS // 8, 8, LANES), axis=0)
        owners = [(i // 4) * (NY // 2) + 4 * q + i % 4 for i in range(NY // 4)]
        for i, k in enumerate(owners):
            rsend[k] = rows[RW * i : RW * i + RW]
        for k in owners:

            @pl.when(k != g)
            def _():
                send(rsend.at[k], rrecv.at[g], S_ROWS, (a, k))

    sums = total(partials, 4)
    bands = jnp.zeros((BANDS, LANES), F32)
    for t in range(FRAMES):
        bands = bands + time8[t : t + 1] * jnp.sum(sums[t * BANDS : (t + 1) * BANDS], axis=1)
    for k in range(NX):
        bsend[k] = bands[BW * k : BW * k + BW]
    gx_peers(lambda to: send(bsend.at[to[0]], brecv.at[a], S_BANDS, to))
    brecv[a] = bsend[a]
    rrecv[g] = rsend[g]

    arrived(grecv.at[pl.ds(0, NX - 1)], S_GRAM)
    gall[p] = total(grecv, NX)
    for k in range(1, 4):
        to = wrap(p + k, 4)
        to_l = lax.div(to, 2)
        send(gall.at[p], gall.at[p], S_GRAMP, (a, (to_l * 8 + z) * 2 + to - 2 * to_l))
    arrived(recv2.at[pl.ds(0, 7)], S_R2)
    fin[...] = total(recv2, 8)
    recv3[a] = fin[...]
    gx_peers(lambda to: send(fin, recv3.at[a], S_R3, to))
    arrived(fg.at[pl.ds(0, NY - 1)], S_F1)
    fsum[...] = total(fg, NY)
    fx[a] = fsum[...]
    gx_peers(lambda to: send(fsum, fx.at[a], S_F2, to))

    gcols[...] = jnp.zeros_like(gcols)

    @pl.loop(0, 4)
    def _(i):
        block = colf[pl.ds(pl.multiple_of(i * 256, 256), 256)]
        gcols[...] += exact(block.T, block)

    gram_cols = gcols[...]
    arrived(gall.at[pl.ds(0, 3)], S_GRAMP)
    pad = jnp.zeros((LANES - RANK, LANES), F32)
    gram_rows, gram_bands = (
        jnp.concatenate([gall[:, i].reshape(RANK, LANES), pad], axis=0) for i in range(2)
    )
    time_n = jnp.concatenate([time8, jnp.zeros((LANES - 8, LANES), F32)], axis=0).T
    gram_time = time_n[:, 0:1] * time8[0:1] + time_n[:, 1:2] * time8[1:2]
    row_model = exact(packed[MSG : MSG + 8], gram_cols * gram_bands * gram_time)
    col_model = exact(packed[0:CW], gram_rows * gram_bands * gram_time)
    band_model = exact(packed[CW:MSG], gram_rows * gram_cols * gram_time)
    time_model = exact(time8, gram_rows * gram_cols * gram_bands)

    arrived(fx.at[pl.ds(0, NX - 1)], S_F2)
    time_out[...] = (time_model[0:FRAMES] - total(fx, NX))[:, 0:RANK]
    arrived(recv3.at[pl.ds(0, NX - 1)], S_R3)
    sums = total(recv3, NX)
    sums = jnp.concatenate(unpack([sums[8 * m : 8 * m + 8] for m in range(3)]), axis=0)
    col_out[...] = (col_model - sums)[:, 0:RANK]
    arrived(rrecv.at[pl.ds(0, NY - 1)], S_ROWS)
    row_out[...] = (row_model[0:RW] - total(rrecv, NY))[:, 0:RANK]
    arrived(brecv.at[pl.ds(0, NX - 1)], S_BANDS)
    band_out[...] = (band_model[0:BW] - total(brecv, NX))[:, 0:RANK]

    sent(rowg.at[pl.ds(0, NY - 1)], S_ROW)
    sent(bandg.at[pl.ds(0, NX - 1)], S_BAND)
    sent(bandx.at[pl.ds(0, NY - 1)], S_BANDX)
    sent(colg.at[0, pl.ds(0, NLZ - 1)], S_COL)
    sent(colg.at[0], S_COLC)
    for n in range(CHUNKS):
        sent(recv1.at[pl.ds(0, 3), pl.ds(0, 2)], S_R1 + n)
    sent(recv2.at[pl.ds(0, 7)], S_R2)
    sent(recv3.at[pl.ds(0, NX - 1)], S_R3)
    sent(fg.at[pl.ds(0, NY - 1)], S_F1)
    sent(fx.at[pl.ds(0, NX - 1)], S_F2)
    sent(grecv.at[pl.ds(0, NX - 1)], S_GRAM)
    sent(gall.at[pl.ds(0, 3)], S_GRAMP)
    sent(rrecv.at[pl.ds(0, NY - 1)], S_ROWS)
    sent(brecv.at[pl.ds(0, NX - 1)], S_BANDS)


def hand_over(*refs):
    sems = refs[8]
    copies = [
        pltpu.make_async_copy(refs[k], refs[4 + k], sems.at[k]) for k in range(4)
    ]
    for copy in copies:
        copy.start()
    for copy in copies:
        copy.wait()


def shards(tensor, row_factor, column_factor, band_factor, time_factor):
    v = pltpu.VMEM
    shapes = tuple(jax.ShapeDtypeStruct((n, RANK), F32) for n in (RW, CW, BW, FRAMES))
    factors = (row_factor, column_factor, band_factor, time_factor)
    factors = [pltpu.with_memory_space_constraint(x.T, pltpu.HBM) for x in factors]
    out = pl.pallas_call(
        kernel,
        out_shape=shapes,
        in_specs=[pl.BlockSpec(memory_space=pl.ANY)] + [pl.BlockSpec(memory_space=pltpu.HBM)] * 4,
        out_specs=[pl.BlockSpec(memory_space=v)] * 4,
        scratch_shapes=[
            v((MSG + 16, LANES), F32),
            v((RW, RANK), F32),
            v((CW, RANK), F32),
            v((BW, RANK), F32),
            v((FRAMES, RANK), F32),
            v((TB, ROWS, COLS), BF16),
            v((RW, LANES), F32),
            v((BW, LANES), F32),
            v((NY, RW, LANES), F32),
            v((NX, BW, LANES), F32),
            v((NY, BW, LANES), F32),
            v((ROWS, LANES), F32),
            v((BANDS, LANES), F32),
            v((NY * BW, LANES), F32),
            v((LANES, LANES), F32),
            v((COLS, TB * ROWS), BF16),
            v((FRAMES, HALF, 2 * LANES), BF16),
            v((FRAMES, COLS, LANES), F32),
            v((4, 8, PACK, LANES), F32),
            v((4, 8, PACK, LANES), F32),
            v((8, PACK, LANES), F32),
            v((8, PACK, LANES), F32),
            v((PACK, LANES), F32),
            v((NX, PACK, LANES), F32),
            v((2, NLZ, PACK, LANES), F32),
            v((COLS, LANES), F32),
            v((COLS, LANES), BF16),
            v((TB * QROWS, LANES), F32),
            v((4, TB, 8, LANES), F32),
            v((FRAMES, LANES), F32),
            v((NY, FRAMES, LANES), F32),
            v((FRAMES, LANES), F32),
            v((NX, FRAMES, LANES), F32),
            v((4, 2, 24, LANES), F32),
            v((NX, 2, 24, LANES), F32),
            v((4, 2, 24, LANES), F32),
            v((LANES, LANES), F32),
            v((NY, RW, LANES), F32),
            v((NY, RW, LANES), F32),
            v((NX, BW, LANES), F32),
            v((NX, BW, LANES), F32),
            pltpu.SemaphoreType.DMA((LOADS + 4,)),
            pltpu.SemaphoreType.DMA((N_SEMS,)),
            pltpu.SemaphoreType.DMA((N_SEMS,)),
        ],
        compiler_params=pltpu.CompilerParams(
            collective_id=0, has_side_effects=True, vmem_limit_bytes=48 * 1024 * 1024
        ),
        cost_estimate=pl.CostEstimate(
            flops=4 * RANK * TB * ROWS * COLS, bytes_accessed=2 * TB * ROWS * COLS, transcendentals=0
        ),
    )(
        tensor.reshape(TB, ROWS, COLS),
        *factors,
    )
    out = pl.pallas_call(
        hand_over,
        out_shape=shapes,
        in_specs=[pl.BlockSpec(memory_space=v)] * 4,
        out_specs=[pl.BlockSpec(memory_space=pl.ANY)] * 4,
        scratch_shapes=[pltpu.SemaphoreType.DMA((4,))],
    )(*[pltpu.with_memory_space_constraint(x, v) for x in out])
    return tuple(x.T for x in out)


def solution(mesh):
    return jax.shard_map(
        shards,
        mesh=mesh,
        in_specs=(
            P(None, "gy", "gx", None),
            P(None, ("gx", "gy")),
            P(None, "gy"),
            P(None, ("gy", "gx")),
            P(),
        ),
        out_specs=(P(None, ("gx", "gy")), P(None, "gy"), P(None, ("gy", "gx")), P()),
        check_vma=False,
    )
```

```python
import jax
import jax.numpy as jnp
from jax import lax
from jax.experimental import pallas as pl
from jax.experimental.pallas import tpu as pltpu
from jax.sharding import PartitionSpec as P

MESH = pl.DeviceIdType.MESH
F32 = jnp.float32
BF16 = jnp.bfloat16

NX, NY, NLZ = 8, 32, 16
RANK, LANES = 96, 128
FRAMES, BANDS, ROWS, COLS = 2, 16, 128, 1024
RW, CW, BW = 4, 32, 2
PACK = CW * RANK // LANES
TB = FRAMES * BANDS
HALF = BANDS * ROWS
CHUNKS = 4
CHUNK = COLS // CHUNKS
PER = NLZ // CHUNKS
LOADS = 8
MSG = CW + 8
QROWS = ROWS // 4

(
    S_ROW, S_BAND, S_BANDX, S_COL, S_COLC, S_R1, S_R2, S_R3, S_F1, S_F2,
    S_GRAM, S_GRAMP, S_ROWS, S_BANDS,
) = [0, 1, 2, 3, 4, 5, 9, 10, 11, 12, 13, 14, 15, 16]
N_SEMS = 17


def dot(x, y):
    return jnp.dot(x, y, preferred_element_type=F32)


def exact(x, y):
    x_high, y_high = x.astype(BF16), y.astype(BF16)
    x_low = (x - x_high.astype(F32)).astype(BF16)
    y_low = (y - y_high.astype(F32)).astype(BF16)
    return dot(x_high, y_high) + (dot(x_high, y_low) + dot(x_low, y_high))


def total(ref, count):
    out = ref[0]
    for k in range(1, count):
        out = out + ref[k]
    return out


def wrap(index, size):
    return jnp.where(index >= size, index - size, index)


def lane_of(x):
    return lax.broadcasted_iota(jnp.int32, x.shape, 1)


def pack(tiles):
    spare = lane_of(tiles[3]) >= RANK
    return [
        jnp.where(spare, pltpu.roll(tiles[3], RANK - 32 * m, 1), tiles[m]) for m in range(3)
    ]


def unpack(tiles):
    lane = lane_of(tiles[0])
    last = jnp.zeros_like(tiles[0])
    for m in (2, 1, 0):
        last = jnp.where(lane < 32 * m + 32, pltpu.roll(tiles[m], 32 * m + 32, 1), last)
    zero = jnp.zeros_like(last)
    return [jnp.where(lane < RANK, tile, zero) for tile in tiles] + [
        jnp.where(lane < RANK, last, zero)
    ]


def kernel(
    tensor, row_in, col_in, band_in, time_in,
    row_out, col_out, band_out, time_out,
    packed, row_v, col_v, band_v, time_v,
    data, mine4, mine2, rowg, bandg, bandx, row_t, band_t, bandx_t, tb_t,
    turned, prod, by_frame, part, recv1, sum1, recv2, fin, recv3,
    colg, colf, low, folded, partials,
    fpart, fg, fsum, fx, gpart, grecv, gall, gcols,
    rsend, rrecv, bsend, brecv,
    local_sems, send_sems, recv_sems,
):
    a = lax.axis_index("gx")
    g = lax.axis_index("gy")
    lz = lax.div(g, 2)
    c = g - 2 * lz
    l = lax.div(lz, 8)
    z = lz - 8 * l
    p = l * 2 + c
    other = 1 - c
    partner = lz * 2 + other
    gy_peers = [wrap(g + k, NY) for k in range(1, NY)]
    gx_peers = [wrap(a + k, NX) for k in range(1, NX)]
    core_peers = [wrap(lz + k, NLZ) * 2 + c for k in range(1, NLZ)]

    def send(src, dst, sem, device):
        pltpu.make_async_remote_copy(
            src_ref=src, dst_ref=dst, send_sem=send_sems.at[sem], recv_sem=recv_sems.at[sem],
            device_id=device, device_id_type=MESH,
        ).start()

    def arrived(ref, sem):
        pltpu.make_async_copy(ref, ref, recv_sems.at[sem]).wait()

    def sent(ref, sem):
        pltpu.make_async_copy(ref, ref, send_sems.at[sem]).wait()

    small = [
        pltpu.make_async_copy(src, dst, local_sems.at[LOADS + k])
        for k, (src, dst) in enumerate(
            [(row_in, row_v), (band_in, band_v), (col_in, col_v), (time_in, time_v)]
        )
    ]
    for copy in small:
        copy.start()

    barrier = pltpu.get_barrier_semaphore()
    for to in gy_peers:
        pl.semaphore_signal(barrier, inc=1, device_id=(a, to), device_id_type=MESH)
    for to in gx_peers:
        pl.semaphore_signal(barrier, inc=1, device_id=(to, g), device_id_type=MESH)

    for k in range(LOADS):
        span = pl.ds(k * (TB // LOADS), TB // LOADS)
        pltpu.make_async_copy(tensor.at[span], data.at[span], local_sems.at[k]).start()

    tb_t[...] = jnp.zeros_like(tb_t)
    packed[...] = jnp.zeros_like(packed)
    for copy in small:
        copy.wait()
    packed[0:CW, 0:RANK] = col_v[...]
    packed[CW : CW + BW, 0:RANK] = band_v[...]
    packed[MSG : MSG + RW, 0:RANK] = row_v[...]
    packed[MSG + 8 : MSG + 8 + FRAMES, 0:RANK] = time_v[...]
    mine2[...] = packed[CW : CW + BW]
    mine4[...] = packed[MSG : MSG + RW]
    time8 = packed[MSG + 8 :]
    rowg[g] = mine4[...]
    bandg[a] = mine2[...]
    bandx[g] = mine2[...]
    for m, tile in enumerate(pack([packed[8 * m : 8 * m + 8] for m in range(4)])):
        colg[c, lz, 8 * m : 8 * m + 8] = tile

    pl.semaphore_wait(barrier, NY - 1 + NX - 1)

    for to in gy_peers:
        send(mine4, rowg.at[g], S_ROW, (a, to))
    for to in gx_peers:
        send(mine2, bandg.at[a], S_BAND, (to, g))
    for to in core_peers:
        send(colg.at[c, lz], colg.at[c, lz], S_COL, (a, to))

    @pl.loop(0, LOADS)
    def _(k):
        per = TB // LOADS
        span = pl.ds(k * per, per)
        pltpu.make_async_copy(tensor.at[span], data.at[span], local_sems.at[k]).wait()
        for i in range(per):
            at = pl.multiple_of((k * per + i) * ROWS, ROWS)
            turned[:, pl.ds(at, ROWS)] = data[k * per + i].T

    for to in gy_peers:
        send(mine2, bandx.at[g], S_BANDX, (a, to))

    arrived(bandg.at[pl.ds(0, NX - 1)], S_BAND)
    for k in range(NX):
        band_t[BW * k : BW * k + BW] = bandg[k]
    for t in range(FRAMES):
        tb_t[t * BANDS : (t + 1) * BANDS] = time8[t : t + 1] * band_t[...]
    tb_t[TB : TB + BANDS] = band_t[...]
    arrived(rowg.at[pl.ds(0, NY - 1)], S_ROW)
    for k in range(NY):
        row_t[RW * k : RW * k + RW] = rowg[k]

    @pl.loop(0, BANDS)
    def _(k):
        span = pl.ds(pl.multiple_of(k * ROWS, ROWS), ROWS)
        rows = row_t[...]
        plain = (tb_t[pl.ds(TB + k, 1)] * rows).astype(BF16)
        for t in range(FRAMES):
            prod[t, span, 0:LANES] = (tb_t[pl.ds(t * BANDS + k, 1)] * rows).astype(BF16)
            prod[t, span, LANES:] = plain

    def slot_lz(n, i):
        return (i // 2) * (NLZ // 2) + 2 * n + i % 2

    def send_pieces(n):
        span = pl.ds(n * PER, PER)
        arrived(recv1.at[span], S_R1 + n)
        sum1[span] = part[c, span] + recv1[span]
        for i in range(PER):
            k = slot_lz(n, i)

            @pl.when(k != lz)
            def _():
                send(sum1.at[n * PER + i], recv2.at[lz], S_R2, (a, k * 2 + c))

            @pl.when(k == lz)
            def _():
                recv2[lz] = sum1[n * PER + i]

    @pl.loop(0, CHUNKS)
    def _(n):
        heres = [
            pl.ds(pl.multiple_of(i * (COLS // 2) + n * (CHUNK // 2), CHUNK // 2), CHUNK // 2)
            for i in range(2)
        ]
        acc = jnp.zeros((CHUNK, LANES), F32)
        for t in range(FRAMES):
            both = dot(
                jnp.concatenate(
                    [turned[here, t * HALF : (t + 1) * HALF] for here in heres], axis=0
                ),
                prod[t],
            )
            for i, here in enumerate(heres):
                by_frame[t, here] = both[i * (CHUNK // 2) : (i + 1) * (CHUNK // 2), LANES:]
            acc = acc + both[:, 0:LANES]
        acc = acc.reshape(CHUNK // CW, 4, 8, LANES)
        tiles = pack([acc[:, m].reshape(CHUNK // 4, LANES) for m in range(4)])
        for k in range(CHUNK // CW):
            for m in range(3):
                part[k % 2, n * PER + k // 2, 8 * m : 8 * m + 8] = tiles[m][8 * k : 8 * k + 8]
        span = pl.ds(n * PER, PER)
        send(part.at[other, span], recv1.at[span], S_R1 + n, (a, partner))

    gram = exact(row_t[...].T, row_t[...])
    for k in range(4):
        gpart[k, 0] = gram[24 * k : 24 * k + 24]
    arrived(colg.at[0, pl.ds(0, NLZ - 1)], S_COL)
    send(colg.at[c], colg.at[c], S_COLC, (a, partner))

    @pl.loop(0, CHUNKS)
    def _(n):
        send_pieces(n)

    arrived(bandx.at[pl.ds(0, NY - 1)], S_BANDX)
    for k in range(NY):
        bandx_t[BW * k : BW * k + BW] = bandx[k]
    gram = exact(bandx_t[...].T, bandx_t[...])
    for k in range(4):
        gpart[k, 1] = gram[24 * k : 24 * k + 24]
    grecv[a] = gpart[p]
    for to in gx_peers:
        send(gpart.at[p], grecv.at[a], S_GRAM, (to, g))

    arrived(colg.at[0], S_COLC)
    for i in range(2):
        tiles = unpack(
            [colg[i, :, 8 * m : 8 * m + 8].reshape(8 * NLZ, LANES) for m in range(3)]
        )
        for k in range(NLZ):
            block = jnp.concatenate([tile[8 * k : 8 * k + 8] for tile in tiles], axis=0)
            at = (2 * k + i) * CW
            colf[at : at + CW] = block
            low[at : at + CW] = block.astype(BF16)

    for t in range(FRAMES):
        fpart[t : t + 1] = jnp.sum(
            by_frame[t] * low[...].astype(F32), axis=0, keepdims=True
        )
    fg[g] = fpart[...]
    for to in gy_peers:
        send(fpart, fg.at[g], S_F1, (a, to))

    @pl.loop(0, 4)
    def _(q):
        half = QROWS // 2
        heres = [pl.ds(pl.multiple_of(i * (ROWS // 2) + q * half, half), half) for i in range(2)]
        block = jnp.concatenate([data[:, here, :] for here in heres], axis=1)
        folded[...] = dot(block.reshape(TB * QROWS, COLS), low[...])
        rows = jnp.zeros((QROWS, LANES), F32)
        row_here = jnp.concatenate([row_t[here] for here in heres], axis=0)
        for j in range(TB):
            block = folded[j * QROWS : (j + 1) * QROWS]
            rows = rows + block * tb_t[j : j + 1]
            block = block * row_here
            partials[q, j] = jnp.sum(block.reshape(QROWS // 8, 8, LANES), axis=0)
        owners = [(i // 4) * (NY // 2) + 4 * q + i % 4 for i in range(NY // 4)]
        for i, k in enumerate(owners):
            rsend[k] = rows[RW * i : RW * i + RW]
        for k in owners:

            @pl.when(k != g)
            def _():
                send(rsend.at[k], rrecv.at[g], S_ROWS, (a, k))

    sums = total(partials, 4)
    bands = jnp.zeros((BANDS, LANES), F32)
    for t in range(FRAMES):
        bands = bands + time8[t : t + 1] * jnp.sum(sums[t * BANDS : (t + 1) * BANDS], axis=1)
    for k in range(NX):
        bsend[k] = bands[BW * k : BW * k + BW]
    for k in range(1, NX):
        to = wrap(a + k, NX)
        send(bsend.at[to], brecv.at[a], S_BANDS, (to, g))
    brecv[a] = bsend[a]
    rrecv[g] = rsend[g]

    arrived(grecv.at[pl.ds(0, NX - 1)], S_GRAM)
    gall[p] = total(grecv, NX)
    for k in range(1, 4):
        to = wrap(p + k, 4)
        to_l = lax.div(to, 2)
        send(gall.at[p], gall.at[p], S_GRAMP, (a, (to_l * 8 + z) * 2 + to - 2 * to_l))
    gcols[...] = jnp.zeros_like(gcols)

    @pl.loop(0, 4)
    def _(i):
        block = colf[pl.ds(pl.multiple_of(i * 256, 256), 256)]
        gcols[...] += exact(block.T, block)

    arrived(recv2.at[pl.ds(0, NLZ - 1)], S_R2)
    fin[...] = total(recv2, NLZ)
    recv3[a] = fin[...]
    for to in gx_peers:
        send(fin, recv3.at[a], S_R3, (to, g))
    arrived(fg.at[pl.ds(0, NY - 1)], S_F1)
    fsum[...] = total(fg, NY)
    fx[a] = fsum[...]
    for to in gx_peers:
        send(fsum, fx.at[a], S_F2, (to, g))

    gram_cols = gcols[...]
    arrived(gall.at[pl.ds(0, 3)], S_GRAMP)
    pad = jnp.zeros((LANES - RANK, LANES), F32)
    gram_rows, gram_bands = (
        jnp.concatenate([gall[:, i].reshape(RANK, LANES), pad], axis=0) for i in range(2)
    )
    time_n = jnp.concatenate([time8, jnp.zeros((LANES - 8, LANES), F32)], axis=0).T
    gram_time = time_n[:, 0:1] * time8[0:1] + time_n[:, 1:2] * time8[1:2]
    row_model = exact(packed[MSG : MSG + 8], gram_cols * gram_bands * gram_time)
    col_model = exact(packed[0:CW], gram_rows * gram_bands * gram_time)
    band_model = exact(packed[CW:MSG], gram_rows * gram_cols * gram_time)
    time_model = exact(time8, gram_rows * gram_cols * gram_bands)

    arrived(fx.at[pl.ds(0, NX - 1)], S_F2)
    time_out[...] = (time_model[0:FRAMES] - total(fx, NX))[:, 0:RANK]
    arrived(recv3.at[pl.ds(0, NX - 1)], S_R3)
    sums = total(recv3, NX)
    sums = jnp.concatenate(unpack([sums[8 * m : 8 * m + 8] for m in range(3)]), axis=0)
    col_out[...] = (col_model - sums)[:, 0:RANK]
    arrived(rrecv.at[pl.ds(0, NY - 1)], S_ROWS)
    row_out[...] = (row_model[0:RW] - total(rrecv, NY))[:, 0:RANK]
    arrived(brecv.at[pl.ds(0, NX - 1)], S_BANDS)
    band_out[...] = (band_model[0:BW] - total(brecv, NX))[:, 0:RANK]

    sent(rowg.at[pl.ds(0, NY - 1)], S_ROW)
    sent(bandg.at[pl.ds(0, NX - 1)], S_BAND)
    sent(bandx.at[pl.ds(0, NY - 1)], S_BANDX)
    sent(colg.at[0, pl.ds(0, NLZ - 1)], S_COL)
    sent(colg.at[0], S_COLC)
    for n in range(CHUNKS):
        sent(recv1.at[pl.ds(n * PER, PER)], S_R1 + n)
    sent(recv2.at[pl.ds(0, NLZ - 1)], S_R2)
    sent(recv3.at[pl.ds(0, NX - 1)], S_R3)
    sent(fg.at[pl.ds(0, NY - 1)], S_F1)
    sent(fx.at[pl.ds(0, NX - 1)], S_F2)
    sent(grecv.at[pl.ds(0, NX - 1)], S_GRAM)
    sent(gall.at[pl.ds(0, 3)], S_GRAMP)
    sent(rrecv.at[pl.ds(0, NY - 1)], S_ROWS)
    sent(brecv.at[pl.ds(0, NX - 1)], S_BANDS)


def hand_over(*refs):
    sems = refs[8]
    copies = [
        pltpu.make_async_copy(refs[k], refs[4 + k], sems.at[k]) for k in range(4)
    ]
    for copy in copies:
        copy.start()
    for copy in copies:
        copy.wait()


def shards(tensor, row_factor, column_factor, band_factor, time_factor):
    v = pltpu.VMEM
    shapes = tuple(jax.ShapeDtypeStruct((n, RANK), F32) for n in (RW, CW, BW, FRAMES))
    factors = (row_factor, column_factor, band_factor, time_factor)
    factors = [pltpu.with_memory_space_constraint(x.T, pltpu.HBM) for x in factors]
    out = pl.pallas_call(
        kernel,
        out_shape=shapes,
        in_specs=[pl.BlockSpec(memory_space=pl.ANY)] + [pl.BlockSpec(memory_space=pltpu.HBM)] * 4,
        out_specs=[pl.BlockSpec(memory_space=v)] * 4,
        scratch_shapes=[
            v((MSG + 16, LANES), F32),
            v((RW, RANK), F32),
            v((CW, RANK), F32),
            v((BW, RANK), F32),
            v((FRAMES, RANK), F32),
            v((TB, ROWS, COLS), BF16),
            v((RW, LANES), F32),
            v((BW, LANES), F32),
            v((NY, RW, LANES), F32),
            v((NX, BW, LANES), F32),
            v((NY, BW, LANES), F32),
            v((ROWS, LANES), F32),
            v((BANDS, LANES), F32),
            v((NY * BW, LANES), F32),
            v((LANES, LANES), F32),
            v((COLS, TB * ROWS), BF16),
            v((FRAMES, HALF, 2 * LANES), BF16),
            v((FRAMES, COLS, LANES), F32),
            v((2, NLZ, PACK, LANES), F32),
            v((NLZ, PACK, LANES), F32),
            v((NLZ, PACK, LANES), F32),
            v((NLZ, PACK, LANES), F32),
            v((PACK, LANES), F32),
            v((NX, PACK, LANES), F32),
            v((2, NLZ, PACK, LANES), F32),
            v((COLS, LANES), F32),
            v((COLS, LANES), BF16),
            v((TB * QROWS, LANES), F32),
            v((4, TB, 8, LANES), F32),
            v((FRAMES, LANES), F32),
            v((NY, FRAMES, LANES), F32),
            v((FRAMES, LANES), F32),
            v((NX, FRAMES, LANES), F32),
            v((4, 2, 24, LANES), F32),
            v((NX, 2, 24, LANES), F32),
            v((4, 2, 24, LANES), F32),
            v((LANES, LANES), F32),
            v((NY, RW, LANES), F32),
            v((NY, RW, LANES), F32),
            v((NX, BW, LANES), F32),
            v((NX, BW, LANES), F32),
            pltpu.SemaphoreType.DMA((LOADS + 4,)),
            pltpu.SemaphoreType.DMA((N_SEMS,)),
            pltpu.SemaphoreType.DMA((N_SEMS,)),
        ],
        compiler_params=pltpu.CompilerParams(
            collective_id=0, has_side_effects=True, vmem_limit_bytes=48 * 1024 * 1024
        ),
        cost_estimate=pl.CostEstimate(
            flops=4 * RANK * TB * ROWS * COLS, bytes_accessed=2 * TB * ROWS * COLS, transcendentals=0
        ),
    )(
        tensor.reshape(TB, ROWS, COLS),
        *factors,
    )
    out = pl.pallas_call(
        hand_over,
        out_shape=shapes,
        in_specs=[pl.BlockSpec(memory_space=v)] * 4,
        out_specs=[pl.BlockSpec(memory_space=pl.ANY)] * 4,
        scratch_shapes=[pltpu.SemaphoreType.DMA((4,))],
    )(*[pltpu.with_memory_space_constraint(x, v) for x in out])
    return tuple(x.T for x in out)


def solution(mesh):
    return jax.shard_map(
        shards,
        mesh=mesh,
        in_specs=(
            P(None, "gy", "gx", None),
            P(None, ("gx", "gy")),
            P(None, "gy"),
            P(None, ("gy", "gx")),
            P(),
        ),
        out_specs=(P(None, ("gx", "gy")), P(None, "gy"), P(None, ("gy", "gx")), P()),
        check_vma=False,
    )
```

```python
import jax
import jax.numpy as jnp
from jax import lax
from jax.experimental import pallas as pl
from jax.experimental.pallas import tpu as pltpu
from jax.sharding import PartitionSpec as P

MESH = pl.DeviceIdType.MESH
F32 = jnp.float32
BF16 = jnp.bfloat16

NX, NY, NLZ = 8, 32, 16
RANK, LANES = 96, 128
FRAMES, BANDS, ROWS, COLS = 2, 16, 128, 1024
RW, CW, BW = 4, 32, 2
PACK = CW * RANK // LANES
TB = FRAMES * BANDS
HALF = BANDS * ROWS
CHUNKS = 4
CHUNK = COLS // CHUNKS
PER = NLZ // CHUNKS
LOADS = 8
MSG = CW + 8
QROWS = ROWS // 4

(
    S_ROW, S_BAND, S_BANDX, S_COL, S_COLC, S_R1, S_R2, S_R3, S_F1, S_F2,
    S_GRAM, S_GRAMP, S_ROWS, S_BANDS,
) = [0, 1, 2, 3, 4, 5, 9, 10, 11, 12, 13, 14, 15, 16]
N_SEMS = 17


def dot(x, y):
    return jnp.dot(x, y, preferred_element_type=F32)


def exact(x, y):
    x_high, y_high = x.astype(BF16), y.astype(BF16)
    x_low = (x - x_high.astype(F32)).astype(BF16)
    y_low = (y - y_high.astype(F32)).astype(BF16)
    return dot(x_high, y_high) + (dot(x_high, y_low) + dot(x_low, y_high))


def total(ref, count):
    out = ref[0]
    for k in range(1, count):
        out = out + ref[k]
    return out


def wrap(index, size):
    return jnp.where(index >= size, index - size, index)


def lane_of(x):
    return lax.broadcasted_iota(jnp.int32, x.shape, 1)


def pack(tiles):
    spare = lane_of(tiles[3]) >= RANK
    return [
        jnp.where(spare, pltpu.roll(tiles[3], RANK - 32 * m, 1), tiles[m]) for m in range(3)
    ]


def unpack(tiles):
    lane = lane_of(tiles[0])
    last = jnp.zeros_like(tiles[0])
    for m in (2, 1, 0):
        last = jnp.where(lane < 32 * m + 32, pltpu.roll(tiles[m], 32 * m + 32, 1), last)
    zero = jnp.zeros_like(last)
    return [jnp.where(lane < RANK, tile, zero) for tile in tiles] + [
        jnp.where(lane < RANK, last, zero)
    ]


def kernel(
    tensor, row_in, col_in, band_in, time_in,
    row_out, col_out, band_out, time_out,
    packed, row_v, col_v, band_v, time_v,
    data, mine4, mine2, rowg, bandg, bandx, row_t, band_t, bandx_t, tb_t,
    turned, prod, by_frame, part, recv1, sum1, recv2, fin, recv3,
    colg, colf, low, folded, partials,
    fpart, fg, fsum, fx, gpart, grecv, gall, gcols,
    rsend, rrecv, bsend, brecv,
    local_sems, send_sems, recv_sems,
):
    a = lax.axis_index("gx")
    g = lax.axis_index("gy")
    lz = lax.div(g, 2)
    c = g - 2 * lz
    l = lax.div(lz, 8)
    z = lz - 8 * l
    p = l * 2 + c
    other = 1 - c
    partner = lz * 2 + other
    gy_peers = [wrap(g + k, NY) for k in range(1, NY)]
    gx_peers = [wrap(a + k, NX) for k in range(1, NX)]
    core_peers = [wrap(lz + k, NLZ) * 2 + c for k in range(1, NLZ)]

    def send(src, dst, sem, device):
        pltpu.make_async_remote_copy(
            src_ref=src, dst_ref=dst, send_sem=send_sems.at[sem], recv_sem=recv_sems.at[sem],
            device_id=device, device_id_type=MESH,
        ).start()

    def arrived(ref, sem):
        pltpu.make_async_copy(ref, ref, recv_sems.at[sem]).wait()

    def sent(ref, sem):
        pltpu.make_async_copy(ref, ref, send_sems.at[sem]).wait()

    small = [
        pltpu.make_async_copy(src, dst, local_sems.at[LOADS + k])
        for k, (src, dst) in enumerate(
            [(row_in, row_v), (band_in, band_v), (col_in, col_v), (time_in, time_v)]
        )
    ]
    for copy in small:
        copy.start()

    barrier = pltpu.get_barrier_semaphore()
    for to in gy_peers:
        pl.semaphore_signal(barrier, inc=1, device_id=(a, to), device_id_type=MESH)
    for to in gx_peers:
        pl.semaphore_signal(barrier, inc=1, device_id=(to, g), device_id_type=MESH)

    for k in range(LOADS):
        span = pl.ds(k * (TB // LOADS), TB // LOADS)
        pltpu.make_async_copy(tensor.at[span], data.at[span], local_sems.at[k]).start()

    tb_t[...] = jnp.zeros_like(tb_t)
    packed[...] = jnp.zeros_like(packed)
    for copy in small:
        copy.wait()
    packed[0:CW, 0:RANK] = col_v[...]
    packed[CW : CW + BW, 0:RANK] = band_v[...]
    packed[MSG : MSG + RW, 0:RANK] = row_v[...]
    packed[MSG + 8 : MSG + 8 + FRAMES, 0:RANK] = time_v[...]
    mine2[...] = packed[CW : CW + BW]
    mine4[...] = packed[MSG : MSG + RW]
    time8 = packed[MSG + 8 :]
    rowg[g] = mine4[...]
    bandg[a] = mine2[...]
    bandx[g] = mine2[...]
    for m, tile in enumerate(pack([packed[8 * m : 8 * m + 8] for m in range(4)])):
        colg[c, lz, 8 * m : 8 * m + 8] = tile

    pl.semaphore_wait(barrier, NY - 1 + NX - 1)

    for to in gy_peers:
        send(mine4, rowg.at[g], S_ROW, (a, to))
    for to in gx_peers:
        send(mine2, bandg.at[a], S_BAND, (to, g))

    @pl.loop(0, LOADS)
    def _(k):
        per = TB // LOADS
        span = pl.ds(k * per, per)
        pltpu.make_async_copy(tensor.at[span], data.at[span], local_sems.at[k]).wait()
        for i in range(per):
            at = pl.multiple_of((k * per + i) * ROWS, ROWS)
            turned[:, pl.ds(at, ROWS)] = data[k * per + i].T

    for to in core_peers:
        send(colg.at[c, lz], colg.at[c, lz], S_COL, (a, to))
    for to in gy_peers:
        send(mine2, bandx.at[g], S_BANDX, (a, to))

    arrived(bandg.at[pl.ds(0, NX - 1)], S_BAND)
    for k in range(NX):
        band_t[BW * k : BW * k + BW] = bandg[k]
    for t in range(FRAMES):
        tb_t[t * BANDS : (t + 1) * BANDS] = time8[t : t + 1] * band_t[...]
    tb_t[TB : TB + BANDS] = band_t[...]
    arrived(rowg.at[pl.ds(0, NY - 1)], S_ROW)
    for k in range(NY):
        row_t[RW * k : RW * k + RW] = rowg[k]

    @pl.loop(0, BANDS)
    def _(k):
        span = pl.ds(pl.multiple_of(k * ROWS, ROWS), ROWS)
        rows = row_t[...]
        plain = (tb_t[pl.ds(TB + k, 1)] * rows).astype(BF16)
        for t in range(FRAMES):
            prod[t, span, 0:LANES] = (tb_t[pl.ds(t * BANDS + k, 1)] * rows).astype(BF16)
            prod[t, span, LANES:] = plain

    def slot_lz(n, i):
        return (i // 2) * (NLZ // 2) + 2 * n + i % 2

    def send_pieces(n):
        span = pl.ds(n * PER, PER)
        arrived(recv1.at[span], S_R1 + n)
        sum1[span] = part[c, span] + recv1[span]
        for i in range(PER):
            k = slot_lz(n, i)

            @pl.when(k != lz)
            def _():
                send(sum1.at[n * PER + i], recv2.at[lz], S_R2, (a, k * 2 + c))

            @pl.when(k == lz)
            def _():
                recv2[lz] = sum1[n * PER + i]

    @pl.loop(0, CHUNKS)
    def _(n):
        heres = [
            pl.ds(pl.multiple_of(i * (COLS // 2) + n * (CHUNK // 2), CHUNK // 2), CHUNK // 2)
            for i in range(2)
        ]
        acc = jnp.zeros((CHUNK, LANES), F32)
        for t in range(FRAMES):
            both = dot(
                jnp.concatenate(
                    [turned[here, t * HALF : (t + 1) * HALF] for here in heres], axis=0
                ),
                prod[t],
            )
            for i, here in enumerate(heres):
                by_frame[t, here] = both[i * (CHUNK // 2) : (i + 1) * (CHUNK // 2), LANES:]
            acc = acc + both[:, 0:LANES]
        acc = acc.reshape(CHUNK // CW, 4, 8, LANES)
        tiles = pack([acc[:, m].reshape(CHUNK // 4, LANES) for m in range(4)])
        for k in range(CHUNK // CW):
            for m in range(3):
                part[k % 2, n * PER + k // 2, 8 * m : 8 * m + 8] = tiles[m][8 * k : 8 * k + 8]
        span = pl.ds(n * PER, PER)
        send(part.at[other, span], recv1.at[span], S_R1 + n, (a, partner))

    gram = exact(row_t[...].T, row_t[...])
    for k in range(4):
        gpart[k, 0] = gram[24 * k : 24 * k + 24]
    arrived(colg.at[0, pl.ds(0, NLZ - 1)], S_COL)
    send(colg.at[c], colg.at[c], S_COLC, (a, partner))

    @pl.loop(0, CHUNKS)
    def _(n):
        send_pieces(n)

    arrived(bandx.at[pl.ds(0, NY - 1)], S_BANDX)
    for k in range(NY):
        bandx_t[BW * k : BW * k + BW] = bandx[k]
    gram = exact(bandx_t[...].T, bandx_t[...])
    for k in range(4):
        gpart[k, 1] = gram[24 * k : 24 * k + 24]
    grecv[a] = gpart[p]
    for to in gx_peers:
        send(gpart.at[p], grecv.at[a], S_GRAM, (to, g))

    arrived(colg.at[0], S_COLC)
    for i in range(2):
        tiles = unpack(
            [colg[i, :, 8 * m : 8 * m + 8].reshape(8 * NLZ, LANES) for m in range(3)]
        )
        for k in range(NLZ):
            block = jnp.concatenate([tile[8 * k : 8 * k + 8] for tile in tiles], axis=0)
            at = (2 * k + i) * CW
            colf[at : at + CW] = block
            low[at : at + CW] = block.astype(BF16)

    for t in range(FRAMES):
        fpart[t : t + 1] = jnp.sum(
            by_frame[t] * low[...].astype(F32), axis=0, keepdims=True
        )
    fg[g] = fpart[...]
    for to in gy_peers:
        send(fpart, fg.at[g], S_F1, (a, to))

    @pl.loop(0, 4)
    def _(q):
        half = QROWS // 2
        heres = [pl.ds(pl.multiple_of(i * (ROWS // 2) + q * half, half), half) for i in range(2)]
        block = jnp.concatenate([data[:, here, :] for here in heres], axis=1)
        folded[...] = dot(block.reshape(TB * QROWS, COLS), low[...])
        rows = jnp.zeros((QROWS, LANES), F32)
        row_here = jnp.concatenate([row_t[here] for here in heres], axis=0)
        for j in range(TB):
            block = folded[j * QROWS : (j + 1) * QROWS]
            rows = rows + block * tb_t[j : j + 1]
            block = block * row_here
            partials[q, j] = jnp.sum(block.reshape(QROWS // 8, 8, LANES), axis=0)
        owners = [(i // 4) * (NY // 2) + 4 * q + i % 4 for i in range(NY // 4)]
        for i, k in enumerate(owners):
            rsend[k] = rows[RW * i : RW * i + RW]
        for k in owners:

            @pl.when(k != g)
            def _():
                send(rsend.at[k], rrecv.at[g], S_ROWS, (a, k))

    sums = total(partials, 4)
    bands = jnp.zeros((BANDS, LANES), F32)
    for t in range(FRAMES):
        bands = bands + time8[t : t + 1] * jnp.sum(sums[t * BANDS : (t + 1) * BANDS], axis=1)
    for k in range(NX):
        bsend[k] = bands[BW * k : BW * k + BW]
    for k in range(1, NX):
        to = wrap(a + k, NX)
        send(bsend.at[to], brecv.at[a], S_BANDS, (to, g))
    brecv[a] = bsend[a]
    rrecv[g] = rsend[g]

    arrived(grecv.at[pl.ds(0, NX - 1)], S_GRAM)
    gall[p] = total(grecv, NX)
    for k in range(1, 4):
        to = wrap(p + k, 4)
        to_l = lax.div(to, 2)
        send(gall.at[p], gall.at[p], S_GRAMP, (a, (to_l * 8 + z) * 2 + to - 2 * to_l))
    gcols[...] = jnp.zeros_like(gcols)

    @pl.loop(0, 4)
    def _(i):
        block = colf[pl.ds(pl.multiple_of(i * 256, 256), 256)]
        gcols[...] += exact(block.T, block)

    arrived(recv2.at[pl.ds(0, NLZ - 1)], S_R2)
    fin[...] = total(recv2, NLZ)
    recv3[a] = fin[...]
    for to in gx_peers:
        send(fin, recv3.at[a], S_R3, (to, g))
    arrived(fg.at[pl.ds(0, NY - 1)], S_F1)
    fsum[...] = total(fg, NY)
    fx[a] = fsum[...]
    for to in gx_peers:
        send(fsum, fx.at[a], S_F2, (to, g))

    gram_cols = gcols[...]
    arrived(gall.at[pl.ds(0, 3)], S_GRAMP)
    pad = jnp.zeros((LANES - RANK, LANES), F32)
    gram_rows, gram_bands = (
        jnp.concatenate([gall[:, i].reshape(RANK, LANES), pad], axis=0) for i in range(2)
    )
    time_n = jnp.concatenate([time8, jnp.zeros((LANES - 8, LANES), F32)], axis=0).T
    gram_time = time_n[:, 0:1] * time8[0:1] + time_n[:, 1:2] * time8[1:2]
    row_model = exact(packed[MSG : MSG + 8], gram_cols * gram_bands * gram_time)
    col_model = exact(packed[0:CW], gram_rows * gram_bands * gram_time)
    band_model = exact(packed[CW:MSG], gram_rows * gram_cols * gram_time)
    time_model = exact(time8, gram_rows * gram_cols * gram_bands)

    arrived(fx.at[pl.ds(0, NX - 1)], S_F2)
    time_out[...] = (time_model[0:FRAMES] - total(fx, NX))[:, 0:RANK]
    arrived(recv3.at[pl.ds(0, NX - 1)], S_R3)
    sums = total(recv3, NX)
    sums = jnp.concatenate(unpack([sums[8 * m : 8 * m + 8] for m in range(3)]), axis=0)
    col_out[...] = (col_model - sums)[:, 0:RANK]
    arrived(rrecv.at[pl.ds(0, NY - 1)], S_ROWS)
    row_out[...] = (row_model[0:RW] - total(rrecv, NY))[:, 0:RANK]
    arrived(brecv.at[pl.ds(0, NX - 1)], S_BANDS)
    band_out[...] = (band_model[0:BW] - total(brecv, NX))[:, 0:RANK]

    sent(rowg.at[pl.ds(0, NY - 1)], S_ROW)
    sent(bandg.at[pl.ds(0, NX - 1)], S_BAND)
    sent(bandx.at[pl.ds(0, NY - 1)], S_BANDX)
    sent(colg.at[0, pl.ds(0, NLZ - 1)], S_COL)
    sent(colg.at[0], S_COLC)
    for n in range(CHUNKS):
        sent(recv1.at[pl.ds(n * PER, PER)], S_R1 + n)
    sent(recv2.at[pl.ds(0, NLZ - 1)], S_R2)
    sent(recv3.at[pl.ds(0, NX - 1)], S_R3)
    sent(fg.at[pl.ds(0, NY - 1)], S_F1)
    sent(fx.at[pl.ds(0, NX - 1)], S_F2)
    sent(grecv.at[pl.ds(0, NX - 1)], S_GRAM)
    sent(gall.at[pl.ds(0, 3)], S_GRAMP)
    sent(rrecv.at[pl.ds(0, NY - 1)], S_ROWS)
    sent(brecv.at[pl.ds(0, NX - 1)], S_BANDS)


def hand_over(*refs):
    sems = refs[8]
    copies = [
        pltpu.make_async_copy(refs[k], refs[4 + k], sems.at[k]) for k in range(4)
    ]
    for copy in copies:
        copy.start()
    for copy in copies:
        copy.wait()


def shards(tensor, row_factor, column_factor, band_factor, time_factor):
    v = pltpu.VMEM
    shapes = tuple(jax.ShapeDtypeStruct((n, RANK), F32) for n in (RW, CW, BW, FRAMES))
    factors = (row_factor, column_factor, band_factor, time_factor)
    factors = [pltpu.with_memory_space_constraint(x.T, pltpu.HBM) for x in factors]
    out = pl.pallas_call(
        kernel,
        out_shape=shapes,
        in_specs=[pl.BlockSpec(memory_space=pl.ANY)] + [pl.BlockSpec(memory_space=pltpu.HBM)] * 4,
        out_specs=[pl.BlockSpec(memory_space=v)] * 4,
        scratch_shapes=[
            v((MSG + 16, LANES), F32),
            v((RW, RANK), F32),
            v((CW, RANK), F32),
            v((BW, RANK), F32),
            v((FRAMES, RANK), F32),
            v((TB, ROWS, COLS), BF16),
            v((RW, LANES), F32),
            v((BW, LANES), F32),
            v((NY, RW, LANES), F32),
            v((NX, BW, LANES), F32),
            v((NY, BW, LANES), F32),
            v((ROWS, LANES), F32),
            v((BANDS, LANES), F32),
            v((NY * BW, LANES), F32),
            v((LANES, LANES), F32),
            v((COLS, TB * ROWS), BF16),
            v((FRAMES, HALF, 2 * LANES), BF16),
            v((FRAMES, COLS, LANES), F32),
            v((2, NLZ, PACK, LANES), F32),
            v((NLZ, PACK, LANES), F32),
            v((NLZ, PACK, LANES), F32),
            v((NLZ, PACK, LANES), F32),
            v((PACK, LANES), F32),
            v((NX, PACK, LANES), F32),
            v((2, NLZ, PACK, LANES), F32),
            v((COLS, LANES), F32),
            v((COLS, LANES), BF16),
            v((TB * QROWS, LANES), F32),
            v((4, TB, 8, LANES), F32),
            v((FRAMES, LANES), F32),
            v((NY, FRAMES, LANES), F32),
            v((FRAMES, LANES), F32),
            v((NX, FRAMES, LANES), F32),
            v((4, 2, 24, LANES), F32),
            v((NX, 2, 24, LANES), F32),
            v((4, 2, 24, LANES), F32),
            v((LANES, LANES), F32),
            v((NY, RW, LANES), F32),
            v((NY, RW, LANES), F32),
            v((NX, BW, LANES), F32),
            v((NX, BW, LANES), F32),
            pltpu.SemaphoreType.DMA((LOADS + 4,)),
            pltpu.SemaphoreType.DMA((N_SEMS,)),
            pltpu.SemaphoreType.DMA((N_SEMS,)),
        ],
        compiler_params=pltpu.CompilerParams(
            collective_id=0, has_side_effects=True, vmem_limit_bytes=48 * 1024 * 1024
        ),
        cost_estimate=pl.CostEstimate(
            flops=4 * RANK * TB * ROWS * COLS, bytes_accessed=2 * TB * ROWS * COLS, transcendentals=0
        ),
    )(
        tensor.reshape(TB, ROWS, COLS),
        *factors,
    )
    out = pl.pallas_call(
        hand_over,
        out_shape=shapes,
        in_specs=[pl.BlockSpec(memory_space=v)] * 4,
        out_specs=[pl.BlockSpec(memory_space=pl.ANY)] * 4,
        scratch_shapes=[pltpu.SemaphoreType.DMA((4,))],
    )(*[pltpu.with_memory_space_constraint(x, v) for x in out])
    return tuple(x.T for x in out)


def solution(mesh):
    return jax.shard_map(
        shards,
        mesh=mesh,
        in_specs=(
            P(None, "gy", "gx", None),
            P(None, ("gx", "gy")),
            P(None, "gy"),
            P(None, ("gy", "gx")),
            P(),
        ),
        out_specs=(P(None, ("gx", "gy")), P(None, "gy"), P(None, ("gy", "gx")), P()),
        check_vma=False,
    )
```

```python
import jax
import jax.numpy as jnp
from jax import lax
from jax.experimental import pallas as pl
from jax.experimental.pallas import tpu as pltpu
from jax.sharding import PartitionSpec as P

MESH = pl.DeviceIdType.MESH
F32 = jnp.float32
BF16 = jnp.bfloat16

NX, NY, NLZ = 8, 32, 16
RANK, LANES = 96, 128
FRAMES, BANDS, ROWS, COLS = 2, 16, 128, 1024
RW, CW, BW = 4, 32, 2
PACK = CW * RANK // LANES
TB = FRAMES * BANDS
HALF = BANDS * ROWS
CHUNKS = 4
CHUNK = COLS // CHUNKS
PER = NLZ // CHUNKS
LOADS = 8
MSG = CW + 8
QROWS = ROWS // 4

(
    S_ROW, S_BAND, S_BANDX, S_COL, S_COLC, S_R1, S_R2, S_R3, S_F1, S_F2,
    S_GRAM, S_GRAMP, S_ROWS, S_BANDS,
) = [0, 1, 2, 3, 4, 5, 9, 10, 11, 12, 13, 14, 15, 16]
N_SEMS = 17


def dot(x, y):
    return jnp.dot(x, y, preferred_element_type=F32)


def exact(x, y):
    x_high, y_high = x.astype(BF16), y.astype(BF16)
    x_low = (x - x_high.astype(F32)).astype(BF16)
    y_low = (y - y_high.astype(F32)).astype(BF16)
    return dot(x_high, y_high) + (dot(x_high, y_low) + dot(x_low, y_high))


def total(ref, count):
    out = ref[0]
    for k in range(1, count):
        out = out + ref[k]
    return out


def wrap(index, size):
    return jnp.where(index >= size, index - size, index)


def lane_of(x):
    return lax.broadcasted_iota(jnp.int32, x.shape, 1)


def pack(tiles):
    spare = lane_of(tiles[3]) >= RANK
    return [
        jnp.where(spare, pltpu.roll(tiles[3], RANK - 32 * m, 1), tiles[m]) for m in range(3)
    ]


def unpack(tiles):
    lane = lane_of(tiles[0])
    last = jnp.zeros_like(tiles[0])
    for m in (2, 1, 0):
        last = jnp.where(lane < 32 * m + 32, pltpu.roll(tiles[m], 32 * m + 32, 1), last)
    zero = jnp.zeros_like(last)
    return [jnp.where(lane < RANK, tile, zero) for tile in tiles] + [
        jnp.where(lane < RANK, last, zero)
    ]


def kernel(
    tensor, row_in, col_in, band_in, time_in,
    row_out, col_out, band_out, time_out,
    packed, row_v, col_v, band_v, time_v,
    data, mine4, mine2, rowg, bandg, bandx, row_t, band_t, bandx_t, tb_t,
    turned, prod, by_frame, part, recv1, sum1, recv2, fin, recv3,
    colg, colf, low, folded, partials,
    fpart, fg, fsum, fx, gpart, grecv, gall, gcols,
    rsend, rrecv, bsend, brecv,
    local_sems, send_sems, recv_sems,
):
    a = lax.axis_index("gx")
    g = lax.axis_index("gy")
    lz = lax.div(g, 2)
    c = g - 2 * lz
    l = lax.div(lz, 8)
    z = lz - 8 * l
    p = l * 2 + c
    other = 1 - c
    partner = lz * 2 + other
    gx_peers = [wrap(a + k, NX) for k in range(1, NX)]
    lz_order = [lane + wrap(z + k, 8) for k in (4, 3, 5, 2, 6, 1, 7, 0) for lane in (8 * l, 8 - 8 * l)]
    del lz_order[-2]
    core_peers = [to * 2 + c for to in lz_order]
    gy_peers = [to * 2 + core for to in lz_order for core in (c, other)] + [partner]

    def send(src, dst, sem, device):
        pltpu.make_async_remote_copy(
            src_ref=src, dst_ref=dst, send_sem=send_sems.at[sem], recv_sem=recv_sems.at[sem],
            device_id=device, device_id_type=MESH,
        ).start()

    def arrived(ref, sem):
        pltpu.make_async_copy(ref, ref, recv_sems.at[sem]).wait()

    def sent(ref, sem):
        pltpu.make_async_copy(ref, ref, send_sems.at[sem]).wait()

    small = [
        pltpu.make_async_copy(src, dst, local_sems.at[LOADS + k])
        for k, (src, dst) in enumerate(
            [(row_in, row_v), (band_in, band_v), (col_in, col_v), (time_in, time_v)]
        )
    ]
    for copy in small:
        copy.start()

    barrier = pltpu.get_barrier_semaphore()
    for to in gy_peers:
        pl.semaphore_signal(barrier, inc=1, device_id=(a, to), device_id_type=MESH)
    for to in gx_peers:
        pl.semaphore_signal(barrier, inc=1, device_id=(to, g), device_id_type=MESH)

    for k in range(LOADS):
        span = pl.ds(k * (TB // LOADS), TB // LOADS)
        pltpu.make_async_copy(tensor.at[span], data.at[span], local_sems.at[k]).start()

    tb_t[...] = jnp.zeros_like(tb_t)
    packed[...] = jnp.zeros_like(packed)
    for copy in small:
        copy.wait()
    packed[0:CW, 0:RANK] = col_v[...]
    packed[CW : CW + BW, 0:RANK] = band_v[...]
    packed[MSG : MSG + RW, 0:RANK] = row_v[...]
    packed[MSG + 8 : MSG + 8 + FRAMES, 0:RANK] = time_v[...]
    mine2[...] = packed[CW : CW + BW]
    mine4[...] = packed[MSG : MSG + RW]
    time8 = packed[MSG + 8 :]
    rowg[g] = mine4[...]
    bandg[a] = mine2[...]
    bandx[g] = mine2[...]
    for m, tile in enumerate(pack([packed[8 * m : 8 * m + 8] for m in range(4)])):
        colg[c, lz, 8 * m : 8 * m + 8] = tile

    pl.semaphore_wait(barrier, NY - 1 + NX - 1)

    for to in gy_peers:
        send(mine4, rowg.at[g], S_ROW, (a, to))
    for to in gx_peers:
        send(mine2, bandg.at[a], S_BAND, (to, g))
    for to in core_peers:
        send(colg.at[c, lz], colg.at[c, lz], S_COL, (a, to))

    @pl.loop(0, LOADS)
    def _(k):
        per = TB // LOADS
        span = pl.ds(k * per, per)
        pltpu.make_async_copy(tensor.at[span], data.at[span], local_sems.at[k]).wait()
        for i in range(per):
            at = pl.multiple_of((k * per + i) * ROWS, ROWS)
            turned[:, pl.ds(at, ROWS)] = data[k * per + i].T

    for to in gy_peers:
        send(mine2, bandx.at[g], S_BANDX, (a, to))

    arrived(bandg.at[pl.ds(0, NX - 1)], S_BAND)
    for k in range(NX):
        band_t[BW * k : BW * k + BW] = bandg[k]
    for t in range(FRAMES):
        tb_t[t * BANDS : (t + 1) * BANDS] = time8[t : t + 1] * band_t[...]
    tb_t[TB : TB + BANDS] = band_t[...]
    arrived(rowg.at[pl.ds(0, NY - 1)], S_ROW)
    for k in range(NY):
        row_t[RW * k : RW * k + RW] = rowg[k]

    @pl.loop(0, BANDS)
    def _(k):
        span = pl.ds(pl.multiple_of(k * ROWS, ROWS), ROWS)
        rows = row_t[...]
        plain = (tb_t[pl.ds(TB + k, 1)] * rows).astype(BF16)
        for t in range(FRAMES):
            prod[t, span, 0:LANES] = (tb_t[pl.ds(t * BANDS + k, 1)] * rows).astype(BF16)
            prod[t, span, LANES:] = plain

    def slot_lz(n, i):
        return (i // 2) * (NLZ // 2) + 2 * n + i % 2

    def send_pieces(n):
        span = pl.ds(n * PER, PER)
        arrived(recv1.at[span], S_R1 + n)
        sum1[span] = part[c, span] + recv1[span]
        for i in range(PER):
            k = slot_lz(n, i)

            @pl.when(k != lz)
            def _():
                send(sum1.at[n * PER + i], recv2.at[lz], S_R2, (a, k * 2 + c))

            @pl.when(k == lz)
            def _():
                recv2[lz] = sum1[n * PER + i]

    @pl.loop(0, CHUNKS)
    def _(n):
        heres = [
            pl.ds(pl.multiple_of(i * (COLS // 2) + n * (CHUNK // 2), CHUNK // 2), CHUNK // 2)
            for i in range(2)
        ]
        acc = jnp.zeros((CHUNK, LANES), F32)
        for t in range(FRAMES):
            both = dot(
                jnp.concatenate(
                    [turned[here, t * HALF : (t + 1) * HALF] for here in heres], axis=0
                ),
                prod[t],
            )
            for i, here in enumerate(heres):
                by_frame[t, here] = both[i * (CHUNK // 2) : (i + 1) * (CHUNK // 2), LANES:]
            acc = acc + both[:, 0:LANES]
        acc = acc.reshape(CHUNK // CW, 4, 8, LANES)
        tiles = pack([acc[:, m].reshape(CHUNK // 4, LANES) for m in range(4)])
        for k in range(CHUNK // CW):
            for m in range(3):
                part[k % 2, n * PER + k // 2, 8 * m : 8 * m + 8] = tiles[m][8 * k : 8 * k + 8]
        span = pl.ds(n * PER, PER)
        send(part.at[other, span], recv1.at[span], S_R1 + n, (a, partner))

    gram = exact(row_t[...].T, row_t[...])
    for k in range(4):
        gpart[k, 0] = gram[24 * k : 24 * k + 24]
    arrived(colg.at[0, pl.ds(0, NLZ - 1)], S_COL)
    send(colg.at[c], colg.at[c], S_COLC, (a, partner))

    @pl.loop(0, CHUNKS)
    def _(n):
        send_pieces(n)

    arrived(bandx.at[pl.ds(0, NY - 1)], S_BANDX)
    for k in range(NY):
        bandx_t[BW * k : BW * k + BW] = bandx[k]
    gram = exact(bandx_t[...].T, bandx_t[...])
    for k in range(4):
        gpart[k, 1] = gram[24 * k : 24 * k + 24]
    grecv[a] = gpart[p]
    for to in gx_peers:
        send(gpart.at[p], grecv.at[a], S_GRAM, (to, g))

    arrived(colg.at[0], S_COLC)
    for i in range(2):
        tiles = unpack(
            [colg[i, :, 8 * m : 8 * m + 8].reshape(8 * NLZ, LANES) for m in range(3)]
        )
        for k in range(NLZ):
            block = jnp.concatenate([tile[8 * k : 8 * k + 8] for tile in tiles], axis=0)
            at = (2 * k + i) * CW
            colf[at : at + CW] = block
            low[at : at + CW] = block.astype(BF16)

    for t in range(FRAMES):
        fpart[t : t + 1] = jnp.sum(
            by_frame[t] * low[...].astype(F32), axis=0, keepdims=True
        )
    fg[g] = fpart[...]
    for to in gy_peers:
        send(fpart, fg.at[g], S_F1, (a, to))

    @pl.loop(0, 4)
    def _(q):
        half = QROWS // 2
        heres = [pl.ds(pl.multiple_of(i * (ROWS // 2) + q * half, half), half) for i in range(2)]
        block = jnp.concatenate([data[:, here, :] for here in heres], axis=1)
        folded[...] = dot(block.reshape(TB * QROWS, COLS), low[...])
        rows = jnp.zeros((QROWS, LANES), F32)
        row_here = jnp.concatenate([row_t[here] for here in heres], axis=0)
        for j in range(TB):
            block = folded[j * QROWS : (j + 1) * QROWS]
            rows = rows + block * tb_t[j : j + 1]
            block = block * row_here
            partials[q, j] = jnp.sum(block.reshape(QROWS // 8, 8, LANES), axis=0)
        owners = [(i // 4) * (NY // 2) + 4 * q + i % 4 for i in range(NY // 4)]
        for i, k in enumerate(owners):
            rsend[k] = rows[RW * i : RW * i + RW]
        for k in owners:

            @pl.when(k != g)
            def _():
                send(rsend.at[k], rrecv.at[g], S_ROWS, (a, k))

    sums = total(partials, 4)
    bands = jnp.zeros((BANDS, LANES), F32)
    for t in range(FRAMES):
        bands = bands + time8[t : t + 1] * jnp.sum(sums[t * BANDS : (t + 1) * BANDS], axis=1)
    for k in range(NX):
        bsend[k] = bands[BW * k : BW * k + BW]
    for k in range(1, NX):
        to = wrap(a + k, NX)
        send(bsend.at[to], brecv.at[a], S_BANDS, (to, g))
    brecv[a] = bsend[a]
    rrecv[g] = rsend[g]

    arrived(grecv.at[pl.ds(0, NX - 1)], S_GRAM)
    gall[p] = total(grecv, NX)
    for k in range(1, 4):
        to = wrap(p + k, 4)
        to_l = lax.div(to, 2)
        send(gall.at[p], gall.at[p], S_GRAMP, (a, (to_l * 8 + z) * 2 + to - 2 * to_l))
    gcols[...] = jnp.zeros_like(gcols)

    @pl.loop(0, 4)
    def _(i):
        block = colf[pl.ds(pl.multiple_of(i * 256, 256), 256)]
        gcols[...] += exact(block.T, block)

    arrived(recv2.at[pl.ds(0, NLZ - 1)], S_R2)
    fin[...] = total(recv2, NLZ)
    recv3[a] = fin[...]
    for to in gx_peers:
        send(fin, recv3.at[a], S_R3, (to, g))
    arrived(fg.at[pl.ds(0, NY - 1)], S_F1)
    fsum[...] = total(fg, NY)
    fx[a] = fsum[...]
    for to in gx_peers:
        send(fsum, fx.at[a], S_F2, (to, g))

    gram_cols = gcols[...]
    arrived(gall.at[pl.ds(0, 3)], S_GRAMP)
    pad = jnp.zeros((LANES - RANK, LANES), F32)
    gram_rows, gram_bands = (
        jnp.concatenate([gall[:, i].reshape(RANK, LANES), pad], axis=0) for i in range(2)
    )
    time_n = jnp.concatenate([time8, jnp.zeros((LANES - 8, LANES), F32)], axis=0).T
    gram_time = time_n[:, 0:1] * time8[0:1] + time_n[:, 1:2] * time8[1:2]
    row_model = exact(packed[MSG : MSG + 8], gram_cols * gram_bands * gram_time)
    col_model = exact(packed[0:CW], gram_rows * gram_bands * gram_time)
    band_model = exact(packed[CW:MSG], gram_rows * gram_cols * gram_time)
    time_model = exact(time8, gram_rows * gram_cols * gram_bands)

    arrived(fx.at[pl.ds(0, NX - 1)], S_F2)
    time_out[...] = (time_model[0:FRAMES] - total(fx, NX))[:, 0:RANK]
    arrived(recv3.at[pl.ds(0, NX - 1)], S_R3)
    sums = total(recv3, NX)
    sums = jnp.concatenate(unpack([sums[8 * m : 8 * m + 8] for m in range(3)]), axis=0)
    col_out[...] = (col_model - sums)[:, 0:RANK]
    arrived(rrecv.at[pl.ds(0, NY - 1)], S_ROWS)
    row_out[...] = (row_model[0:RW] - total(rrecv, NY))[:, 0:RANK]
    arrived(brecv.at[pl.ds(0, NX - 1)], S_BANDS)
    band_out[...] = (band_model[0:BW] - total(brecv, NX))[:, 0:RANK]

    sent(rowg.at[pl.ds(0, NY - 1)], S_ROW)
    sent(bandg.at[pl.ds(0, NX - 1)], S_BAND)
    sent(bandx.at[pl.ds(0, NY - 1)], S_BANDX)
    sent(colg.at[0, pl.ds(0, NLZ - 1)], S_COL)
    sent(colg.at[0], S_COLC)
    for n in range(CHUNKS):
        sent(recv1.at[pl.ds(n * PER, PER)], S_R1 + n)
    sent(recv2.at[pl.ds(0, NLZ - 1)], S_R2)
    sent(recv3.at[pl.ds(0, NX - 1)], S_R3)
    sent(fg.at[pl.ds(0, NY - 1)], S_F1)
    sent(fx.at[pl.ds(0, NX - 1)], S_F2)
    sent(grecv.at[pl.ds(0, NX - 1)], S_GRAM)
    sent(gall.at[pl.ds(0, 3)], S_GRAMP)
    sent(rrecv.at[pl.ds(0, NY - 1)], S_ROWS)
    sent(brecv.at[pl.ds(0, NX - 1)], S_BANDS)


def hand_over(*refs):
    sems = refs[8]
    copies = [
        pltpu.make_async_copy(refs[k], refs[4 + k], sems.at[k]) for k in range(4)
    ]
    for copy in copies:
        copy.start()
    for copy in copies:
        copy.wait()


def shards(tensor, row_factor, column_factor, band_factor, time_factor):
    v = pltpu.VMEM
    shapes = tuple(jax.ShapeDtypeStruct((n, RANK), F32) for n in (RW, CW, BW, FRAMES))
    factors = (row_factor, column_factor, band_factor, time_factor)
    factors = [pltpu.with_memory_space_constraint(x.T, pltpu.HBM) for x in factors]
    out = pl.pallas_call(
        kernel,
        out_shape=shapes,
        in_specs=[pl.BlockSpec(memory_space=pl.ANY)] + [pl.BlockSpec(memory_space=pltpu.HBM)] * 4,
        out_specs=[pl.BlockSpec(memory_space=v)] * 4,
        scratch_shapes=[
            v((MSG + 16, LANES), F32),
            v((RW, RANK), F32),
            v((CW, RANK), F32),
            v((BW, RANK), F32),
            v((FRAMES, RANK), F32),
            v((TB, ROWS, COLS), BF16),
            v((RW, LANES), F32),
            v((BW, LANES), F32),
            v((NY, RW, LANES), F32),
            v((NX, BW, LANES), F32),
            v((NY, BW, LANES), F32),
            v((ROWS, LANES), F32),
            v((BANDS, LANES), F32),
            v((NY * BW, LANES), F32),
            v((LANES, LANES), F32),
            v((COLS, TB * ROWS), BF16),
            v((FRAMES, HALF, 2 * LANES), BF16),
            v((FRAMES, COLS, LANES), F32),
            v((2, NLZ, PACK, LANES), F32),
            v((NLZ, PACK, LANES), F32),
            v((NLZ, PACK, LANES), F32),
            v((NLZ, PACK, LANES), F32),
            v((PACK, LANES), F32),
            v((NX, PACK, LANES), F32),
            v((2, NLZ, PACK, LANES), F32),
            v((COLS, LANES), F32),
            v((COLS, LANES), BF16),
            v((TB * QROWS, LANES), F32),
            v((4, TB, 8, LANES), F32),
            v((FRAMES, LANES), F32),
            v((NY, FRAMES, LANES), F32),
            v((FRAMES, LANES), F32),
            v((NX, FRAMES, LANES), F32),
            v((4, 2, 24, LANES), F32),
            v((NX, 2, 24, LANES), F32),
            v((4, 2, 24, LANES), F32),
            v((LANES, LANES), F32),
            v((NY, RW, LANES), F32),
            v((NY, RW, LANES), F32),
            v((NX, BW, LANES), F32),
            v((NX, BW, LANES), F32),
            pltpu.SemaphoreType.DMA((LOADS + 4,)),
            pltpu.SemaphoreType.DMA((N_SEMS,)),
            pltpu.SemaphoreType.DMA((N_SEMS,)),
        ],
        compiler_params=pltpu.CompilerParams(
            collective_id=0, has_side_effects=True, vmem_limit_bytes=48 * 1024 * 1024
        ),
        cost_estimate=pl.CostEstimate(
            flops=4 * RANK * TB * ROWS * COLS, bytes_accessed=2 * TB * ROWS * COLS, transcendentals=0
        ),
    )(
        tensor.reshape(TB, ROWS, COLS),
        *factors,
    )
    out = pl.pallas_call(
        hand_over,
        out_shape=shapes,
        in_specs=[pl.BlockSpec(memory_space=v)] * 4,
        out_specs=[pl.BlockSpec(memory_space=pl.ANY)] * 4,
        scratch_shapes=[pltpu.SemaphoreType.DMA((4,))],
    )(*[pltpu.with_memory_space_constraint(x, v) for x in out])
    return tuple(x.T for x in out)


def solution(mesh):
    return jax.shard_map(
        shards,
        mesh=mesh,
        in_specs=(
            P(None, "gy", "gx", None),
            P(None, ("gx", "gy")),
            P(None, "gy"),
            P(None, ("gy", "gx")),
            P(),
        ),
        out_specs=(P(None, ("gx", "gy")), P(None, "gy"), P(None, ("gy", "gx")), P()),
        check_vma=False,
    )
```

```python
import jax
import jax.numpy as jnp
from jax import lax
from jax.experimental import pallas as pl
from jax.experimental.pallas import tpu as pltpu
from jax.sharding import PartitionSpec as P

MESH = pl.DeviceIdType.MESH
F32 = jnp.float32
BF16 = jnp.bfloat16

NX, NY, NLZ = 8, 32, 16
RANK, LANES = 96, 128
FRAMES, BANDS, ROWS, COLS = 2, 16, 128, 1024
RW, CW, BW = 4, 32, 2
PACK = CW * RANK // LANES
TB = FRAMES * BANDS
HALF = BANDS * ROWS
CHUNKS = 4
CHUNK = COLS // CHUNKS
PER = NLZ // CHUNKS
LOADS = 8
MSG = CW + 8
QROWS = ROWS // 4

(
    S_ROW, S_BAND, S_BANDX, S_COL, S_COLC, S_R1, S_R2, S_R3, S_F1, S_F2,
    S_GRAM, S_GRAMP, S_ROWS, S_BANDS,
) = [0, 1, 2, 3, 4, 5, 9, 10, 11, 12, 13, 14, 15, 16]
N_SEMS = 17


def dot(x, y):
    return jnp.dot(x, y, preferred_element_type=F32)


def exact(x, y):
    x_high, y_high = x.astype(BF16), y.astype(BF16)
    x_low = (x - x_high.astype(F32)).astype(BF16)
    y_low = (y - y_high.astype(F32)).astype(BF16)
    return dot(x_high, y_high) + (dot(x_high, y_low) + dot(x_low, y_high))


def total(ref, count):
    out = ref[0]
    for k in range(1, count):
        out = out + ref[k]
    return out


def wrap(index, size):
    return jnp.where(index >= size, index - size, index)


def lane_of(x):
    return lax.broadcasted_iota(jnp.int32, x.shape, 1)


def pack(tiles):
    spare = lane_of(tiles[3]) >= RANK
    return [
        jnp.where(spare, pltpu.roll(tiles[3], RANK - 32 * m, 1), tiles[m]) for m in range(3)
    ]


def unpack(tiles):
    lane = lane_of(tiles[0])
    last = jnp.zeros_like(tiles[0])
    for m in (2, 1, 0):
        last = jnp.where(lane < 32 * m + 32, pltpu.roll(tiles[m], 32 * m + 32, 1), last)
    zero = jnp.zeros_like(last)
    return [jnp.where(lane < RANK, tile, zero) for tile in tiles] + [
        jnp.where(lane < RANK, last, zero)
    ]


def kernel(
    tensor, row_in, col_in, band_in, time_in,
    row_out, col_out, band_out, time_out,
    packed, row_v, col_v, band_v, time_v,
    data, mine4, mine2, rowg, bandg, bandx, row_t, band_t, bandx_t, tb_t,
    turned, prod, by_frame, part, recv1, sum1, recv2, fin, recv3,
    colg, colf, low, folded, partials,
    fpart, fg, fsum, fx, gpart, grecv, gall, gcols,
    rsend, rrecv, bsend, brecv,
    local_sems, send_sems, recv_sems,
):
    a = lax.axis_index("gx")
    g = lax.axis_index("gy")
    lz = lax.div(g, 2)
    c = g - 2 * lz
    l = lax.div(lz, 8)
    z = lz - 8 * l
    p = l * 2 + c
    other = 1 - c
    partner = lz * 2 + other
    gx_peers = [wrap(a + k, NX) for k in range(1, NX)]
    lz_order = [lane + wrap(z + k, 8) for k in (4, 3, 5, 2, 6, 1, 7, 0) for lane in (8 * l, 8 - 8 * l)]
    del lz_order[-2]
    core_peers = [to * 2 + c for to in lz_order]
    gy_peers = [to * 2 + core for to in lz_order for core in (c, other)] + [partner]

    def send(src, dst, sem, device):
        pltpu.make_async_remote_copy(
            src_ref=src, dst_ref=dst, send_sem=send_sems.at[sem], recv_sem=recv_sems.at[sem],
            device_id=device, device_id_type=MESH,
        ).start()

    def arrived(ref, sem):
        pltpu.make_async_copy(ref, ref, recv_sems.at[sem]).wait()

    def sent(ref, sem):
        pltpu.make_async_copy(ref, ref, send_sems.at[sem]).wait()

    small = [
        pltpu.make_async_copy(src, dst, local_sems.at[LOADS + k])
        for k, (src, dst) in enumerate(
            [(row_in, row_v), (band_in, band_v), (col_in, col_v), (time_in, time_v)]
        )
    ]
    for copy in small:
        copy.start()

    barrier = pltpu.get_barrier_semaphore()
    for to in gy_peers:
        pl.semaphore_signal(barrier, inc=1, device_id=(a, to), device_id_type=MESH)
    for to in gx_peers:
        pl.semaphore_signal(barrier, inc=1, device_id=(to, g), device_id_type=MESH)

    for k in range(LOADS):
        span = pl.ds(k * (TB // LOADS), TB // LOADS)
        pltpu.make_async_copy(tensor.at[span], data.at[span], local_sems.at[k]).start()

    tb_t[...] = jnp.zeros_like(tb_t)
    packed[...] = jnp.zeros_like(packed)
    for copy in small:
        copy.wait()
    packed[0:CW, 0:RANK] = col_v[...]
    packed[CW : CW + BW, 0:RANK] = band_v[...]
    packed[MSG : MSG + RW, 0:RANK] = row_v[...]
    packed[MSG + 8 : MSG + 8 + FRAMES, 0:RANK] = time_v[...]
    mine2[...] = packed[CW : CW + BW]
    mine4[...] = packed[MSG : MSG + RW]
    time8 = packed[MSG + 8 :]
    rowg[g] = mine4[...]
    bandg[a] = mine2[...]
    bandx[g] = mine2[...]
    for m, tile in enumerate(pack([packed[8 * m : 8 * m + 8] for m in range(4)])):
        colg[c, lz, 8 * m : 8 * m + 8] = tile

    pl.semaphore_wait(barrier, NY - 1 + NX - 1)

    for to in core_peers:
        send(colg.at[c, lz], colg.at[c, lz], S_COL, (a, to))
    for to in gy_peers:
        send(mine4, rowg.at[g], S_ROW, (a, to))
    for to in gx_peers:
        send(mine2, bandg.at[a], S_BAND, (to, g))

    @pl.loop(0, LOADS)
    def _(k):
        per = TB // LOADS
        span = pl.ds(k * per, per)
        pltpu.make_async_copy(tensor.at[span], data.at[span], local_sems.at[k]).wait()
        for i in range(per):
            at = pl.multiple_of((k * per + i) * ROWS, ROWS)
            turned[:, pl.ds(at, ROWS)] = data[k * per + i].T

    for to in gy_peers:
        send(mine2, bandx.at[g], S_BANDX, (a, to))

    arrived(bandg.at[pl.ds(0, NX - 1)], S_BAND)
    for k in range(NX):
        band_t[BW * k : BW * k + BW] = bandg[k]
    for t in range(FRAMES):
        tb_t[t * BANDS : (t + 1) * BANDS] = time8[t : t + 1] * band_t[...]
    tb_t[TB : TB + BANDS] = band_t[...]
    arrived(rowg.at[pl.ds(0, NY - 1)], S_ROW)
    for k in range(NY):
        row_t[RW * k : RW * k + RW] = rowg[k]

    @pl.loop(0, BANDS)
    def _(k):
        span = pl.ds(pl.multiple_of(k * ROWS, ROWS), ROWS)
        rows = row_t[...]
        plain = (tb_t[pl.ds(TB + k, 1)] * rows).astype(BF16)
        for t in range(FRAMES):
            prod[t, span, 0:LANES] = (tb_t[pl.ds(t * BANDS + k, 1)] * rows).astype(BF16)
            prod[t, span, LANES:] = plain

    def slot_lz(n, i):
        return (i // 2) * (NLZ // 2) + 2 * n + i % 2

    def send_pieces(n):
        span = pl.ds(n * PER, PER)
        arrived(recv1.at[span], S_R1 + n)
        sum1[span] = part[c, span] + recv1[span]
        for i in range(PER):
            k = slot_lz(n, i)

            @pl.when(k != lz)
            def _():
                send(sum1.at[n * PER + i], recv2.at[lz], S_R2, (a, k * 2 + c))

            @pl.when(k == lz)
            def _():
                recv2[lz] = sum1[n * PER + i]

    @pl.loop(0, CHUNKS)
    def _(n):
        heres = [
            pl.ds(pl.multiple_of(i * (COLS // 2) + n * (CHUNK // 2), CHUNK // 2), CHUNK // 2)
            for i in range(2)
        ]
        acc = jnp.zeros((CHUNK, LANES), F32)
        for t in range(FRAMES):
            both = dot(
                jnp.concatenate(
                    [turned[here, t * HALF : (t + 1) * HALF] for here in heres], axis=0
                ),
                prod[t],
            )
            for i, here in enumerate(heres):
                by_frame[t, here] = both[i * (CHUNK // 2) : (i + 1) * (CHUNK // 2), LANES:]
            acc = acc + both[:, 0:LANES]
        acc = acc.reshape(CHUNK // CW, 4, 8, LANES)
        tiles = pack([acc[:, m].reshape(CHUNK // 4, LANES) for m in range(4)])
        for k in range(CHUNK // CW):
            for m in range(3):
                part[k % 2, n * PER + k // 2, 8 * m : 8 * m + 8] = tiles[m][8 * k : 8 * k + 8]
        span = pl.ds(n * PER, PER)
        send(part.at[other, span], recv1.at[span], S_R1 + n, (a, partner))

    gram = exact(row_t[...].T, row_t[...])
    for k in range(4):
        gpart[k, 0] = gram[24 * k : 24 * k + 24]
    arrived(colg.at[0, pl.ds(0, NLZ - 1)], S_COL)
    send(colg.at[c], colg.at[c], S_COLC, (a, partner))

    @pl.loop(0, CHUNKS)
    def _(n):
        send_pieces(n)

    arrived(bandx.at[pl.ds(0, NY - 1)], S_BANDX)
    for k in range(NY):
        bandx_t[BW * k : BW * k + BW] = bandx[k]
    gram = exact(bandx_t[...].T, bandx_t[...])
    for k in range(4):
        gpart[k, 1] = gram[24 * k : 24 * k + 24]
    grecv[a] = gpart[p]
    for to in gx_peers:
        send(gpart.at[p], grecv.at[a], S_GRAM, (to, g))

    arrived(colg.at[0], S_COLC)
    for i in range(2):
        tiles = unpack(
            [colg[i, :, 8 * m : 8 * m + 8].reshape(8 * NLZ, LANES) for m in range(3)]
        )
        for k in range(NLZ):
            block = jnp.concatenate([tile[8 * k : 8 * k + 8] for tile in tiles], axis=0)
            at = (2 * k + i) * CW
            colf[at : at + CW] = block
            low[at : at + CW] = block.astype(BF16)

    for t in range(FRAMES):
        fpart[t : t + 1] = jnp.sum(
            by_frame[t] * low[...].astype(F32), axis=0, keepdims=True
        )
    fg[g] = fpart[...]
    for to in gy_peers:
        send(fpart, fg.at[g], S_F1, (a, to))

    @pl.loop(0, 4)
    def _(q):
        half = QROWS // 2
        heres = [pl.ds(pl.multiple_of(i * (ROWS // 2) + q * half, half), half) for i in range(2)]
        block = jnp.concatenate([data[:, here, :] for here in heres], axis=1)
        folded[...] = dot(block.reshape(TB * QROWS, COLS), low[...])
        rows = jnp.zeros((QROWS, LANES), F32)
        row_here = jnp.concatenate([row_t[here] for here in heres], axis=0)
        for j in range(TB):
            block = folded[j * QROWS : (j + 1) * QROWS]
            rows = rows + block * tb_t[j : j + 1]
            block = block * row_here
            partials[q, j] = jnp.sum(block.reshape(QROWS // 8, 8, LANES), axis=0)
        owners = [(i // 4) * (NY // 2) + 4 * q + i % 4 for i in range(NY // 4)]
        for i, k in enumerate(owners):
            rsend[k] = rows[RW * i : RW * i + RW]
        for k in owners:

            @pl.when(k != g)
            def _():
                send(rsend.at[k], rrecv.at[g], S_ROWS, (a, k))

    sums = total(partials, 4)
    bands = jnp.zeros((BANDS, LANES), F32)
    for t in range(FRAMES):
        bands = bands + time8[t : t + 1] * jnp.sum(sums[t * BANDS : (t + 1) * BANDS], axis=1)
    for k in range(NX):
        bsend[k] = bands[BW * k : BW * k + BW]
    for k in range(1, NX):
        to = wrap(a + k, NX)
        send(bsend.at[to], brecv.at[a], S_BANDS, (to, g))
    brecv[a] = bsend[a]
    rrecv[g] = rsend[g]

    arrived(grecv.at[pl.ds(0, NX - 1)], S_GRAM)
    gall[p] = total(grecv, NX)
    for k in range(1, 4):
        to = wrap(p + k, 4)
        to_l = lax.div(to, 2)
        send(gall.at[p], gall.at[p], S_GRAMP, (a, (to_l * 8 + z) * 2 + to - 2 * to_l))
    gcols[...] = jnp.zeros_like(gcols)

    @pl.loop(0, 4)
    def _(i):
        block = colf[pl.ds(pl.multiple_of(i * 256, 256), 256)]
        gcols[...] += exact(block.T, block)

    arrived(recv2.at[pl.ds(0, NLZ - 1)], S_R2)
    fin[...] = total(recv2, NLZ)
    recv3[a] = fin[...]
    for to in gx_peers:
        send(fin, recv3.at[a], S_R3, (to, g))
    arrived(fg.at[pl.ds(0, NY - 1)], S_F1)
    fsum[...] = total(fg, NY)
    fx[a] = fsum[...]
    for to in gx_peers:
        send(fsum, fx.at[a], S_F2, (to, g))

    gram_cols = gcols[...]
    arrived(gall.at[pl.ds(0, 3)], S_GRAMP)
    pad = jnp.zeros((LANES - RANK, LANES), F32)
    gram_rows, gram_bands = (
        jnp.concatenate([gall[:, i].reshape(RANK, LANES), pad], axis=0) for i in range(2)
    )
    time_n = jnp.concatenate([time8, jnp.zeros((LANES - 8, LANES), F32)], axis=0).T
    gram_time = time_n[:, 0:1] * time8[0:1] + time_n[:, 1:2] * time8[1:2]
    row_model = exact(packed[MSG : MSG + 8], gram_cols * gram_bands * gram_time)
    col_model = exact(packed[0:CW], gram_rows * gram_bands * gram_time)
    band_model = exact(packed[CW:MSG], gram_rows * gram_cols * gram_time)
    time_model = exact(time8, gram_rows * gram_cols * gram_bands)

    arrived(fx.at[pl.ds(0, NX - 1)], S_F2)
    time_out[...] = (time_model[0:FRAMES] - total(fx, NX))[:, 0:RANK]
    arrived(recv3.at[pl.ds(0, NX - 1)], S_R3)
    sums = total(recv3, NX)
    sums = jnp.concatenate(unpack([sums[8 * m : 8 * m + 8] for m in range(3)]), axis=0)
    col_out[...] = (col_model - sums)[:, 0:RANK]
    arrived(rrecv.at[pl.ds(0, NY - 1)], S_ROWS)
    row_out[...] = (row_model[0:RW] - total(rrecv, NY))[:, 0:RANK]
    arrived(brecv.at[pl.ds(0, NX - 1)], S_BANDS)
    band_out[...] = (band_model[0:BW] - total(brecv, NX))[:, 0:RANK]

    sent(rowg.at[pl.ds(0, NY - 1)], S_ROW)
    sent(bandg.at[pl.ds(0, NX - 1)], S_BAND)
    sent(bandx.at[pl.ds(0, NY - 1)], S_BANDX)
    sent(colg.at[0, pl.ds(0, NLZ - 1)], S_COL)
    sent(colg.at[0], S_COLC)
    for n in range(CHUNKS):
        sent(recv1.at[pl.ds(n * PER, PER)], S_R1 + n)
    sent(recv2.at[pl.ds(0, NLZ - 1)], S_R2)
    sent(recv3.at[pl.ds(0, NX - 1)], S_R3)
    sent(fg.at[pl.ds(0, NY - 1)], S_F1)
    sent(fx.at[pl.ds(0, NX - 1)], S_F2)
    sent(grecv.at[pl.ds(0, NX - 1)], S_GRAM)
    sent(gall.at[pl.ds(0, 3)], S_GRAMP)
    sent(rrecv.at[pl.ds(0, NY - 1)], S_ROWS)
    sent(brecv.at[pl.ds(0, NX - 1)], S_BANDS)


def hand_over(*refs):
    sems = refs[8]
    copies = [
        pltpu.make_async_copy(refs[k], refs[4 + k], sems.at[k]) for k in range(4)
    ]
    for copy in copies:
        copy.start()
    for copy in copies:
        copy.wait()


def shards(tensor, row_factor, column_factor, band_factor, time_factor):
    v = pltpu.VMEM
    shapes = tuple(jax.ShapeDtypeStruct((n, RANK), F32) for n in (RW, CW, BW, FRAMES))
    factors = (row_factor, column_factor, band_factor, time_factor)
    factors = [pltpu.with_memory_space_constraint(x.T, pltpu.HBM) for x in factors]
    out = pl.pallas_call(
        kernel,
        out_shape=shapes,
        in_specs=[pl.BlockSpec(memory_space=pl.ANY)] + [pl.BlockSpec(memory_space=pltpu.HBM)] * 4,
        out_specs=[pl.BlockSpec(memory_space=v)] * 4,
        scratch_shapes=[
            v((MSG + 16, LANES), F32),
            v((RW, RANK), F32),
            v((CW, RANK), F32),
            v((BW, RANK), F32),
            v((FRAMES, RANK), F32),
            v((TB, ROWS, COLS), BF16),
            v((RW, LANES), F32),
            v((BW, LANES), F32),
            v((NY, RW, LANES), F32),
            v((NX, BW, LANES), F32),
            v((NY, BW, LANES), F32),
            v((ROWS, LANES), F32),
            v((BANDS, LANES), F32),
            v((NY * BW, LANES), F32),
            v((LANES, LANES), F32),
            v((COLS, TB * ROWS), BF16),
            v((FRAMES, HALF, 2 * LANES), BF16),
            v((FRAMES, COLS, LANES), F32),
            v((2, NLZ, PACK, LANES), F32),
            v((NLZ, PACK, LANES), F32),
            v((NLZ, PACK, LANES), F32),
            v((NLZ, PACK, LANES), F32),
            v((PACK, LANES), F32),
            v((NX, PACK, LANES), F32),
            v((2, NLZ, PACK, LANES), F32),
            v((COLS, LANES), F32),
            v((COLS, LANES), BF16),
            v((TB * QROWS, LANES), F32),
            v((4, TB, 8, LANES), F32),
            v((FRAMES, LANES), F32),
            v((NY, FRAMES, LANES), F32),
            v((FRAMES, LANES), F32),
            v((NX, FRAMES, LANES), F32),
            v((4, 2, 24, LANES), F32),
            v((NX, 2, 24, LANES), F32),
            v((4, 2, 24, LANES), F32),
            v((LANES, LANES), F32),
            v((NY, RW, LANES), F32),
            v((NY, RW, LANES), F32),
            v((NX, BW, LANES), F32),
            v((NX, BW, LANES), F32),
            pltpu.SemaphoreType.DMA((LOADS + 4,)),
            pltpu.SemaphoreType.DMA((N_SEMS,)),
            pltpu.SemaphoreType.DMA((N_SEMS,)),
        ],
        compiler_params=pltpu.CompilerParams(
            collective_id=0, has_side_effects=True, vmem_limit_bytes=48 * 1024 * 1024
        ),
        cost_estimate=pl.CostEstimate(
            flops=4 * RANK * TB * ROWS * COLS, bytes_accessed=2 * TB * ROWS * COLS, transcendentals=0
        ),
    )(
        tensor.reshape(TB, ROWS, COLS),
        *factors,
    )
    out = pl.pallas_call(
        hand_over,
        out_shape=shapes,
        in_specs=[pl.BlockSpec(memory_space=v)] * 4,
        out_specs=[pl.BlockSpec(memory_space=pl.ANY)] * 4,
        scratch_shapes=[pltpu.SemaphoreType.DMA((4,))],
    )(*[pltpu.with_memory_space_constraint(x, v) for x in out])
    return tuple(x.T for x in out)


def solution(mesh):
    return jax.shard_map(
        shards,
        mesh=mesh,
        in_specs=(
            P(None, "gy", "gx", None),
            P(None, ("gx", "gy")),
            P(None, "gy"),
            P(None, ("gy", "gx")),
            P(),
        ),
        out_specs=(P(None, ("gx", "gy")), P(None, "gy"), P(None, ("gy", "gx")), P()),
        check_vma=False,
    )
```

```python
import jax
import jax.numpy as jnp
from jax import lax
from jax.experimental import pallas as pl
from jax.experimental.pallas import tpu as pltpu
from jax.sharding import PartitionSpec as P

MESH = pl.DeviceIdType.MESH
F32 = jnp.float32
BF16 = jnp.bfloat16

NX, NY, NLZ = 8, 32, 16
RANK, LANES = 96, 128
FRAMES, BANDS, ROWS, COLS = 2, 16, 128, 1024
RW, CW, BW = 4, 32, 2
PACK = CW * RANK // LANES
TB = FRAMES * BANDS
HALF = BANDS * ROWS
CHUNKS = 4
CHUNK = COLS // CHUNKS
PER = NLZ // CHUNKS
LOADS = 8
MSG = CW + 8
QROWS = ROWS // 4

(
    S_ROW, S_BAND, S_BANDX, S_COL, S_COLC, S_R1, S_R2, S_R3, S_F1, S_F2,
    S_GRAM, S_GRAMP, S_ROWS, S_BANDS,
) = [0, 1, 2, 3, 4, 5, 9, 10, 11, 12, 13, 14, 15, 16]
N_SEMS = 17


def dot(x, y):
    return jnp.dot(x, y, preferred_element_type=F32)


def exact(x, y):
    x_high, y_high = x.astype(BF16), y.astype(BF16)
    x_low = (x - x_high.astype(F32)).astype(BF16)
    y_low = (y - y_high.astype(F32)).astype(BF16)
    return dot(x_high, y_high) + (dot(x_high, y_low) + dot(x_low, y_high))


def total(ref, count):
    out = ref[0]
    for k in range(1, count):
        out = out + ref[k]
    return out


def wrap(index, size):
    return jnp.where(index >= size, index - size, index)


def lane_of(x):
    return lax.broadcasted_iota(jnp.int32, x.shape, 1)


def pack(tiles):
    spare = lane_of(tiles[3]) >= RANK
    return [
        jnp.where(spare, pltpu.roll(tiles[3], RANK - 32 * m, 1), tiles[m]) for m in range(3)
    ]


def unpack(tiles):
    lane = lane_of(tiles[0])
    last = jnp.zeros_like(tiles[0])
    for m in (2, 1, 0):
        last = jnp.where(lane < 32 * m + 32, pltpu.roll(tiles[m], 32 * m + 32, 1), last)
    zero = jnp.zeros_like(last)
    return [jnp.where(lane < RANK, tile, zero) for tile in tiles] + [
        jnp.where(lane < RANK, last, zero)
    ]


def kernel(
    tensor, row_in, col_in, band_in, time_in,
    row_out, col_out, band_out, time_out,
    packed, row_v, col_v, band_v, time_v,
    data, mine4, mine2, rowg, bandg, bandx, row_t, band_t, bandx_t, tb_t,
    turned, prod, by_frame, part, recv1, sum1, recv2, fin, recv3,
    colg, colf, low, folded, partials,
    fpart, fg, fsum, fx, gpart, grecv, gall, gcols,
    rsend, rrecv, bsend, brecv,
    local_sems, send_sems, recv_sems,
):
    a = lax.axis_index("gx")
    g = lax.axis_index("gy")
    lz = lax.div(g, 2)
    c = g - 2 * lz
    l = lax.div(lz, 8)
    z = lz - 8 * l
    p = l * 2 + c
    other = 1 - c
    partner = lz * 2 + other
    gx_peers = [wrap(a + k, NX) for k in range(1, NX)]
    lz_order = [lane + wrap(z + k, 8) for k in (4, 3, 5, 2, 6, 1, 7, 0) for lane in (8 * l, 8 - 8 * l)]
    del lz_order[-2]
    core_peers = [to * 2 + c for to in lz_order]
    gy_peers = [to * 2 + core for to in lz_order for core in (c, other)] + [partner]

    def send(src, dst, sem, device):
        pltpu.make_async_remote_copy(
            src_ref=src, dst_ref=dst, send_sem=send_sems.at[sem], recv_sem=recv_sems.at[sem],
            device_id=device, device_id_type=MESH,
        ).start()

    def arrived(ref, sem):
        pltpu.make_async_copy(ref, ref, recv_sems.at[sem]).wait()

    def sent(ref, sem):
        pltpu.make_async_copy(ref, ref, send_sems.at[sem]).wait()

    small = [
        pltpu.make_async_copy(src, dst, local_sems.at[LOADS + k])
        for k, (src, dst) in enumerate(
            [(row_in, row_v), (band_in, band_v), (col_in, col_v), (time_in, time_v)]
        )
    ]
    for copy in small:
        copy.start()

    barrier = pltpu.get_barrier_semaphore()
    for to in gy_peers:
        pl.semaphore_signal(barrier, inc=1, device_id=(a, to), device_id_type=MESH)
    for to in gx_peers:
        pl.semaphore_signal(barrier, inc=1, device_id=(to, g), device_id_type=MESH)

    for k in range(LOADS):
        span = pl.ds(k * (TB // LOADS), TB // LOADS)
        pltpu.make_async_copy(tensor.at[span], data.at[span], local_sems.at[k]).start()

    tb_t[...] = jnp.zeros_like(tb_t)
    packed[...] = jnp.zeros_like(packed)
    for copy in small:
        copy.wait()
    packed[0:CW, 0:RANK] = col_v[...]
    packed[CW : CW + BW, 0:RANK] = band_v[...]
    packed[MSG : MSG + RW, 0:RANK] = row_v[...]
    packed[MSG + 8 : MSG + 8 + FRAMES, 0:RANK] = time_v[...]
    mine2[...] = packed[CW : CW + BW]
    mine4[...] = packed[MSG : MSG + RW]
    time8 = packed[MSG + 8 :]
    rowg[g] = mine4[...]
    bandg[a] = mine2[...]
    bandx[g] = mine2[...]
    for m, tile in enumerate(pack([packed[8 * m : 8 * m + 8] for m in range(4)])):
        colg[c, lz, 8 * m : 8 * m + 8] = tile

    pl.semaphore_wait(barrier, NY - 1 + NX - 1)

    for to in gy_peers:
        send(mine4, rowg.at[g], S_ROW, (a, to))
    for to in gx_peers:
        send(mine2, bandg.at[a], S_BAND, (to, g))

    @pl.loop(0, LOADS)
    def _(k):
        per = TB // LOADS
        span = pl.ds(k * per, per)
        pltpu.make_async_copy(tensor.at[span], data.at[span], local_sems.at[k]).wait()
        for i in range(per):
            at = pl.multiple_of((k * per + i) * ROWS, ROWS)
            turned[:, pl.ds(at, ROWS)] = data[k * per + i].T

        @pl.when(k == 0)
        def _():
            for to in core_peers:
                send(colg.at[c, lz], colg.at[c, lz], S_COL, (a, to))

    for to in gy_peers:
        send(mine2, bandx.at[g], S_BANDX, (a, to))

    arrived(bandg.at[pl.ds(0, NX - 1)], S_BAND)
    for k in range(NX):
        band_t[BW * k : BW * k + BW] = bandg[k]
    for t in range(FRAMES):
        tb_t[t * BANDS : (t + 1) * BANDS] = time8[t : t + 1] * band_t[...]
    tb_t[TB : TB + BANDS] = band_t[...]
    arrived(rowg.at[pl.ds(0, NY - 1)], S_ROW)
    for k in range(NY):
        row_t[RW * k : RW * k + RW] = rowg[k]

    @pl.loop(0, BANDS)
    def _(k):
        span = pl.ds(pl.multiple_of(k * ROWS, ROWS), ROWS)
        rows = row_t[...]
        plain = (tb_t[pl.ds(TB + k, 1)] * rows).astype(BF16)
        for t in range(FRAMES):
            prod[t, span, 0:LANES] = (tb_t[pl.ds(t * BANDS + k, 1)] * rows).astype(BF16)
            prod[t, span, LANES:] = plain

    def slot_lz(n, i):
        return (i // 2) * (NLZ // 2) + 2 * n + i % 2

    def send_pieces(n):
        span = pl.ds(n * PER, PER)
        arrived(recv1.at[span], S_R1 + n)
        sum1[span] = part[c, span] + recv1[span]
        for i in range(PER):
            k = slot_lz(n, i)

            @pl.when(k != lz)
            def _():
                send(sum1.at[n * PER + i], recv2.at[lz], S_R2, (a, k * 2 + c))

            @pl.when(k == lz)
            def _():
                recv2[lz] = sum1[n * PER + i]

    @pl.loop(0, CHUNKS)
    def _(n):
        heres = [
            pl.ds(pl.multiple_of(i * (COLS // 2) + n * (CHUNK // 2), CHUNK // 2), CHUNK // 2)
            for i in range(2)
        ]
        acc = jnp.zeros((CHUNK, LANES), F32)
        for t in range(FRAMES):
            both = dot(
                jnp.concatenate(
                    [turned[here, t * HALF : (t + 1) * HALF] for here in heres], axis=0
                ),
                prod[t],
            )
            for i, here in enumerate(heres):
                by_frame[t, here] = both[i * (CHUNK // 2) : (i + 1) * (CHUNK // 2), LANES:]
            acc = acc + both[:, 0:LANES]
        acc = acc.reshape(CHUNK // CW, 4, 8, LANES)
        tiles = pack([acc[:, m].reshape(CHUNK // 4, LANES) for m in range(4)])
        for k in range(CHUNK // CW):
            for m in range(3):
                part[k % 2, n * PER + k // 2, 8 * m : 8 * m + 8] = tiles[m][8 * k : 8 * k + 8]
        span = pl.ds(n * PER, PER)
        send(part.at[other, span], recv1.at[span], S_R1 + n, (a, partner))

    gram = exact(row_t[...].T, row_t[...])
    for k in range(4):
        gpart[k, 0] = gram[24 * k : 24 * k + 24]
    arrived(colg.at[0, pl.ds(0, NLZ - 1)], S_COL)
    send(colg.at[c], colg.at[c], S_COLC, (a, partner))

    @pl.loop(0, CHUNKS)
    def _(n):
        send_pieces(n)

    arrived(bandx.at[pl.ds(0, NY - 1)], S_BANDX)
    for k in range(NY):
        bandx_t[BW * k : BW * k + BW] = bandx[k]
    gram = exact(bandx_t[...].T, bandx_t[...])
    for k in range(4):
        gpart[k, 1] = gram[24 * k : 24 * k + 24]
    grecv[a] = gpart[p]
    for to in gx_peers:
        send(gpart.at[p], grecv.at[a], S_GRAM, (to, g))

    arrived(colg.at[0], S_COLC)
    for i in range(2):
        tiles = unpack(
            [colg[i, :, 8 * m : 8 * m + 8].reshape(8 * NLZ, LANES) for m in range(3)]
        )
        for k in range(NLZ):
            block = jnp.concatenate([tile[8 * k : 8 * k + 8] for tile in tiles], axis=0)
            at = (2 * k + i) * CW
            colf[at : at + CW] = block
            low[at : at + CW] = block.astype(BF16)

    for t in range(FRAMES):
        fpart[t : t + 1] = jnp.sum(
            by_frame[t] * low[...].astype(F32), axis=0, keepdims=True
        )
    fg[g] = fpart[...]
    for to in gy_peers:
        send(fpart, fg.at[g], S_F1, (a, to))

    @pl.loop(0, 4)
    def _(q):
        half = QROWS // 2
        heres = [pl.ds(pl.multiple_of(i * (ROWS // 2) + q * half, half), half) for i in range(2)]
        block = jnp.concatenate([data[:, here, :] for here in heres], axis=1)
        folded[...] = dot(block.reshape(TB * QROWS, COLS), low[...])
        rows = jnp.zeros((QROWS, LANES), F32)
        row_here = jnp.concatenate([row_t[here] for here in heres], axis=0)
        for j in range(TB):
            block = folded[j * QROWS : (j + 1) * QROWS]
            rows = rows + block * tb_t[j : j + 1]
            block = block * row_here
            partials[q, j] = jnp.sum(block.reshape(QROWS // 8, 8, LANES), axis=0)
        owners = [(i // 4) * (NY // 2) + 4 * q + i % 4 for i in range(NY // 4)]
        for i, k in enumerate(owners):
            rsend[k] = rows[RW * i : RW * i + RW]
        for k in owners:

            @pl.when(k != g)
            def _():
                send(rsend.at[k], rrecv.at[g], S_ROWS, (a, k))

    sums = total(partials, 4)
    bands = jnp.zeros((BANDS, LANES), F32)
    for t in range(FRAMES):
        bands = bands + time8[t : t + 1] * jnp.sum(sums[t * BANDS : (t + 1) * BANDS], axis=1)
    for k in range(NX):
        bsend[k] = bands[BW * k : BW * k + BW]
    for k in range(1, NX):
        to = wrap(a + k, NX)
        send(bsend.at[to], brecv.at[a], S_BANDS, (to, g))
    brecv[a] = bsend[a]
    rrecv[g] = rsend[g]

    arrived(grecv.at[pl.ds(0, NX - 1)], S_GRAM)
    gall[p] = total(grecv, NX)
    for k in range(1, 4):
        to = wrap(p + k, 4)
        to_l = lax.div(to, 2)
        send(gall.at[p], gall.at[p], S_GRAMP, (a, (to_l * 8 + z) * 2 + to - 2 * to_l))
    gcols[...] = jnp.zeros_like(gcols)

    @pl.loop(0, 4)
    def _(i):
        block = colf[pl.ds(pl.multiple_of(i * 256, 256), 256)]
        gcols[...] += exact(block.T, block)

    arrived(recv2.at[pl.ds(0, NLZ - 1)], S_R2)
    fin[...] = total(recv2, NLZ)
    recv3[a] = fin[...]
    for to in gx_peers:
        send(fin, recv3.at[a], S_R3, (to, g))
    arrived(fg.at[pl.ds(0, NY - 1)], S_F1)
    fsum[...] = total(fg, NY)
    fx[a] = fsum[...]
    for to in gx_peers:
        send(fsum, fx.at[a], S_F2, (to, g))

    gram_cols = gcols[...]
    arrived(gall.at[pl.ds(0, 3)], S_GRAMP)
    pad = jnp.zeros((LANES - RANK, LANES), F32)
    gram_rows, gram_bands = (
        jnp.concatenate([gall[:, i].reshape(RANK, LANES), pad], axis=0) for i in range(2)
    )
    time_n = jnp.concatenate([time8, jnp.zeros((LANES - 8, LANES), F32)], axis=0).T
    gram_time = time_n[:, 0:1] * time8[0:1] + time_n[:, 1:2] * time8[1:2]
    row_model = exact(packed[MSG : MSG + 8], gram_cols * gram_bands * gram_time)
    col_model = exact(packed[0:CW], gram_rows * gram_bands * gram_time)
    band_model = exact(packed[CW:MSG], gram_rows * gram_cols * gram_time)
    time_model = exact(time8, gram_rows * gram_cols * gram_bands)

    arrived(fx.at[pl.ds(0, NX - 1)], S_F2)
    time_out[...] = (time_model[0:FRAMES] - total(fx, NX))[:, 0:RANK]
    arrived(recv3.at[pl.ds(0, NX - 1)], S_R3)
    sums = total(recv3, NX)
    sums = jnp.concatenate(unpack([sums[8 * m : 8 * m + 8] for m in range(3)]), axis=0)
    col_out[...] = (col_model - sums)[:, 0:RANK]
    arrived(rrecv.at[pl.ds(0, NY - 1)], S_ROWS)
    row_out[...] = (row_model[0:RW] - total(rrecv, NY))[:, 0:RANK]
    arrived(brecv.at[pl.ds(0, NX - 1)], S_BANDS)
    band_out[...] = (band_model[0:BW] - total(brecv, NX))[:, 0:RANK]

    sent(rowg.at[pl.ds(0, NY - 1)], S_ROW)
    sent(bandg.at[pl.ds(0, NX - 1)], S_BAND)
    sent(bandx.at[pl.ds(0, NY - 1)], S_BANDX)
    sent(colg.at[0, pl.ds(0, NLZ - 1)], S_COL)
    sent(colg.at[0], S_COLC)
    for n in range(CHUNKS):
        sent(recv1.at[pl.ds(n * PER, PER)], S_R1 + n)
    sent(recv2.at[pl.ds(0, NLZ - 1)], S_R2)
    sent(recv3.at[pl.ds(0, NX - 1)], S_R3)
    sent(fg.at[pl.ds(0, NY - 1)], S_F1)
    sent(fx.at[pl.ds(0, NX - 1)], S_F2)
    sent(grecv.at[pl.ds(0, NX - 1)], S_GRAM)
    sent(gall.at[pl.ds(0, 3)], S_GRAMP)
    sent(rrecv.at[pl.ds(0, NY - 1)], S_ROWS)
    sent(brecv.at[pl.ds(0, NX - 1)], S_BANDS)


def hand_over(*refs):
    sems = refs[8]
    copies = [
        pltpu.make_async_copy(refs[k], refs[4 + k], sems.at[k]) for k in range(4)
    ]
    for copy in copies:
        copy.start()
    for copy in copies:
        copy.wait()


def shards(tensor, row_factor, column_factor, band_factor, time_factor):
    v = pltpu.VMEM
    shapes = tuple(jax.ShapeDtypeStruct((n, RANK), F32) for n in (RW, CW, BW, FRAMES))
    factors = (row_factor, column_factor, band_factor, time_factor)
    factors = [pltpu.with_memory_space_constraint(x.T, pltpu.HBM) for x in factors]
    out = pl.pallas_call(
        kernel,
        out_shape=shapes,
        in_specs=[pl.BlockSpec(memory_space=pl.ANY)] + [pl.BlockSpec(memory_space=pltpu.HBM)] * 4,
        out_specs=[pl.BlockSpec(memory_space=v)] * 4,
        scratch_shapes=[
            v((MSG + 16, LANES), F32),
            v((RW, RANK), F32),
            v((CW, RANK), F32),
            v((BW, RANK), F32),
            v((FRAMES, RANK), F32),
            v((TB, ROWS, COLS), BF16),
            v((RW, LANES), F32),
            v((BW, LANES), F32),
            v((NY, RW, LANES), F32),
            v((NX, BW, LANES), F32),
            v((NY, BW, LANES), F32),
            v((ROWS, LANES), F32),
            v((BANDS, LANES), F32),
            v((NY * BW, LANES), F32),
            v((LANES, LANES), F32),
            v((COLS, TB * ROWS), BF16),
            v((FRAMES, HALF, 2 * LANES), BF16),
            v((FRAMES, COLS, LANES), F32),
            v((2, NLZ, PACK, LANES), F32),
            v((NLZ, PACK, LANES), F32),
            v((NLZ, PACK, LANES), F32),
            v((NLZ, PACK, LANES), F32),
            v((PACK, LANES), F32),
            v((NX, PACK, LANES), F32),
            v((2, NLZ, PACK, LANES), F32),
            v((COLS, LANES), F32),
            v((COLS, LANES), BF16),
            v((TB * QROWS, LANES), F32),
            v((4, TB, 8, LANES), F32),
            v((FRAMES, LANES), F32),
            v((NY, FRAMES, LANES), F32),
            v((FRAMES, LANES), F32),
            v((NX, FRAMES, LANES), F32),
            v((4, 2, 24, LANES), F32),
            v((NX, 2, 24, LANES), F32),
            v((4, 2, 24, LANES), F32),
            v((LANES, LANES), F32),
            v((NY, RW, LANES), F32),
            v((NY, RW, LANES), F32),
            v((NX, BW, LANES), F32),
            v((NX, BW, LANES), F32),
            pltpu.SemaphoreType.DMA((LOADS + 4,)),
            pltpu.SemaphoreType.DMA((N_SEMS,)),
            pltpu.SemaphoreType.DMA((N_SEMS,)),
        ],
        compiler_params=pltpu.CompilerParams(
            collective_id=0, has_side_effects=True, vmem_limit_bytes=48 * 1024 * 1024
        ),
        cost_estimate=pl.CostEstimate(
            flops=4 * RANK * TB * ROWS * COLS, bytes_accessed=2 * TB * ROWS * COLS, transcendentals=0
        ),
    )(
        tensor.reshape(TB, ROWS, COLS),
        *factors,
    )
    out = pl.pallas_call(
        hand_over,
        out_shape=shapes,
        in_specs=[pl.BlockSpec(memory_space=v)] * 4,
        out_specs=[pl.BlockSpec(memory_space=pl.ANY)] * 4,
        scratch_shapes=[pltpu.SemaphoreType.DMA((4,))],
    )(*[pltpu.with_memory_space_constraint(x, v) for x in out])
    return tuple(x.T for x in out)


def solution(mesh):
    return jax.shard_map(
        shards,
        mesh=mesh,
        in_specs=(
            P(None, "gy", "gx", None),
            P(None, ("gx", "gy")),
            P(None, "gy"),
            P(None, ("gy", "gx")),
            P(),
        ),
        out_specs=(P(None, ("gx", "gy")), P(None, "gy"), P(None, ("gy", "gx")), P()),
        check_vma=False,
    )
```
